512 devices in a mesh: ctx: 64 (over x, z_lo, y), dp: 8 (over z_hi, core).
Axes of the slice: x: 4, y: 8, z: 8 (z_hi: 4, z_lo: 2; z = z_hi * 2 + z_lo), core: 2. Of those that a mesh axis runs over, the one named last changes fastest.
Arguments:
- queries: bfloat16 [8, 8192, 4096], P('dp', 'ctx'), may hold values from -9 to 9
- keys: bfloat16 [8, 8192, 512], P('dp', 'ctx'), may hold values from -6 to 6
- values: bfloat16 [8, 8192, 512], P('dp', 'ctx'), may hold values from -6 to 6
- output_gradient: bfloat16 [8, 8192, 4096], P('dp', 'ctx'), may hold values from -6 to 6
- adapter_query_down: bfloat16 [8, 8192, 16], P('dp', 'ctx'), may hold values from -0.29882812 to 0.29882812
- adapter_value_down: bfloat16 [8, 8192, 16], P('dp', 'ctx'), may hold values from -0.029907227 to 0.029907227
Outputs:
- query_gradient: bfloat16 [8, 8192, 4096], P('dp', 'ctx')
- key_gradient: bfloat16 [8, 8192, 512], P('dp', 'ctx')
- value_gradient: bfloat16 [8, 8192, 512], P('dp', 'ctx')
- adapter_query_up_gradient: float32 [16, 4096], replicated
- adapter_value_up_gradient: float32 [16, 512], replicated
The draws below stay inside these ranges and needn't reach their ends.
All inputs are finite; a program needn't handle non-finite values.
Results may differ from the reference program's by a relative error of at most 0.009.
Values may be sent and summed in bfloat16 or wider, within the bound.
No kernel may reach another device: no remote copies, remote signals or barrier semaphores. Data moves between devices by JAX's collectives and lax.ppermute only.
A program may use at most 64 MiB of HBM per device.

```python
import jax
import jax.numpy as jnp
from jax import lax

QUERY_HEAD_COUNT = 32
KEY_VALUE_HEADS = 4
HEAD_WIDTH = 128
ADAPTER_RANK = 16
TOK_DEV = 128
GROUP = 512
TOKEN_LENGTH = 8192
BATCH_COUNT = 8


def draw_queries(key, part):
    key = jax.random.fold_in(key, 11)
    shape = (BATCH_COUNT, TOKEN_LENGTH, QUERY_HEAD_COUNT, HEAD_WIDTH)
    field = jnp.clip(jax.random.normal(key, shape, jnp.float32), -6.0, 6.0)
    return field.reshape(BATCH_COUNT, TOKEN_LENGTH, QUERY_HEAD_COUNT * HEAD_WIDTH).astype(jnp.bfloat16)


def draw_keys(key, part):
    key = jax.random.fold_in(key, 23)
    shape = (BATCH_COUNT, TOKEN_LENGTH, KEY_VALUE_HEADS, HEAD_WIDTH)
    field = jnp.clip(jax.random.normal(key, shape, jnp.float32), -6.0, 6.0)
    return field.reshape(BATCH_COUNT, TOKEN_LENGTH, KEY_VALUE_HEADS * HEAD_WIDTH).astype(jnp.bfloat16)


def levels(own_key, shape, shards, least, high):
    gain, own = 1.0, jax.random.fold_in(own_key, 6)
    for dim, shards_of in shards:
        steps = jnp.exp(jax.random.uniform(jax.random.fold_in(own, dim), (shards_of,), jnp.float32, least / len(shards), high / len(shards)))
        gain = gain * jnp.repeat(steps, shape[dim] // shards_of).reshape([-1 if axis == dim else 1 for axis in range(len(shape))])
    return gain


def normal_values(stream_key, shape, scale, bound, shards=(), kind=jnp.bfloat16):
    result = jax.random.normal(stream_key, shape, jnp.float32) * scale
    if len(shards) > 0:
        result = levels(stream_key, shape, shards, -0.22, 0.18) * result
    return jnp.clip(result, min=-bound, max=bound).astype(kind)


def setup_inputs(seed: int = 0) -> dict:
    streams_of = jax.random.split(jax.random.key(seed), 7)
    return {
        "queries": draw_queries(jax.random.fold_in(streams_of[6], 71), 0),
        "keys": draw_keys(jax.random.fold_in(streams_of[6], 71), 0),
        "values": normal_values(streams_of[2], (BATCH_COUNT, TOKEN_LENGTH, KEY_VALUE_HEADS * HEAD_WIDTH), 1.0, 6.0, ((0, 8), (1, 64))),
        "output_gradient": normal_values(streams_of[3], (BATCH_COUNT, TOKEN_LENGTH, QUERY_HEAD_COUNT * HEAD_WIDTH), 1.0, 6.0, ((0, 8), (1, 64))),
        "adapter_query_down": normal_values(streams_of[4], (BATCH_COUNT, TOKEN_LENGTH, ADAPTER_RANK), 0.05, 0.29882812, ((0, 8), (1, 64))),
        "adapter_value_down": normal_values(streams_of[5], (BATCH_COUNT, TOKEN_LENGTH, ADAPTER_RANK), 0.005, 0.029907227, ((0, 8), (1, 64))),
    }


ADAPTER_SCALE = 2.0


def group_grads(block):
    queries, keys, values, output_gradient = block
    size = queries.shape[0]
    kv_count = keys.shape[1]
    per_head = queries.shape[1] // kv_count
    blocks = size // TOK_DEV
    highest_precision = lax.Precision.HIGHEST
    query_wide = queries.astype(jnp.float32).reshape(size, kv_count, per_head, HEAD_WIDTH).transpose(1, 2, 0, 3)
    output_gradient_wide = output_gradient.astype(jnp.float32).reshape(size, kv_count, per_head, HEAD_WIDTH).transpose(1, 2, 0, 3)
    key_wide = keys.astype(jnp.float32).transpose(1, 0, 2)
    value_wide = values.astype(jnp.float32).transpose(1, 0, 2)
    softmax_scale = HEAD_WIDTH ** -0.5
    score_matrix = jnp.einsum("bvxj,bej->bvxe", query_wide, key_wide, precision=highest_precision) * softmax_scale
    causal = jnp.arange(size)[:, None] >= jnp.arange(size)[None, :]
    score_matrix = jnp.where(causal[None, None], score_matrix, -1e30)
    top = jnp.max(score_matrix, axis=-1, keepdims=True)
    raised = jnp.exp(score_matrix - top)
    probs = raised / jnp.sum(raised, axis=-1, keepdims=True)
    attention_weights = lax.optimization_barrier(probs.astype(jnp.bfloat16)).astype(jnp.float32)
    attended_output = jnp.einsum("ojcu,oue->ojce", attention_weights, value_wide, precision=highest_precision)
    delta = jnp.sum(output_gradient_wide * attended_output, axis=-1, keepdims=True)
    score_gradient = jnp.einsum("bvxj,bej->bvxe", output_gradient_wide, value_wide, precision=highest_precision)
    logit_gradient = lax.optimization_barrier((probs * (score_gradient - delta)).astype(jnp.bfloat16)).astype(jnp.float32)
    query_gradient = jnp.einsum("ojcu,oue->ojce", logit_gradient, key_wide, precision=highest_precision) * softmax_scale
    shape_b = (kv_count, per_head, blocks, TOK_DEV)
    logit_b = logit_gradient.reshape(shape_b + (size,))
    weights_b = attention_weights.reshape(shape_b + (size,))
    query_b = query_wide.reshape(shape_b + (HEAD_WIDTH,))
    grad_b = output_gradient_wide.reshape(shape_b + (HEAD_WIDTH,))
    key_blocks = jnp.einsum("grbus,grbud->bgsd", logit_b, query_b, precision=highest_precision) * softmax_scale
    value_blocks = jnp.einsum("grbus,grbud->bgsd", weights_b, grad_b, precision=highest_precision)
    key_blocks = lax.optimization_barrier(key_blocks.astype(jnp.bfloat16)).astype(jnp.float32)
    value_blocks = lax.optimization_barrier(value_blocks.astype(jnp.bfloat16)).astype(jnp.float32)
    key_gradient = jnp.sum(key_blocks, axis=0)
    value_gradient = jnp.sum(value_blocks, axis=0)
    query_gradient = query_gradient.transpose(2, 0, 1, 3).reshape(size, kv_count * per_head, HEAD_WIDTH).astype(jnp.bfloat16)
    key_gradient = key_gradient.transpose(1, 0, 2).astype(jnp.bfloat16)
    value_gradient = value_gradient.transpose(1, 0, 2).astype(jnp.bfloat16)
    return query_gradient, key_gradient, value_gradient


def to_groups(array):
    return array.reshape(TOKEN_LENGTH // GROUP, GROUP, array.shape[1], array.shape[2])


def from_groups(array):
    return array.reshape(TOKEN_LENGTH, array.shape[2], array.shape[3])


def half_grads(queries, keys, values, output_gradient):
    grads = lax.map(group_grads, (to_groups(queries), to_groups(keys), to_groups(values), to_groups(output_gradient)))
    return tuple(from_groups(piece) for piece in grads)


def sequence_grads(block):
    queries, keys, values, output_gradient = block
    queries = queries.reshape(TOKEN_LENGTH, QUERY_HEAD_COUNT, HEAD_WIDTH)
    output_gradient = output_gradient.reshape(TOKEN_LENGTH, QUERY_HEAD_COUNT, HEAD_WIDTH)
    keys = keys.reshape(TOKEN_LENGTH, KEY_VALUE_HEADS, HEAD_WIDTH)
    values = values.reshape(TOKEN_LENGTH, KEY_VALUE_HEADS, HEAD_WIDTH)
    query_half = QUERY_HEAD_COUNT // 2
    key_half = KEY_VALUE_HEADS // 2
    plain = half_grads(queries[:, :query_half], keys[:, :key_half], values[:, :key_half], output_gradient[:, :query_half])
    offset = GROUP // 2
    rolled = half_grads(jnp.roll(queries[:, query_half:], -offset, 0), jnp.roll(keys[:, key_half:], -offset, 0),
                        jnp.roll(values[:, key_half:], -offset, 0), jnp.roll(output_gradient[:, query_half:], -offset, 0))
    rolled = tuple(jnp.roll(piece, offset, 0) for piece in rolled)
    query_gradient = jnp.concatenate([plain[0], rolled[0]], axis=1).reshape(TOKEN_LENGTH, QUERY_HEAD_COUNT * HEAD_WIDTH)
    key_gradient = jnp.concatenate([plain[1], rolled[1]], axis=1).reshape(TOKEN_LENGTH, KEY_VALUE_HEADS * HEAD_WIDTH)
    value_gradient = jnp.concatenate([plain[2], rolled[2]], axis=1).reshape(TOKEN_LENGTH, KEY_VALUE_HEADS * HEAD_WIDTH)
    return query_gradient, key_gradient, value_gradient


def reference(queries, keys, values, output_gradient, adapter_query_down, adapter_value_down):
    query_gradient, key_gradient, value_gradient = lax.map(sequence_grads, (queries, keys, values, output_gradient))
    adapter_query_up_gradient = ADAPTER_SCALE * jnp.dot(adapter_query_down.reshape(-1, ADAPTER_RANK).T, query_gradient.reshape(-1, QUERY_HEAD_COUNT * HEAD_WIDTH),
                                           preferred_element_type=jnp.float32)
    adapter_value_up_gradient = ADAPTER_SCALE * jnp.dot(adapter_value_down.reshape(-1, ADAPTER_RANK).T, value_gradient.reshape(-1, KEY_VALUE_HEADS * HEAD_WIDTH),
                                           preferred_element_type=jnp.float32)
    return query_gradient, key_gradient, value_gradient, adapter_query_up_gradient, adapter_value_up_gradient
```

```python
import jax
import jax.numpy as jnp
from jax import lax
from jax.experimental import pallas as pl
from jax.experimental.pallas import tpu as pltpu
from jax.sharding import Mesh, PartitionSpec as P

QUERY_HEAD_COUNT = 32
KEY_VALUE_HEADS = 4
WIDTH = 128
ROWS = 128
RANK = 16
GROUP_DEVS = 4
ADAPTER_SCALE = 2.0
SOFTMAX_SCALE = WIDTH ** (-0.5)
LOG2E = 1.4426950408889634
PER_HEAD = QUERY_HEAD_COUNT // KEY_VALUE_HEADS
HALF_HEADS = QUERY_HEAD_COUNT // 2
UNIT = 4 * ROWS
SEL_ROWS = UNIT + RANK
FULL_ROWS = SEL_ROWS + UNIT
ADAPTER_ROWS = 640
HALF_ADAPTER_ROWS = (HALF_HEADS + 2) * RANK

AXES = ("x", "zl", "yh", "yl", "zh", "core")
SIZES = (4, 2, 4, 2, 4, 2)
CTX = ("x", "zl", "yh", "yl")
DP = ("zh", "core")
NEAR = ("x", "zl", "yl", "core")
FAR = ("yh", "zh")
CTX_SIZE = 64

NT = (((1,), (1,)), ((), ()))
NN = (((1,), (0,)), ((), ()))
bf16 = jnp.bfloat16
f32 = jnp.float32


def dot(a, b, dims):
    return lax.dot_general(a, b, dims, preferred_element_type=f32)


def eye(n):
    return (
        lax.broadcasted_iota(jnp.int32, (n, n), 0) == lax.broadcasted_iota(jnp.int32, (n, n), 1)
    ).astype(bf16)


def transposed_narrow(narrow):
    return dot(eye(RANK), narrow, NT).astype(bf16)


def head_columns(head):
    return pl.ds(pl.multiple_of(head * WIDTH, WIDTH), WIDTH)


def pack_kernel(place_ref, k_ref, v_ref, av_ref, full_ref, sel_ref):
    short = place_ref[0]
    av_t = transposed_narrow(av_ref[...])
    for which, half in ((0, short), (1, 1 - short)):
        base = which * SEL_ROWS
        for part, ref in ((0, k_ref), (1, v_ref)):
            for h in range(2):
                block = ref[:, head_columns(half * 2 + h)]
                rows = pl.ds(base + (part * 2 + h) * ROWS, ROWS)
                full_ref[rows, :] = block
                if which == 0:
                    sel_ref[rows, :] = block
    full_ref[UNIT:SEL_ROWS, :] = av_t
    sel_ref[UNIT:SEL_ROWS, :] = av_t


def attend_head(q_ref, g_ref, keys, values, av_t, aq_t, dq_ref, ad_ref):
    count = len(keys)
    key_all = jnp.concatenate(keys, axis=0) if count > 1 else keys[0]
    value_all = jnp.concatenate(values, axis=0) if count > 1 else values[0]
    key_t = key_all.T
    step = 2
    q_list, g_list, w_list, s_list = [], [], [], []
    allowed = lax.broadcasted_iota(jnp.int32, (ROWS, ROWS), 0) <= lax.broadcasted_iota(
        jnp.int32, (ROWS, ROWS), 1
    )
    allowed = jnp.concatenate([allowed.astype(f32)] * step, axis=1) > 0.5
    for c in range(PER_HEAD // step):
        heads = range(c * step, (c + 1) * step)
        q = jnp.concatenate([q_ref[:, h * WIDTH : (h + 1) * WIDTH] for h in heads], axis=0)
        g = jnp.concatenate([g_ref[:, h * WIDTH : (h + 1) * WIDTH] for h in heads], axis=0)
        scores = dot(key_all, q, NT)
        diagonal = jnp.where(allowed, scores[:ROWS], -1e30)
        scores = jnp.concatenate([diagonal, scores[ROWS:]], axis=0) if count > 1 else diagonal
        top = jnp.max(scores, axis=0, keepdims=True)
        raised = jnp.exp2((scores - top) * (SOFTMAX_SCALE * LOG2E))
        probs = raised * (1.0 / jnp.sum(raised, axis=0, keepdims=True))
        weights = probs.astype(bf16)
        score_grad = dot(value_all, g, NT)
        delta = jnp.sum(probs * score_grad, axis=0, keepdims=True)
        logit_grad = (probs * (score_grad - delta)).astype(bf16)
        dq_t = (dot(key_t, logit_grad, NN) * SOFTMAX_SCALE).astype(bf16)
        for i, h in enumerate(heads):
            part = dq_t[:, i * ROWS : (i + 1) * ROWS]
            dq_ref[:, h * WIDTH : (h + 1) * WIDTH] = part.T
            ad_ref[h * RANK : (h + 1) * RANK, :] = dot(aq_t, part, NT).astype(bf16)
        q_list.append(q)
        g_list.append(g)
        w_list.append(weights)
        s_list.append(logit_grad)
    q_all = jnp.concatenate(q_list, axis=0)
    g_all = jnp.concatenate(g_list, axis=0)
    dk = (dot(jnp.concatenate(s_list, axis=1), q_all, NN) * SOFTMAX_SCALE).astype(bf16)
    dv = dot(jnp.concatenate(w_list, axis=1), g_all, NN).astype(bf16)
    av_all = jnp.concatenate(av_t, axis=1) if count > 1 else av_t[0]
    ad_v = dot(av_all, dv, NN).astype(bf16)
    return dk, dv, ad_v


def block_of(ref, base, g):
    k = ref[pl.ds(pl.multiple_of(base + g * ROWS, 16), ROWS), :]
    v = ref[pl.ds(pl.multiple_of(base + (2 + g) * ROWS, 16), ROWS), :]
    return k, v


def put(ref, base, g, dk, dv):
    ref[pl.ds(pl.multiple_of(base + g * ROWS, 16), ROWS), :] = dk
    ref[pl.ds(pl.multiple_of(base + (2 + g) * ROWS, 16), ROWS), :] = dv


def run_head(blocks, outs, q_ref, g_ref, aq_ref, dq_ref, ad_ref):
    g = pl.program_id(0)
    aq_t = transposed_narrow(aq_ref[...])
    pairs = [block_of(ref, base, g) for ref, base in blocks]
    av_t = [ref[UNIT:SEL_ROWS, :] for ref, _ in blocks]
    dk, dv, ad_v = attend_head(
        q_ref, g_ref, [p[0] for p in pairs], [p[1] for p in pairs], av_t, aq_t, dq_ref, ad_ref
    )
    for n, (ref, base) in enumerate(outs):
        rows = slice(n * ROWS, (n + 1) * ROWS)
        put(ref, base, g, dk[rows], dv[rows])
    return ad_v


def short_kernel(place_ref, q_ref, g_ref, aq_ref, full_ref, one_ref, dq_ref, ad_ref, own_ref, back_ref, adq):
    g = pl.program_id(0)
    odd = place_ref[1]

    def go(blocks, outs):
        ad_v = run_head(blocks, outs, q_ref, g_ref, aq_ref, dq_ref, adq)
        ad_ref[pl.ds(pl.multiple_of(g * PER_HEAD * RANK, 16), PER_HEAD * RANK), :] = adq[...]
        ad_ref[pl.ds(pl.multiple_of(HALF_HEADS * RANK + g * RANK, 16), RANK), :] = ad_v

    @pl.when(odd == 0)
    def _():
        go([(full_ref, 0)], [(own_ref, 0)])

    @pl.when(odd == 1)
    def _():
        go([(full_ref, 0), (one_ref, 0)], [(own_ref, 0), (back_ref, 0)])


def long_kernel(
    place_ref, q_ref, g_ref, aq_ref, full_ref, one_ref, two_ref, three_ref, ads_ref, backs_ref, dq_in,
    dq_ref, ad_ref, own_ref, r1_ref, r2_ref, r3_ref, adq,
):
    g = pl.program_id(0)
    short = place_ref[0]
    odd = place_ref[1]
    long = 1 - short

    @pl.when(g == 0)
    def _():
        ad_ref[QUERY_HEAD_COUNT * RANK + 4 * RANK :, :] = jnp.zeros(
            (ADAPTER_ROWS - (QUERY_HEAD_COUNT + 4) * RANK, WIDTH), bf16
        )
        n = HALF_HEADS * RANK
        ad_ref[pl.ds(pl.multiple_of(short * n, 16), n), :] = ads_ref[:n, :]
        ad_ref[pl.ds(pl.multiple_of(2 * n + short * 2 * RANK, 16), 2 * RANK), :] = ads_ref[n:, :]

    def go(blocks, outs):
        ad_v = run_head(blocks, outs, q_ref, g_ref, aq_ref, dq_ref, adq)
        n = PER_HEAD * RANK
        ad_ref[pl.ds(pl.multiple_of((long * 2 + g) * n, 16), n), :] = adq[...]
        ad_ref[pl.ds(pl.multiple_of(QUERY_HEAD_COUNT * RANK + (long * 2 + g) * RANK, 16), RANK), :] = ad_v

    @pl.when(odd == 0)
    def _():
        go(
            [(full_ref, SEL_ROWS), (one_ref, 0), (two_ref, 0)],
            [(own_ref, 0), (r1_ref, 0), (r2_ref, 0)],
        )

    @pl.when(odd == 1)
    def _():
        go(
            [(full_ref, SEL_ROWS), (one_ref, SEL_ROWS), (two_ref, 0), (three_ref, 0)],
            [(own_ref, 0), (r1_ref, UNIT), (r2_ref, 0), (r3_ref, 0)],
        )

    @pl.when((g == 0) & (odd == 0))
    def _():
        r1_ref[UNIT:, :] = jnp.zeros((UNIT, WIDTH), bf16)

    @pl.when((g == 0) & (odd == 1))
    def _():
        r1_ref[:UNIT, :] = backs_ref[...]


def finish_kernel(place_ref, sum_ref, short_ref, long_ref, r1_ref, r2_ref, r3_ref, dk_ref, dv_ref, aq_ref, av_ref):
    short = place_ref[0]
    even = place_ref[1] == 0
    for part, ref in ((0, dk_ref), (1, dv_ref)):
        for h in range(2):
            base = (part * 2 + h) * ROWS
            rows = slice(base, base + ROWS)
            total = short_ref[rows, :].astype(f32) + r1_ref[rows, :].astype(f32)
            total = total + r2_ref[rows, :].astype(f32)
            total = total + jnp.where(even, r3_ref[rows, :].astype(f32), 0.0)
            ref[:, head_columns(short * 2 + h)] = total.astype(bf16)
            other = r1_ref[UNIT + base : UNIT + base + ROWS, :].astype(f32)
            total = long_ref[rows, :].astype(f32) + jnp.where(even, other, 0.0)
            ref[:, head_columns((1 - short) * 2 + h)] = total.astype(bf16)
    for h in range(QUERY_HEAD_COUNT):
        aq_ref[:, h * WIDTH : (h + 1) * WIDTH] = (
            sum_ref[h * RANK : (h + 1) * RANK, :].astype(f32) * ADAPTER_SCALE
        )
    for h in range(KEY_VALUE_HEADS):
        base = (QUERY_HEAD_COUNT + h) * RANK
        av_ref[:, h * WIDTH : (h + 1) * WIDTH] = sum_ref[base : base + RANK, :].astype(f32) * ADAPTER_SCALE


def shape(dims, kind=bf16):
    return jax.ShapeDtypeStruct(dims, kind)


def whole(dims):
    return pl.BlockSpec(dims, lambda *_: (0,) * len(dims))


def passed_along(block, distance, senders=range(CTX_SIZE)):
    return lax.ppermute(block, CTX, [(i, (i + distance) % CTX_SIZE) for i in senders])


PARAMS = pltpu.CompilerParams(vmem_limit_bytes=48 * 1024 * 1024)


def pack(place, k, v, av):
    return pl.pallas_call(
        pack_kernel,
        grid_spec=pltpu.PrefetchScalarGridSpec(
            num_scalar_prefetch=1,
            grid=(1,),
            in_specs=[whole(k.shape), whole(v.shape), whole(av.shape)],
            out_specs=[whole((FULL_ROWS, WIDTH)), whole((SEL_ROWS, WIDTH))],
        ),
        out_shape=[shape((FULL_ROWS, WIDTH)), shape((SEL_ROWS, WIDTH))],
        compiler_params=PARAMS,
        name="pack",
    )(place, k, v, av)


HEAD_COLUMNS = PER_HEAD * WIDTH


def attend_short(place, q, grad, aq, full, one):
    half = pl.BlockSpec((ROWS, HEAD_COLUMNS), lambda g, place: (0, place[0] * 2 + g))
    return pl.pallas_call(
        short_kernel,
        grid_spec=pltpu.PrefetchScalarGridSpec(
            num_scalar_prefetch=1,
            grid=(2,),
            in_specs=[half, half, whole(aq.shape), whole(full.shape), whole(one.shape)],
            out_specs=[half, whole((HALF_ADAPTER_ROWS, WIDTH)), whole((UNIT, WIDTH)), whole((UNIT, WIDTH))],
            scratch_shapes=[pltpu.VMEM((PER_HEAD * RANK, WIDTH), bf16)],
        ),
        out_shape=[
            shape(q.shape),
            shape((HALF_ADAPTER_ROWS, WIDTH)),
            shape((UNIT, WIDTH)),
            shape((UNIT, WIDTH)),
        ],
        compiler_params=PARAMS,
        cost_estimate=pl.CostEstimate(flops=700_000_000, bytes_accessed=3_000_000, transcendentals=0),
        name="short",
    )(place, q, grad, aq, full, one)


def attend_long(place, q, grad, aq, full, one, two, three, ads, backs, dq):
    half = pl.BlockSpec((ROWS, HEAD_COLUMNS), lambda g, place: (0, (1 - place[0]) * 2 + g))
    return pl.pallas_call(
        long_kernel,
        grid_spec=pltpu.PrefetchScalarGridSpec(
            num_scalar_prefetch=1,
            grid=(2,),
            in_specs=[half, half]
            + [whole(a.shape) for a in (aq, full, one, two, three, ads, backs)]
            + [pl.BlockSpec(memory_space=pl.ANY)],
            out_specs=[
                half,
                whole((ADAPTER_ROWS, WIDTH)),
                whole((UNIT, WIDTH)),
                whole((2 * UNIT, WIDTH)),
                whole((UNIT, WIDTH)),
                whole((UNIT, WIDTH)),
            ],
            scratch_shapes=[pltpu.VMEM((PER_HEAD * RANK, WIDTH), bf16)],
        ),
        out_shape=[
            shape(q.shape),
            shape((ADAPTER_ROWS, WIDTH)),
            shape((UNIT, WIDTH)),
            shape((2 * UNIT, WIDTH)),
            shape((UNIT, WIDTH)),
            shape((UNIT, WIDTH)),
        ],
        input_output_aliases={10: 0},
        compiler_params=PARAMS,
        cost_estimate=pl.CostEstimate(flops=1_400_000_000, bytes_accessed=4_000_000, transcendentals=0),
        name="long",
    )(place, q, grad, aq, full, one, two, three, ads, backs, dq)


def finish(place, total, short, long, r1, r2, r3):
    operands = (total, short, long, r1, r2, r3)
    outs = [
        shape((ROWS, KEY_VALUE_HEADS * WIDTH)),
        shape((ROWS, KEY_VALUE_HEADS * WIDTH)),
        shape((RANK, QUERY_HEAD_COUNT * WIDTH), f32),
        shape((RANK, KEY_VALUE_HEADS * WIDTH), f32),
    ]
    return pl.pallas_call(
        finish_kernel,
        grid_spec=pltpu.PrefetchScalarGridSpec(
            num_scalar_prefetch=1,
            grid=(1,),
            in_specs=[whole(a.shape) for a in operands],
            out_specs=[whole(o.shape) for o in outs],
        ),
        out_shape=outs,
        compiler_params=PARAMS,
        name="finish",
    )(place, *operands)


def copies_to_all(block, axes):
    size = lax.axis_size(axes)
    return lax.all_to_all(jnp.broadcast_to(block[None], (size,) + block.shape), axes, 0, 0)


def summed(pieces):
    return jnp.sum(pieces.astype(f32), axis=0).astype(bf16)


def sum_over_all(part):
    size = lax.axis_size(NEAR)
    mine = summed(lax.all_to_all(part.reshape(size, part.shape[0] // size, WIDTH), NEAR, 0, 0))
    mine = summed(copies_to_all(mine, FAR))
    return copies_to_all(mine, NEAR).reshape(part.shape)


def body(queries, keys, values, output_gradient, adapter_query_down, adapter_value_down):
    position = lax.axis_index(CTX) % GROUP_DEVS
    place = jnp.stack([position // 2, position % 2]).astype(jnp.int32)
    q, grad, aq = queries[0], output_gradient[0], adapter_query_down[0]
    full, sel = pack(place, keys[0], values[0], adapter_value_down[0])
    one = passed_along(full, 1)
    two = passed_along(sel, 2)
    three = passed_along(sel, 3, range(0, CTX_SIZE, 2))
    dq, ads, own_short, backs = attend_short(place, q, grad, aq, full, one)
    dq, part, own_long, r1, r2, r3 = attend_long(
        place, q, grad, aq, full, one, two, three, ads, backs, dq
    )
    r1 = passed_along(r1, -1)
    r2 = passed_along(r2, -2)
    r3 = passed_along(r3, -3, range(1, CTX_SIZE, 2))
    total = sum_over_all(part)
    dk, dv, adapter_q, adapter_v = finish(place, total, own_short, own_long, r1, r2, r3)
    return dq[None], dk[None], dv[None], adapter_q, adapter_v


def solution(mesh):
    split = Mesh(mesh.devices.reshape(SIZES), AXES)
    tokens = P(DP, CTX, None)
    return jax.shard_map(
        body,
        mesh=split,
        in_specs=(tokens,) * 6,
        out_specs=(tokens, tokens, tokens, P(), P()),
        check_vma=False,
    )
```

```python
import jax
import jax.numpy as jnp
from jax import lax
from jax.experimental import pallas as pl
from jax.experimental.pallas import tpu as pltpu
from jax.sharding import Mesh, PartitionSpec as P

QUERY_HEAD_COUNT = 32
KEY_VALUE_HEADS = 4
WIDTH = 128
ROWS = 128
RANK = 16
GROUP_DEVS = 4
ADAPTER_SCALE = 2.0
SOFTMAX_SCALE = WIDTH ** (-0.5)
LOG2E = 1.4426950408889634
STEP = 8
PER_HEAD = QUERY_HEAD_COUNT // KEY_VALUE_HEADS
HALF_HEADS = QUERY_HEAD_COUNT // 2
UNIT = 4 * ROWS
SEL_ROWS = UNIT + RANK
ADAPTER_ROWS = 640
HALF_ADAPTER_ROWS = (HALF_HEADS + 2) * RANK

AXES = ("x", "zl", "yh", "yl", "zh", "core")
SIZES = (4, 2, 4, 2, 4, 2)
CTX = ("x", "zl", "yh", "yl")
DP = ("zh", "core")
NEAR = ("x", "zl", "yl", "core")
FAR = ("yh", "zh")
CTX_SIZE = 64

NT = (((1,), (1,)), ((), ()))
NN = (((1,), (0,)), ((), ()))
bf16 = jnp.bfloat16
f32 = jnp.float32


def dot(a, b, dims):
    return lax.dot_general(a, b, dims, preferred_element_type=f32)


def head_columns(head):
    return pl.ds(pl.multiple_of(head * WIDTH, WIDTH), WIDTH)


def pack_kernel(place_ref, k_ref, v_ref, av_ref, sel_ref, oth_ref, sems):
    short = place_ref[0]
    copies = []

    def start(src, dst):
        copy = pltpu.make_async_copy(src, dst, sems.at[len(copies)])
        copy.start()
        copies.append(copy)

    for half, packed in ((short, sel_ref), (1 - short, oth_ref)):
        for part, ref in ((0, k_ref), (1, v_ref)):
            for h in range(2):
                block = ref.at[:, head_columns(half * 2 + h)]
                start(block, packed.at[pl.ds((part * 2 + h) * ROWS, ROWS)])
    start(av_ref, sel_ref.at[pl.ds(UNIT, RANK)])
    for copy in copies:
        copy.wait()


def attend_head(q_ref, g_ref, dq_ref, g, keys, values, av_t, aq_t, put_adapter):
    count = len(keys)
    key_all = jnp.concatenate(keys, axis=0) if count > 1 else keys[0]
    value_all = jnp.concatenate(values, axis=0) if count > 1 else values[0]
    key_t = key_all.T
    allowed = lax.broadcasted_iota(jnp.int32, (ROWS, STEP * ROWS), 0) <= (
        lax.broadcasted_iota(jnp.int32, (ROWS, STEP * ROWS), 1) % ROWS
    )
    q_list, g_list, w_list, s_list = [], [], [], []
    for c in range(PER_HEAD // STEP):
        heads = range(g * PER_HEAD + c * STEP, g * PER_HEAD + (c + 1) * STEP)
        q = jnp.concatenate([q_ref[:, h * WIDTH : (h + 1) * WIDTH] for h in heads], axis=0)
        grad = jnp.concatenate([g_ref[:, h * WIDTH : (h + 1) * WIDTH] for h in heads], axis=0)
        scores = dot(key_all, q, NT)
        score_grad = dot(value_all, grad, NT)
        diagonal = jnp.where(allowed, scores[:ROWS], -1e30)
        scores = jnp.concatenate([diagonal, scores[ROWS:]], axis=0) if count > 1 else diagonal
        top = jnp.max(scores, axis=0, keepdims=True)
        raised = jnp.exp2((scores - top) * (SOFTMAX_SCALE * LOG2E))
        probs = raised * (1.0 / jnp.sum(raised, axis=0, keepdims=True))
        delta = jnp.sum(probs * score_grad, axis=0, keepdims=True)
        logit_grad = (probs * (score_grad - delta)).astype(bf16)
        dq_t = (dot(key_t, logit_grad, NN) * SOFTMAX_SCALE).astype(bf16)
        dq = jnp.concatenate([dq_t[:, i * ROWS : (i + 1) * ROWS].T for i in range(STEP)], axis=1)
        dq_ref[:, heads[0] * WIDTH : (heads[-1] + 1) * WIDTH] = dq
        adapter = dot(aq_t, dq, NN).astype(bf16)
        for i, h in enumerate(heads):
            put_adapter(h, adapter[:, i * WIDTH : (i + 1) * WIDTH])
        q_list.append(q)
        g_list.append(grad)
        w_list.append(probs.astype(bf16))
        s_list.append(logit_grad)
    q_all = jnp.concatenate(q_list, axis=0)
    g_all = jnp.concatenate(g_list, axis=0)
    dk = (dot(jnp.concatenate(s_list, axis=1), q_all, NN) * SOFTMAX_SCALE).astype(bf16)
    dv = dot(jnp.concatenate(w_list, axis=1), g_all, NN).astype(bf16)
    av_all = jnp.concatenate(av_t, axis=1) if count > 1 else av_t[0]
    return dk, dv, dot(av_all, dv, NN).astype(bf16)


def attend_half(half, q_hbm, g_hbm, dq_hbm, q_ref, g_ref, dq_ref, sems, variants, aq_t, put_adapter, put_value):
    copies = []
    for g in range(2):
        here = pl.ds(g * HEAD_COLUMNS, HEAD_COLUMNS)
        there = pl.ds(pl.multiple_of(half * HALF_COLUMNS + g * HEAD_COLUMNS, WIDTH), HEAD_COLUMNS)
        copies.append(
            [
                pltpu.make_async_copy(q_hbm.at[:, there], q_ref.at[:, here], sems.at[g]),
                pltpu.make_async_copy(g_hbm.at[:, there], g_ref.at[:, here], sems.at[2 + g]),
                pltpu.make_async_copy(dq_ref.at[:, here], dq_hbm.at[:, there], sems.at[4 + g]),
            ]
        )
    for copy in copies:
        copy[0].start()
        copy[1].start()

    def go(blocks, av_refs, outs):
        for g in range(2):
            copies[g][0].wait()
            copies[g][1].wait()
            keys = [ref[g * ROWS : (g + 1) * ROWS, :] for ref in blocks]
            values = [ref[(2 + g) * ROWS : (3 + g) * ROWS, :] for ref in blocks]
            av_t = [ref[UNIT:SEL_ROWS, :] for ref in av_refs]
            dk, dv, ad_v = attend_head(q_ref, g_ref, dq_ref, g, keys, values, av_t, aq_t, put_adapter)
            copies[g][2].start()
            put_value(g, ad_v)
            for n, (ref, base) in enumerate(outs):
                rows = slice(n * ROWS, (n + 1) * ROWS)
                ref[base + g * ROWS : base + (g + 1) * ROWS, :] = dk[rows]
                ref[base + (2 + g) * ROWS : base + (3 + g) * ROWS, :] = dv[rows]

    for condition, *rest in variants:
        pl.when(condition)(lambda rest=rest: go(*rest))
    copies[0][2].wait()
    copies[1][2].wait()


def short_kernel(
    place_ref, aq_ref, sel_ref, one_ref, q_hbm, g_hbm, dq_hbm, ad_ref, own_ref, back_ref, q_ref, g_ref, dq_ref, sems
):
    odd = place_ref[1]

    def put_adapter(h, value):
        ad_ref[h * RANK : (h + 1) * RANK, :] = value

    def put_value(g, value):
        ad_ref[(HALF_HEADS + g) * RANK : (HALF_HEADS + g + 1) * RANK, :] = value

    variants = [
        (odd == 0, [sel_ref], [sel_ref], [(own_ref, 0)]),
        (odd == 1, [sel_ref, one_ref], [sel_ref, one_ref], [(own_ref, 0), (back_ref, 0)]),
    ]
    attend_half(
        place_ref[0], q_hbm, g_hbm, dq_hbm, q_ref, g_ref, dq_ref, sems, variants, aq_ref[...], put_adapter, put_value
    )


def long_kernel(
    place_ref, aq_ref, sel_ref, oth_ref, one_ref, other_ref, two_ref, three_ref, ads_ref, backs_ref, q_hbm, g_hbm, dq_in,
    dq_hbm, ad_ref, own_ref, r1_ref, r2_ref, r3_ref, q_ref, g_ref, dq_ref, sems,
):
    short = place_ref[0]
    odd = place_ref[1]
    long = 1 - short
    n = HALF_HEADS * RANK

    def put_adapter(h, value):
        ad_ref[pl.ds(pl.multiple_of(long * n + h * RANK, RANK), RANK), :] = value

    def put_value(g, value):
        ad_ref[pl.ds(pl.multiple_of(2 * n + (long * 2 + g) * RANK, RANK), RANK), :] = value

    variants = [
        (
            odd == 0,
            [oth_ref, one_ref, two_ref],
            [sel_ref, one_ref, two_ref],
            [(own_ref, 0), (r1_ref, 0), (r2_ref, 0)],
        ),
        (
            odd == 1,
            [oth_ref, other_ref, two_ref, three_ref],
            [sel_ref, one_ref, two_ref, three_ref],
            [(own_ref, 0), (r1_ref, UNIT), (r2_ref, 0), (r3_ref, 0)],
        ),
    ]
    attend_half(long, q_hbm, g_hbm, dq_hbm, q_ref, g_ref, dq_ref, sems, variants, aq_ref[...], put_adapter, put_value)
    ad_ref[2 * n + 4 * RANK :, :] = jnp.zeros((ADAPTER_ROWS - 2 * n - 4 * RANK, WIDTH), bf16)
    ad_ref[pl.ds(pl.multiple_of(short * n, RANK), n), :] = ads_ref[:n, :]
    ad_ref[pl.ds(pl.multiple_of(2 * n + short * 2 * RANK, RANK), 2 * RANK), :] = ads_ref[n:, :]

    @pl.when(odd == 0)
    def _():
        r1_ref[UNIT:, :] = jnp.zeros((UNIT, WIDTH), bf16)

    @pl.when(odd == 1)
    def _():
        r1_ref[:UNIT, :] = backs_ref[...]


def finish_kernel(place_ref, sum_ref, short_ref, long_ref, r1_ref, r2_ref, r3_ref, dk_ref, dv_ref, aq_ref, av_ref):
    short = place_ref[0]
    even = place_ref[1] == 0
    for part, ref in ((0, dk_ref), (1, dv_ref)):
        for h in range(2):
            base = (part * 2 + h) * ROWS
            rows = slice(base, base + ROWS)
            total = short_ref[rows, :].astype(f32) + r1_ref[rows, :].astype(f32)
            total = total + r2_ref[rows, :].astype(f32)
            total = total + jnp.where(even, r3_ref[rows, :].astype(f32), 0.0)
            ref[:, head_columns(short * 2 + h)] = total.astype(bf16)
            other = r1_ref[UNIT + base : UNIT + base + ROWS, :].astype(f32)
            total = long_ref[rows, :].astype(f32) + jnp.where(even, other, 0.0)
            ref[:, head_columns((1 - short) * 2 + h)] = total.astype(bf16)
    for h in range(QUERY_HEAD_COUNT):
        aq_ref[:, h * WIDTH : (h + 1) * WIDTH] = (
            sum_ref[h * RANK : (h + 1) * RANK, :].astype(f32) * ADAPTER_SCALE
        )
    for h in range(KEY_VALUE_HEADS):
        base = (QUERY_HEAD_COUNT + h) * RANK
        av_ref[:, h * WIDTH : (h + 1) * WIDTH] = sum_ref[base : base + RANK, :].astype(f32) * ADAPTER_SCALE


def shape(dims, kind=bf16):
    return jax.ShapeDtypeStruct(dims, kind)


def whole(dims):
    return pl.BlockSpec(dims, lambda *_: (0,) * len(dims))


def passed_along(block, distance, senders=range(CTX_SIZE)):
    return lax.ppermute(block, CTX, [(i, (i + distance) % CTX_SIZE) for i in senders])


PARAMS = pltpu.CompilerParams(vmem_limit_bytes=40 * 1024 * 1024)
HEAD_COLUMNS = PER_HEAD * WIDTH
HALF_COLUMNS = 2 * HEAD_COLUMNS
SMEM = pl.BlockSpec(memory_space=pltpu.SMEM)
VMEM = pl.BlockSpec(memory_space=pltpu.VMEM)
HBM = pl.BlockSpec(memory_space=pltpu.HBM)


def pack(place, k, v, av_t):
    return pl.pallas_call(
        pack_kernel,
        in_specs=[SMEM, HBM, HBM, HBM],
        out_specs=[VMEM, VMEM],
        out_shape=[shape((SEL_ROWS, WIDTH)), shape((UNIT, WIDTH))],
        scratch_shapes=[pltpu.SemaphoreType.DMA((9,))],
        compiler_params=PARAMS,
        name="pack",
    )(place, k, v, av_t)


HALF_SCRATCH = [
    pltpu.VMEM((ROWS, HALF_COLUMNS), bf16),
    pltpu.VMEM((ROWS, HALF_COLUMNS), bf16),
    pltpu.VMEM((ROWS, HALF_COLUMNS), bf16),
    pltpu.SemaphoreType.DMA((6,)),
]


def attend_short(place, aq_t, sel, one, q, grad):
    return pl.pallas_call(
        short_kernel,
        in_specs=[SMEM, VMEM, VMEM, VMEM, HBM, HBM],
        out_specs=[HBM, VMEM, VMEM, VMEM],
        out_shape=[
            shape(q.shape),
            shape((HALF_ADAPTER_ROWS, WIDTH)),
            shape((UNIT, WIDTH)),
            shape((UNIT, WIDTH)),
        ],
        scratch_shapes=HALF_SCRATCH,
        compiler_params=PARAMS,
        cost_estimate=pl.CostEstimate(flops=700_000_000, bytes_accessed=3_000_000, transcendentals=0),
        name="short",
    )(place, aq_t, sel, one, q, grad)


def attend_long(place, aq_t, sel, oth, one, other, two, three, ads, backs, q, grad, dq):
    return pl.pallas_call(
        long_kernel,
        in_specs=[SMEM] + [VMEM] * 9 + [HBM] * 3,
        out_specs=[HBM] + [VMEM] * 5,
        out_shape=[
            shape(q.shape),
            shape((ADAPTER_ROWS, WIDTH)),
            shape((UNIT, WIDTH)),
            shape((2 * UNIT, WIDTH)),
            shape((UNIT, WIDTH)),
            shape((UNIT, WIDTH)),
        ],
        scratch_shapes=HALF_SCRATCH,
        input_output_aliases={12: 0},
        compiler_params=PARAMS,
        cost_estimate=pl.CostEstimate(flops=1_400_000_000, bytes_accessed=4_000_000, transcendentals=0),
        name="long",
    )(place, aq_t, sel, oth, one, other, two, three, ads, backs, q, grad, dq)


def finish(place, total, short, long, r1, r2, r3):
    operands = (total, short, long, r1, r2, r3)
    outs = [
        shape((ROWS, KEY_VALUE_HEADS * WIDTH)),
        shape((ROWS, KEY_VALUE_HEADS * WIDTH)),
        shape((RANK, QUERY_HEAD_COUNT * WIDTH), f32),
        shape((RANK, KEY_VALUE_HEADS * WIDTH), f32),
    ]
    return pl.pallas_call(
        finish_kernel,
        grid_spec=pltpu.PrefetchScalarGridSpec(
            num_scalar_prefetch=1,
            grid=(1,),
            in_specs=[whole(a.shape) for a in operands],
            out_specs=[whole(o.shape) for o in outs],
        ),
        out_shape=outs,
        compiler_params=PARAMS,
        name="finish",
    )(place, *operands)


def copies_to_all(block, axes):
    size = lax.axis_size(axes)
    return lax.all_to_all(jnp.broadcast_to(block[None], (size,) + block.shape), axes, 0, 0)


def summed(pieces):
    return jnp.sum(pieces.astype(f32), axis=0).astype(bf16)


def sum_over_all(part, beside):
    size = lax.axis_size(NEAR)
    mine = summed(lax.all_to_all(part.reshape(size, part.shape[0] // size, WIDTH), NEAR, 0, 0))
    mine = summed(copies_to_all(mine, FAR))
    mine, beside = lax.optimization_barrier((mine, beside))
    return copies_to_all(mine, NEAR).reshape(part.shape), beside


def body(queries, keys, values, output_gradient, adapter_query_down, adapter_value_down):
    position = lax.axis_index(CTX) % GROUP_DEVS
    place = jnp.stack([position // 2, position % 2]).astype(jnp.int32)
    q, grad, aq_t = queries[0], output_gradient[0], adapter_query_down[0].T
    sel, oth = pack(place, keys[0], values[0], adapter_value_down[0].T)
    one = passed_along(sel, 1)
    two = passed_along(sel, 2)
    three = passed_along(sel, 3, range(0, CTX_SIZE, 2))
    other = passed_along(oth, 1, range(0, CTX_SIZE, 2))
    dq, ads, own_short, backs = attend_short(place, aq_t, sel, one, q, grad)
    dq, part, own_long, r1, r2, r3 = attend_long(
        place, aq_t, sel, oth, one, other, two, three, ads, backs, q, grad, dq
    )
    r1 = passed_along(r1, -1)
    r2 = passed_along(r2, -2)
    r3 = passed_along(r3, -3, range(1, CTX_SIZE, 2))
    total, (r1, r2, r3) = sum_over_all(part, (r1, r2, r3))
    dk, dv, adapter_q, adapter_v = finish(place, total, own_short, own_long, r1, r2, r3)
    return dq[None], dk[None], dv[None], adapter_q, adapter_v


def solution(mesh):
    split = Mesh(mesh.devices.reshape(SIZES), AXES)
    tokens = P(DP, CTX, None)
    return jax.shard_map(
        body,
        mesh=split,
        in_specs=(tokens,) * 6,
        out_specs=(tokens, tokens, tokens, P(), P()),
        check_vma=False,
    )
```

```python
import jax
import jax.numpy as jnp
from jax import lax
from jax.experimental import pallas as pl
from jax.experimental.pallas import tpu as pltpu
from jax.sharding import Mesh, PartitionSpec as P

QUERY_HEAD_COUNT = 32
KEY_VALUE_HEADS = 4
WIDTH = 128
ROWS = 128
RANK = 16
GROUP_DEVS = 4
ADAPTER_SCALE = 2.0
SOFTMAX_SCALE = WIDTH ** (-0.5)
LOG2E = 1.4426950408889634
PER_HEAD = QUERY_HEAD_COUNT // KEY_VALUE_HEADS
HALF_HEADS = QUERY_HEAD_COUNT // 2
UNIT = 4 * ROWS
SEL_ROWS = UNIT + RANK
ADAPTER_ROWS = 768
HALF_ADAPTER_ROWS = (HALF_HEADS + 2) * RANK

AXES = ("x", "zl", "yh", "yl", "zh", "core")
SIZES = (4, 2, 4, 2, 4, 2)
CTX = ("x", "zl", "yh", "yl")
DP = ("zh", "core")
NEAR = ("x", "zl", "yl", "core")
FAR = ("yh", "zh")
CTX_SIZE = 64

NT = (((1,), (1,)), ((), ()))
NN = (((1,), (0,)), ((), ()))
bf16 = jnp.bfloat16
f32 = jnp.float32


def dot(a, b, dims):
    return lax.dot_general(a, b, dims, preferred_element_type=f32)


def head_columns(head):
    return pl.ds(pl.multiple_of(head * WIDTH, WIDTH), WIDTH)


def attend_head(q_wide, g_wide, put_dq, keys, values, av_t, aq_t):
    count = len(keys)
    key_all = jnp.concatenate(keys, axis=0) if count > 1 else keys[0]
    value_all = jnp.concatenate(values, axis=0) if count > 1 else values[0]
    rows = PER_HEAD * ROWS
    allowed = lax.broadcasted_iota(jnp.int32, (ROWS, rows), 0) <= (
        lax.broadcasted_iota(jnp.int32, (ROWS, rows), 1) % ROWS
    )
    heads = [slice(h * WIDTH, (h + 1) * WIDTH) for h in range(PER_HEAD)]
    q = jnp.concatenate([q_wide[:, h] for h in heads], axis=0)
    grad = jnp.concatenate([g_wide[:, h] for h in heads], axis=0)
    scores = dot(key_all, q, NT)
    score_grad = dot(value_all, grad, NT)
    diagonal = jnp.where(allowed, scores[:ROWS], -1e30)
    scores = jnp.concatenate([diagonal, scores[ROWS:]], axis=0) if count > 1 else diagonal
    top = jnp.max(scores, axis=0, keepdims=True)
    raised = jnp.exp2((scores - top) * (SOFTMAX_SCALE * LOG2E))
    probs = raised * (1.0 / jnp.sum(raised, axis=0, keepdims=True))
    delta = jnp.sum(probs * score_grad, axis=0, keepdims=True)
    logit_grad = (probs * (score_grad - delta)).astype(bf16)
    dq_t = (dot(key_all.T, logit_grad, NN) * SOFTMAX_SCALE).astype(bf16)
    dq = jnp.concatenate([dq_t[:, h].T for h in heads], axis=1)
    put_dq(dq)
    dv = dot(probs.astype(bf16), grad, NN).astype(bf16)
    dk = (dot(logit_grad, q, NN) * SOFTMAX_SCALE).astype(bf16)
    av_all = jnp.concatenate(av_t, axis=1) if count > 1 else av_t[0]
    return dk, dv, dot(aq_t, dq, NN).astype(bf16), dot(av_all, dv, NN).astype(bf16)


def attend_half(half, q_ref, g_ref, dq_hbm, dq_ref, sems, variants, aq_t, put_adapter, put_value):
    def columns(g):
        return pl.ds(pl.multiple_of(half * HALF_COLUMNS + g * HEAD_COLUMNS, WIDTH), HEAD_COLUMNS)

    copies = [
        pltpu.make_async_copy(
            dq_ref.at[:, pl.ds(g * HEAD_COLUMNS, HEAD_COLUMNS)], dq_hbm.at[:, columns(g)], sems.at[g]
        )
        for g in range(2)
    ]

    def go(blocks, av_refs, outs):
        for g in range(2):
            keys = [ref[g * ROWS : (g + 1) * ROWS, :] for ref in blocks]
            values = [ref[(2 + g) * ROWS : (3 + g) * ROWS, :] for ref in blocks]
            av_t = [ref[UNIT:SEL_ROWS, :] for ref in av_refs]

            def put_dq(dq, g=g):
                dq_ref[:, g * HEAD_COLUMNS : (g + 1) * HEAD_COLUMNS] = dq
                copies[g].start()

            dk, dv, ad_q, ad_v = attend_head(
                q_ref[:, columns(g)], g_ref[:, columns(g)], put_dq, keys, values, av_t, aq_t
            )
            for h in range(PER_HEAD):
                put_adapter(g * PER_HEAD + h, ad_q[:, h * WIDTH : (h + 1) * WIDTH])
            put_value(g, ad_v)
            for n, (ref, base) in enumerate(outs):
                rows = slice(n * ROWS, (n + 1) * ROWS)
                ref[base + g * ROWS : base + (g + 1) * ROWS, :] = dk[rows]
                ref[base + (2 + g) * ROWS : base + (3 + g) * ROWS, :] = dv[rows]

    for condition, *rest in variants:
        pl.when(condition)(lambda rest=rest: go(*rest))
    copies[0].wait()
    copies[1].wait()


def short_kernel(
    place_ref, aq_ref, sel_ref, one_ref, q_ref, g_ref, dq_hbm, ad_ref, own_ref, back_ref, dq_ref, sems
):
    odd = place_ref[1]

    def put_adapter(h, value):
        ad_ref[h * RANK : (h + 1) * RANK, :] = value

    def put_value(g, value):
        ad_ref[(HALF_HEADS + g) * RANK : (HALF_HEADS + g + 1) * RANK, :] = value

    variants = [
        (odd == 0, [sel_ref], [sel_ref], [(own_ref, 0)]),
        (odd == 1, [sel_ref, one_ref], [sel_ref, one_ref], [(own_ref, 0), (back_ref, 0)]),
    ]
    attend_half(place_ref[0], q_ref, g_ref, dq_hbm, dq_ref, sems, variants, aq_ref[...], put_adapter, put_value)


def long_kernel(
    place_ref, aq_ref, sel_ref, oth_ref, one_ref, other_ref, two_ref, three_ref, ads_ref, backs_ref, q_ref, g_ref, dq_in,
    dq_hbm, ad_ref, own_ref, r1_ref, r2_ref, r3_ref, dq_ref, sems,
):
    short = place_ref[0]
    odd = place_ref[1]
    long = 1 - short
    n = HALF_HEADS * RANK

    def put_adapter(h, value):
        ad_ref[pl.ds(pl.multiple_of(long * n + h * RANK, RANK), RANK), :] = value

    def put_value(g, value):
        ad_ref[pl.ds(pl.multiple_of(2 * n + (long * 2 + g) * RANK, RANK), RANK), :] = value

    variants = [
        (
            odd == 0,
            [oth_ref, one_ref, two_ref],
            [sel_ref, one_ref, two_ref],
            [(own_ref, 0), (r1_ref, 0), (r2_ref, 0)],
        ),
        (
            odd == 1,
            [oth_ref, other_ref, two_ref, three_ref],
            [sel_ref, one_ref, two_ref, three_ref],
            [(own_ref, 0), (r1_ref, UNIT), (r2_ref, 0), (r3_ref, 0)],
        ),
    ]
    attend_half(long, q_ref, g_ref, dq_hbm, dq_ref, sems, variants, aq_ref[...], put_adapter, put_value)
    ad_ref[2 * n + 4 * RANK :, :] = jnp.zeros((ADAPTER_ROWS - 2 * n - 4 * RANK, WIDTH), bf16)
    ad_ref[pl.ds(pl.multiple_of(short * n, RANK), n), :] = ads_ref[:n, :]
    ad_ref[pl.ds(pl.multiple_of(2 * n + short * 2 * RANK, RANK), 2 * RANK), :] = ads_ref[n:, :]

    @pl.when(odd == 0)
    def _():
        r1_ref[UNIT:, :] = jnp.zeros((UNIT, WIDTH), bf16)

    @pl.when(odd == 1)
    def _():
        r1_ref[:UNIT, :] = backs_ref[...]


def key_sum_kernel(place_ref, short_ref, long_ref, r1_ref, r2_ref, r3_ref, dk_ref, dv_ref):
    short = place_ref[0]
    even = place_ref[1] == 0
    for part, ref in ((0, dk_ref), (1, dv_ref)):
        for h in range(2):
            base = (part * 2 + h) * ROWS
            rows = slice(base, base + ROWS)
            total = short_ref[rows, :].astype(f32) + r1_ref[rows, :].astype(f32)
            total = total + r2_ref[rows, :].astype(f32)
            total = total + jnp.where(even, r3_ref[rows, :].astype(f32), 0.0)
            ref[:, head_columns(short * 2 + h)] = total.astype(bf16)
            other = r1_ref[UNIT + base : UNIT + base + ROWS, :].astype(f32)
            total = long_ref[rows, :].astype(f32) + jnp.where(even, other, 0.0)
            ref[:, head_columns((1 - short) * 2 + h)] = total.astype(bf16)


def adapter_kernel(sum_ref, aq_ref, av_ref):
    for h in range(QUERY_HEAD_COUNT):
        aq_ref[:, h * WIDTH : (h + 1) * WIDTH] = (
            sum_ref[h * RANK : (h + 1) * RANK, :].astype(f32) * ADAPTER_SCALE
        )
    for h in range(KEY_VALUE_HEADS):
        base = (QUERY_HEAD_COUNT + h) * RANK
        av_ref[:, h * WIDTH : (h + 1) * WIDTH] = sum_ref[base : base + RANK, :].astype(f32) * ADAPTER_SCALE


def shape(dims, kind=bf16):
    return jax.ShapeDtypeStruct(dims, kind)


def whole(dims):
    return pl.BlockSpec(dims, lambda *_: (0,) * len(dims))


def passed_along(block, distance, senders=range(CTX_SIZE)):
    return lax.ppermute(block, CTX, [(i, (i + distance) % CTX_SIZE) for i in senders])


SUM_FLOPS = 20_000_000_000
PARAMS = pltpu.CompilerParams(vmem_limit_bytes=40 * 1024 * 1024)
HEAD_COLUMNS = PER_HEAD * WIDTH
HALF_COLUMNS = 2 * HEAD_COLUMNS
SMEM = pl.BlockSpec(memory_space=pltpu.SMEM)
VMEM = pl.BlockSpec(memory_space=pltpu.VMEM)
HBM = pl.BlockSpec(memory_space=pltpu.HBM)


def pack(short, k, v, av_t):
    half = 2 * WIDTH

    def chosen(array, first):
        return jnp.where(first, array[:, :half], array[:, half:])

    def stacked(first):
        pieces = [chosen(k, first), chosen(v, first)]
        return [piece[:, h * WIDTH : (h + 1) * WIDTH] for piece in pieces for h in range(2)]

    sel = jnp.concatenate(stacked(short == 0) + [av_t], axis=0)
    oth = jnp.concatenate(stacked(short == 1), axis=0)
    return sel, oth


HALF_SCRATCH = [pltpu.VMEM((ROWS, HALF_COLUMNS), bf16), pltpu.SemaphoreType.DMA((2,))]


def attend_short(place, aq_t, sel, one, q, grad):
    return pl.pallas_call(
        short_kernel,
        in_specs=[SMEM] + [VMEM] * 5,
        out_specs=[HBM, VMEM, VMEM, VMEM],
        out_shape=[
            shape(q.shape),
            shape((HALF_ADAPTER_ROWS, WIDTH)),
            shape((UNIT, WIDTH)),
            shape((UNIT, WIDTH)),
        ],
        scratch_shapes=HALF_SCRATCH,
        compiler_params=PARAMS,
        cost_estimate=pl.CostEstimate(flops=700_000_000, bytes_accessed=3_000_000, transcendentals=0),
        name="short",
    )(place, aq_t, sel, one, q, grad)


def attend_long(place, aq_t, sel, oth, one, other, two, three, ads, backs, q, grad, dq):
    return pl.pallas_call(
        long_kernel,
        in_specs=[SMEM] + [VMEM] * 11 + [HBM],
        out_specs=[HBM] + [VMEM] * 5,
        out_shape=[
            shape(q.shape),
            shape((ADAPTER_ROWS, WIDTH)),
            shape((UNIT, WIDTH)),
            shape((2 * UNIT, WIDTH)),
            shape((UNIT, WIDTH)),
            shape((UNIT, WIDTH)),
        ],
        scratch_shapes=HALF_SCRATCH,
        input_output_aliases={12: 0},
        compiler_params=PARAMS,
        cost_estimate=pl.CostEstimate(flops=1_400_000_000, bytes_accessed=4_000_000, transcendentals=0),
        name="long",
    )(place, aq_t, sel, oth, one, other, two, three, ads, backs, q, grad, dq)


def key_sums(place, short, long, r1, r2, r3):
    out = shape((ROWS, KEY_VALUE_HEADS * WIDTH))
    return pl.pallas_call(
        key_sum_kernel,
        in_specs=[SMEM] + [VMEM] * 5,
        out_specs=[VMEM, VMEM],
        out_shape=[out, out],
        compiler_params=PARAMS,
        cost_estimate=pl.CostEstimate(flops=SUM_FLOPS, bytes_accessed=2_000_000, transcendentals=0),
        name="key_sums",
    )(place, short, long, r1, r2, r3)


def adapter_out(total):
    return pl.pallas_call(
        adapter_kernel,
        in_specs=[VMEM],
        out_specs=[VMEM, VMEM],
        out_shape=[
            shape((RANK, QUERY_HEAD_COUNT * WIDTH), f32),
            shape((RANK, KEY_VALUE_HEADS * WIDTH), f32),
        ],
        compiler_params=PARAMS,
        name="adapter_out",
    )(total)


def copies_to_all(block, axes):
    size = lax.axis_size(axes)
    return lax.all_to_all(jnp.broadcast_to(block[None], (size,) + block.shape), axes, 0, 0)


def summed(pieces):
    return jnp.sum(pieces.astype(f32), axis=0).astype(bf16)


def sum_over_all(part):
    size = lax.axis_size(NEAR)
    mine = summed(lax.all_to_all(part.reshape(size, part.shape[0] // size, WIDTH), NEAR, 0, 0))
    mine = summed(copies_to_all(mine, FAR))
    return copies_to_all(mine, NEAR).reshape(part.shape)


def body(queries, keys, values, output_gradient, adapter_query_down, adapter_value_down):
    position = lax.axis_index(CTX) % GROUP_DEVS
    place = jnp.stack([position // 2, position % 2]).astype(jnp.int32)
    q, grad, aq_t = queries[0], output_gradient[0], adapter_query_down[0].T
    sel, oth = pack(position // 2, keys[0], values[0], adapter_value_down[0].T)
    one = passed_along(sel, 1)
    two = passed_along(sel, 2)
    three = passed_along(one, 2, range(1, CTX_SIZE, 2))
    other = passed_along(oth, 1, range(0, CTX_SIZE, 2))
    dq, ads, own_short, backs = attend_short(place, aq_t, sel, one, q, grad)
    dq, part, own_long, r1, r2, r3 = attend_long(
        place, aq_t, sel, oth, one, other, two, three, ads, backs, q, grad, dq
    )
    r1 = passed_along(r1, -1)
    r2 = passed_along(r2, -2)
    r3 = passed_along(r3, -3, range(1, CTX_SIZE, 2))
    dk, dv = key_sums(place, own_short, own_long, r1, r2, r3)
    total = sum_over_all(part)
    adapter_q, adapter_v = adapter_out(total)
    return dq[None], dk[None], dv[None], adapter_q, adapter_v


def solution(mesh):
    split = Mesh(mesh.devices.reshape(SIZES), AXES)
    tokens = P(DP, CTX, None)
    return jax.shard_map(
        body,
        mesh=split,
        in_specs=(tokens,) * 6,
        out_specs=(tokens, tokens, tokens, P(), P()),
        check_vma=False,
    )
```

```python
import jax
import jax.numpy as jnp
from jax import lax
from jax.experimental import pallas as pl
from jax.experimental.pallas import tpu as pltpu
from jax.sharding import Mesh, PartitionSpec as P

QUERY_HEAD_COUNT = 32
KEY_VALUE_HEADS = 4
WIDTH = 128
ROWS = 128
RANK = 16
GROUP_DEVS = 4
ADAPTER_SCALE = 2.0
SOFTMAX_SCALE = WIDTH ** (-0.5)
LOG2E = 1.4426950408889634
PER_HEAD = QUERY_HEAD_COUNT // KEY_VALUE_HEADS
HALF_HEADS = QUERY_HEAD_COUNT // 2
UNIT = 4 * ROWS
SEL_ROWS = UNIT + RANK
ADAPTER_ROWS = 768
HALF_ADAPTER_ROWS = (HALF_HEADS + 2) * RANK

AXES = ("x", "zl", "yh", "yl", "zh", "core")
SIZES = (4, 2, 4, 2, 4, 2)
CTX = ("x", "zl", "yh", "yl")
DP = ("zh", "core")
NEAR = ("x", "zl", "yl", "core")
FAR = ("yh", "zh")
CTX_SIZE = 64

NT = (((1,), (1,)), ((), ()))
NN = (((1,), (0,)), ((), ()))
bf16 = jnp.bfloat16
f32 = jnp.float32


def dot(a, b, dims):
    return lax.dot_general(a, b, dims, preferred_element_type=f32)


def group_place():
    position = lax.axis_index(CTX) % GROUP_DEVS
    return position // 2, position % 2


def head_columns(head):
    return pl.ds(pl.multiple_of(head * WIDTH, WIDTH), WIDTH)


def attend_head(q_wide, g_wide, keys, values, av_t, aq_t):
    count = len(keys)
    key_all = jnp.concatenate(keys, axis=0) if count > 1 else keys[0]
    value_all = jnp.concatenate(values, axis=0) if count > 1 else values[0]
    rows = PER_HEAD * ROWS
    allowed = lax.broadcasted_iota(jnp.int32, (ROWS, rows), 0) <= (
        lax.broadcasted_iota(jnp.int32, (ROWS, rows), 1) % ROWS
    )
    heads = [slice(h * WIDTH, (h + 1) * WIDTH) for h in range(PER_HEAD)]
    q = jnp.concatenate([q_wide[:, h] for h in heads], axis=0)
    grad = jnp.concatenate([g_wide[:, h] for h in heads], axis=0)
    scores = dot(key_all, q, NT)
    score_grad = dot(value_all, grad, NT)
    diagonal = jnp.where(allowed, scores[:ROWS], -1e30)
    scores = jnp.concatenate([diagonal, scores[ROWS:]], axis=0) if count > 1 else diagonal
    top = jnp.max(scores, axis=0, keepdims=True)
    raised = jnp.exp2((scores - top) * (SOFTMAX_SCALE * LOG2E))
    probs = raised * (1.0 / jnp.sum(raised, axis=0, keepdims=True))
    delta = jnp.sum(probs * score_grad, axis=0, keepdims=True)
    logit_grad = (probs * (score_grad - delta)).astype(bf16)
    dq_t = (dot(key_all.T, logit_grad, NN) * SOFTMAX_SCALE).astype(bf16)
    dq = jnp.concatenate([dq_t[:, h].T for h in heads], axis=1)
    dv = dot(probs.astype(bf16), grad, NN).astype(bf16)
    dk = (dot(logit_grad, q, NN) * SOFTMAX_SCALE).astype(bf16)
    av_all = jnp.concatenate(av_t, axis=1) if count > 1 else av_t[0]
    return dq, dk, dv, dot(aq_t, dq, NN).astype(bf16), dot(av_all, dv, NN).astype(bf16)


def attend_half(half, q_ref, g_ref, dq_ref, variants, aq_t, put_adapter, put_value):
    def columns(g):
        return pl.ds(pl.multiple_of(half * HALF_COLUMNS + g * HEAD_COLUMNS, WIDTH), HEAD_COLUMNS)

    def go(blocks, av_refs, outs):
        for g in range(2):
            keys = [ref[g * ROWS : (g + 1) * ROWS, :] for ref in blocks]
            values = [ref[(2 + g) * ROWS : (3 + g) * ROWS, :] for ref in blocks]
            av_t = [ref[UNIT:SEL_ROWS, :] for ref in av_refs]
            dq, dk, dv, ad_q, ad_v = attend_head(
                q_ref[:, columns(g)], g_ref[:, columns(g)], keys, values, av_t, aq_t
            )
            dq_ref[:, g * HEAD_COLUMNS : (g + 1) * HEAD_COLUMNS] = dq
            for h in range(PER_HEAD):
                put_adapter(g * PER_HEAD + h, ad_q[:, h * WIDTH : (h + 1) * WIDTH])
            put_value(g, ad_v)
            for n, (ref, base) in enumerate(outs):
                rows = slice(n * ROWS, (n + 1) * ROWS)
                ref[base + g * ROWS : base + (g + 1) * ROWS, :] = dk[rows]
                ref[base + (2 + g) * ROWS : base + (3 + g) * ROWS, :] = dv[rows]

    for condition, *rest in variants:
        pl.when(condition)(lambda rest=rest: go(*rest))


def short_kernel(aq_ref, sel_ref, one_ref, q_ref, g_ref, dq_ref, ad_ref, own_ref, back_ref):
    short, odd = group_place()

    def put_adapter(h, value):
        ad_ref[h * RANK : (h + 1) * RANK, :] = value

    def put_value(g, value):
        ad_ref[(HALF_HEADS + g) * RANK : (HALF_HEADS + g + 1) * RANK, :] = value

    variants = [
        (odd == 0, [sel_ref], [sel_ref], [(own_ref, 0)]),
        (odd == 1, [sel_ref, one_ref], [sel_ref, one_ref], [(own_ref, 0), (back_ref, 0)]),
    ]
    attend_half(short, q_ref, g_ref, dq_ref, variants, aq_ref[...], put_adapter, put_value)


def long_kernel(
    aq_ref, sel_ref, oth_ref, one_ref, other_ref, two_ref, three_ref, ads_ref, backs_ref, q_ref, g_ref,
    dq_ref, ad_ref, own_ref, r1_ref, r2_ref, r3_ref,
):
    short, odd = group_place()
    long = 1 - short
    n = HALF_HEADS * RANK

    def put_adapter(h, value):
        ad_ref[pl.ds(pl.multiple_of(long * n + h * RANK, RANK), RANK), :] = value

    def put_value(g, value):
        ad_ref[pl.ds(pl.multiple_of(2 * n + (long * 2 + g) * RANK, RANK), RANK), :] = value

    variants = [
        (
            odd == 0,
            [oth_ref, one_ref, two_ref],
            [sel_ref, one_ref, two_ref],
            [(own_ref, 0), (r1_ref, 0), (r2_ref, 0)],
        ),
        (
            odd == 1,
            [oth_ref, other_ref, two_ref, three_ref],
            [sel_ref, one_ref, two_ref, three_ref],
            [(own_ref, 0), (r1_ref, UNIT), (r2_ref, 0), (r3_ref, 0)],
        ),
    ]
    attend_half(long, q_ref, g_ref, dq_ref, variants, aq_ref[...], put_adapter, put_value)
    ad_ref[2 * n + 4 * RANK :, :] = jnp.zeros((ADAPTER_ROWS - 2 * n - 4 * RANK, WIDTH), bf16)
    ad_ref[pl.ds(pl.multiple_of(short * n, RANK), n), :] = ads_ref[:n, :]
    ad_ref[pl.ds(pl.multiple_of(2 * n + short * 2 * RANK, RANK), 2 * RANK), :] = ads_ref[n:, :]

    @pl.when(odd == 0)
    def _():
        r1_ref[UNIT:, :] = jnp.zeros((UNIT, WIDTH), bf16)

    @pl.when(odd == 1)
    def _():
        r1_ref[:UNIT, :] = backs_ref[...]


def gradients_kernel(
    dq_short_ref, dq_long_ref, short_ref, long_ref, r1_ref, r2_ref, r3_ref, dq_hbm, dk_ref, dv_ref, sems
):
    short, odd = group_place()
    even = odd == 0

    def half_out(ref, half, sem):
        columns = pl.ds(pl.multiple_of(half * HALF_COLUMNS, WIDTH), HALF_COLUMNS)
        return pltpu.make_async_copy(ref, dq_hbm.at[:, columns], sem)

    copies = [half_out(dq_short_ref, short, sems.at[0]), half_out(dq_long_ref, 1 - short, sems.at[1])]
    for copy in copies:
        copy.start()
    for part, ref in ((0, dk_ref), (1, dv_ref)):
        for h in range(2):
            base = (part * 2 + h) * ROWS
            rows = slice(base, base + ROWS)
            total = short_ref[rows, :].astype(f32) + r1_ref[rows, :].astype(f32)
            total = total + r2_ref[rows, :].astype(f32)
            total = total + jnp.where(even, r3_ref[rows, :].astype(f32), 0.0)
            ref[:, head_columns(short * 2 + h)] = total.astype(bf16)
            other = r1_ref[UNIT + base : UNIT + base + ROWS, :].astype(f32)
            total = long_ref[rows, :].astype(f32) + jnp.where(even, other, 0.0)
            ref[:, head_columns((1 - short) * 2 + h)] = total.astype(bf16)
    for copy in copies:
        copy.wait()


def adapter_kernel(sum_ref, aq_ref, av_ref):
    for h in range(QUERY_HEAD_COUNT):
        aq_ref[:, h * WIDTH : (h + 1) * WIDTH] = (
            sum_ref[h * RANK : (h + 1) * RANK, :].astype(f32) * ADAPTER_SCALE
        )
    for h in range(KEY_VALUE_HEADS):
        base = (QUERY_HEAD_COUNT + h) * RANK
        av_ref[:, h * WIDTH : (h + 1) * WIDTH] = sum_ref[base : base + RANK, :].astype(f32) * ADAPTER_SCALE


def shape(dims, kind=bf16):
    return jax.ShapeDtypeStruct(dims, kind)


def passed_along(block, distance, senders=range(CTX_SIZE)):
    return lax.ppermute(block, CTX, [(i, (i + distance) % CTX_SIZE) for i in senders])


SUM_FLOPS = 20_000_000_000
PARAMS = pltpu.CompilerParams(vmem_limit_bytes=40 * 1024 * 1024)
HEAD_COLUMNS = PER_HEAD * WIDTH
HALF_COLUMNS = 2 * HEAD_COLUMNS
VMEM = pl.BlockSpec(memory_space=pltpu.VMEM)
HBM = pl.BlockSpec(memory_space=pltpu.HBM)


def pack(short, k, v, av_t):
    half = 2 * WIDTH

    def chosen(array, first):
        return jnp.where(first, array[:, :half], array[:, half:])

    def stacked(first):
        pieces = [chosen(k, first), chosen(v, first)]
        return [piece[:, h * WIDTH : (h + 1) * WIDTH] for piece in pieces for h in range(2)]

    sel = jnp.concatenate(stacked(short == 0) + [av_t], axis=0)
    oth = jnp.concatenate(stacked(short == 1), axis=0)
    return sel, oth


def attend_short(*operands):
    return pl.pallas_call(
        short_kernel,
        in_specs=[VMEM] * 5,
        out_specs=[VMEM] * 4,
        out_shape=[
            shape((ROWS, HALF_COLUMNS)),
            shape((HALF_ADAPTER_ROWS, WIDTH)),
            shape((UNIT, WIDTH)),
            shape((UNIT, WIDTH)),
        ],
        compiler_params=PARAMS,
        cost_estimate=pl.CostEstimate(flops=700_000_000, bytes_accessed=3_000_000, transcendentals=0),
        name="short",
    )(*operands)


def attend_long(*operands):
    return pl.pallas_call(
        long_kernel,
        in_specs=[VMEM] * 11,
        out_specs=[VMEM] * 6,
        out_shape=[
            shape((ROWS, HALF_COLUMNS)),
            shape((ADAPTER_ROWS, WIDTH)),
            shape((UNIT, WIDTH)),
            shape((2 * UNIT, WIDTH)),
            shape((UNIT, WIDTH)),
            shape((UNIT, WIDTH)),
        ],
        compiler_params=PARAMS,
        cost_estimate=pl.CostEstimate(flops=1_400_000_000, bytes_accessed=4_000_000, transcendentals=0),
        name="long",
    )(*operands)


def gradients_out(*operands):
    out = shape((ROWS, KEY_VALUE_HEADS * WIDTH))
    return pl.pallas_call(
        gradients_kernel,
        in_specs=[VMEM] * 7,
        out_specs=[HBM, VMEM, VMEM],
        out_shape=[shape((ROWS, 2 * HALF_COLUMNS)), out, out],
        scratch_shapes=[pltpu.SemaphoreType.DMA((2,))],
        compiler_params=PARAMS,
        cost_estimate=pl.CostEstimate(flops=SUM_FLOPS, bytes_accessed=2_000_000, transcendentals=0),
        name="gradients_out",
    )(*operands)


def adapter_out(total):
    return pl.pallas_call(
        adapter_kernel,
        in_specs=[VMEM],
        out_specs=[VMEM, VMEM],
        out_shape=[
            shape((RANK, QUERY_HEAD_COUNT * WIDTH), f32),
            shape((RANK, KEY_VALUE_HEADS * WIDTH), f32),
        ],
        compiler_params=PARAMS,
        name="adapter_out",
    )(total)


def copies_to_all(block, axes):
    size = lax.axis_size(axes)
    return lax.all_to_all(jnp.broadcast_to(block[None], (size,) + block.shape), axes, 0, 0)


def summed(pieces):
    return jnp.sum(pieces.astype(f32), axis=0).astype(bf16)


def sum_over_all(part):
    size = lax.axis_size(NEAR)
    mine = summed(lax.all_to_all(part.reshape(size, part.shape[0] // size, WIDTH), NEAR, 0, 0))
    mine = summed(copies_to_all(mine, FAR))
    return copies_to_all(mine, NEAR).reshape(part.shape)


def body(queries, keys, values, output_gradient, adapter_query_down, adapter_value_down):
    q, grad, aq_t = queries[0], output_gradient[0], adapter_query_down[0].T
    sel, oth = pack(group_place()[0], keys[0], values[0], adapter_value_down[0].T)
    one = passed_along(sel, 1)
    later_sel, later_oth = lax.optimization_barrier((sel, oth))
    two = passed_along(later_sel, 2)
    other = passed_along(later_oth, 1, range(0, CTX_SIZE, 2))
    three = passed_along(one, 2, range(1, CTX_SIZE, 2))
    dq_short, ads, own_short, backs = attend_short(aq_t, sel, one, q, grad)
    dq_long, part, own_long, r1, r2, r3 = attend_long(
        aq_t, sel, oth, one, other, two, three, ads, backs, q, grad
    )
    r1 = passed_along(r1, -1)
    r2 = passed_along(r2, -2)
    r3 = passed_along(r3, -3, range(1, CTX_SIZE, 2))
    dq, dk, dv = gradients_out(dq_short, dq_long, own_short, own_long, r1, r2, r3)
    total = sum_over_all(part)
    adapter_q, adapter_v = adapter_out(total)
    return dq[None], dk[None], dv[None], adapter_q, adapter_v


def solution(mesh):
    split = Mesh(mesh.devices.reshape(SIZES), AXES)
    tokens = P(DP, CTX, None)
    return jax.shard_map(
        body,
        mesh=split,
        in_specs=(tokens,) * 6,
        out_specs=(tokens, tokens, tokens, P(), P()),
        check_vma=False,
    )
```

```python
import jax
import jax.numpy as jnp
from jax import lax
from jax.experimental import pallas as pl
from jax.experimental.pallas import tpu as pltpu
from jax.sharding import Mesh, PartitionSpec as P

QUERY_HEAD_COUNT = 32
KEY_VALUE_HEADS = 4
WIDTH = 128
ROWS = 128
RANK = 16
GROUP_DEVS = 4
ADAPTER_SCALE = 2.0
SOFTMAX_SCALE = WIDTH ** (-0.5)
LOG2E = 1.4426950408889634
PER_HEAD = QUERY_HEAD_COUNT // KEY_VALUE_HEADS
HALF_HEADS = QUERY_HEAD_COUNT // 2
UNIT = 4 * ROWS
SEL_ROWS = UNIT + RANK
ADAPTER_ROWS = 768
HALF_ADAPTER_ROWS = (HALF_HEADS + 2) * RANK

AXES = ("x", "zl", "yh", "yl", "zh", "core")
SIZES = (4, 2, 4, 2, 4, 2)
CTX = ("x", "zl", "yh", "yl")
DP = ("zh", "core")
NEAR = ("x", "zl", "yl", "core")
FAR = ("yh", "zh")
CTX_SIZE = 64

NT = (((1,), (1,)), ((), ()))
NN = (((1,), (0,)), ((), ()))
bf16 = jnp.bfloat16
f32 = jnp.float32


def dot(a, b, dims):
    return lax.dot_general(a, b, dims, preferred_element_type=f32)


def group_place():
    position = lax.axis_index(CTX) % GROUP_DEVS
    return position // 2, position % 2


def head_columns(head):
    return pl.ds(pl.multiple_of(head * WIDTH, WIDTH), WIDTH)


def attend_head(q_wide, g_wide, keys, values, av_t, aq_t):
    count = len(keys)
    key_all = jnp.concatenate(keys, axis=0) if count > 1 else keys[0]
    value_all = jnp.concatenate(values, axis=0) if count > 1 else values[0]
    rows = PER_HEAD * ROWS
    allowed = lax.broadcasted_iota(jnp.int32, (ROWS, rows), 0) <= (
        lax.broadcasted_iota(jnp.int32, (ROWS, rows), 1) % ROWS
    )
    heads = [slice(h * WIDTH, (h + 1) * WIDTH) for h in range(PER_HEAD)]
    q = jnp.concatenate([q_wide[:, h] for h in heads], axis=0)
    grad = jnp.concatenate([g_wide[:, h] for h in heads], axis=0)
    scores = dot(key_all, q, NT)
    score_grad = dot(value_all, grad, NT)
    diagonal = jnp.where(allowed, scores[:ROWS], -1e30)
    scores = jnp.concatenate([diagonal, scores[ROWS:]], axis=0) if count > 1 else diagonal
    top = jnp.max(scores, axis=0, keepdims=True)
    raised = jnp.exp2((scores - top) * (SOFTMAX_SCALE * LOG2E))
    probs = raised * (1.0 / jnp.sum(raised, axis=0, keepdims=True))
    delta = jnp.sum(probs * score_grad, axis=0, keepdims=True)
    logit_grad = (probs * (score_grad - delta)).astype(bf16)
    dq_t = (dot(key_all.T, logit_grad, NN) * SOFTMAX_SCALE).astype(bf16)
    dq = jnp.concatenate([dq_t[:, h].T for h in heads], axis=1)
    dv = dot(probs.astype(bf16), grad, NN).astype(bf16)
    dk = (dot(logit_grad, q, NN) * SOFTMAX_SCALE).astype(bf16)
    av_all = jnp.concatenate(av_t, axis=1) if count > 1 else av_t[0]
    return dq, dk, dv, dot(aq_t, dq, NN).astype(bf16), dot(av_all, dv, NN).astype(bf16)


def attend_half(half, q_ref, g_ref, dq_ref, variants, aq_t, put_adapter, put_value):
    def columns(g):
        return pl.ds(pl.multiple_of(half * HALF_COLUMNS + g * HEAD_COLUMNS, WIDTH), HEAD_COLUMNS)

    def go(blocks, av_refs, outs):
        for g in range(2):
            keys = [ref[g * ROWS : (g + 1) * ROWS, :] for ref in blocks]
            values = [ref[(2 + g) * ROWS : (3 + g) * ROWS, :] for ref in blocks]
            av_t = [ref[UNIT:SEL_ROWS, :] for ref in av_refs]
            dq, dk, dv, ad_q, ad_v = attend_head(
                q_ref[:, columns(g)], g_ref[:, columns(g)], keys, values, av_t, aq_t
            )
            dq_ref[:, g * HEAD_COLUMNS : (g + 1) * HEAD_COLUMNS] = dq
            for h in range(PER_HEAD):
                put_adapter(g * PER_HEAD + h, ad_q[:, h * WIDTH : (h + 1) * WIDTH])
            put_value(g, ad_v)
            for n, (ref, base) in enumerate(outs):
                rows = slice(n * ROWS, (n + 1) * ROWS)
                ref[base + g * ROWS : base + (g + 1) * ROWS, :] = dk[rows]
                ref[base + (2 + g) * ROWS : base + (3 + g) * ROWS, :] = dv[rows]

    for condition, *rest in variants:
        pl.when(condition)(lambda rest=rest: go(*rest))


def short_kernel(aq_ref, sel_ref, one_ref, _, q_ref, g_ref, dq_ref, ad_ref, own_ref, back_ref):
    short, odd = group_place()

    def put_adapter(h, value):
        ad_ref[h * RANK : (h + 1) * RANK, :] = value

    def put_value(g, value):
        ad_ref[(HALF_HEADS + g) * RANK : (HALF_HEADS + g + 1) * RANK, :] = value

    variants = [
        (odd == 0, [sel_ref], [sel_ref], [(own_ref, 0)]),
        (odd == 1, [sel_ref, one_ref], [sel_ref, one_ref], [(own_ref, 0), (back_ref, 0)]),
    ]
    attend_half(short, q_ref, g_ref, dq_ref, variants, aq_ref[...], put_adapter, put_value)


def long_kernel(
    aq_ref, sel_ref, oth_ref, one_ref, other_ref, two_ref, three_ref, ads_ref, backs_ref, q_ref, g_ref,
    dq_ref, ad_ref, own_ref, r1_ref, r2_ref, r3_ref,
):
    short, odd = group_place()
    long = 1 - short
    n = HALF_HEADS * RANK

    def put_adapter(h, value):
        ad_ref[pl.ds(pl.multiple_of(long * n + h * RANK, RANK), RANK), :] = value

    def put_value(g, value):
        ad_ref[pl.ds(pl.multiple_of(2 * n + (long * 2 + g) * RANK, RANK), RANK), :] = value

    variants = [
        (
            odd == 0,
            [oth_ref, one_ref, two_ref],
            [sel_ref, one_ref, two_ref],
            [(own_ref, 0), (r1_ref, 0), (r2_ref, 0)],
        ),
        (
            odd == 1,
            [oth_ref, other_ref, two_ref, three_ref],
            [sel_ref, one_ref, two_ref, three_ref],
            [(own_ref, 0), (r1_ref, UNIT), (r2_ref, 0), (r3_ref, 0)],
        ),
    ]
    attend_half(long, q_ref, g_ref, dq_ref, variants, aq_ref[...], put_adapter, put_value)
    ad_ref[2 * n + 4 * RANK :, :] = jnp.zeros((ADAPTER_ROWS - 2 * n - 4 * RANK, WIDTH), bf16)
    ad_ref[pl.ds(pl.multiple_of(short * n, RANK), n), :] = ads_ref[:n, :]
    ad_ref[pl.ds(pl.multiple_of(2 * n + short * 2 * RANK, RANK), 2 * RANK), :] = ads_ref[n:, :]

    @pl.when(odd == 0)
    def _():
        r1_ref[UNIT:, :] = jnp.zeros((UNIT, WIDTH), bf16)

    @pl.when(odd == 1)
    def _():
        r1_ref[:UNIT, :] = backs_ref[...]


def gradients_kernel(
    dq_short_ref, dq_long_ref, short_ref, long_ref, r1_ref, r2_ref, r3_ref, dq_hbm, dk_ref, dv_ref, sems
):
    short, odd = group_place()
    even = odd == 0

    def half_out(ref, half, sem):
        columns = pl.ds(pl.multiple_of(half * HALF_COLUMNS, WIDTH), HALF_COLUMNS)
        return pltpu.make_async_copy(ref, dq_hbm.at[:, columns], sem)

    copies = [half_out(dq_short_ref, short, sems.at[0]), half_out(dq_long_ref, 1 - short, sems.at[1])]
    for copy in copies:
        copy.start()
    for part, ref in ((0, dk_ref), (1, dv_ref)):
        for h in range(2):
            base = (part * 2 + h) * ROWS
            rows = slice(base, base + ROWS)
            total = short_ref[rows, :].astype(f32) + r1_ref[rows, :].astype(f32)
            total = total + r2_ref[rows, :].astype(f32)
            total = total + jnp.where(even, r3_ref[rows, :].astype(f32), 0.0)
            ref[:, head_columns(short * 2 + h)] = total.astype(bf16)
            other = r1_ref[UNIT + base : UNIT + base + ROWS, :].astype(f32)
            total = long_ref[rows, :].astype(f32) + jnp.where(even, other, 0.0)
            ref[:, head_columns((1 - short) * 2 + h)] = total.astype(bf16)
    for copy in copies:
        copy.wait()


def adapter_kernel(sum_ref, aq_ref, av_ref):
    for h in range(QUERY_HEAD_COUNT):
        aq_ref[:, h * WIDTH : (h + 1) * WIDTH] = (
            sum_ref[h * RANK : (h + 1) * RANK, :].astype(f32) * ADAPTER_SCALE
        )
    for h in range(KEY_VALUE_HEADS):
        base = (QUERY_HEAD_COUNT + h) * RANK
        av_ref[:, h * WIDTH : (h + 1) * WIDTH] = sum_ref[base : base + RANK, :].astype(f32) * ADAPTER_SCALE


def shape(dims, kind=bf16):
    return jax.ShapeDtypeStruct(dims, kind)


def passed_along(block, distance, senders=range(CTX_SIZE)):
    return lax.ppermute(block, CTX, [(i, (i + distance) % CTX_SIZE) for i in senders])


SUM_FLOPS = 20_000_000_000
PARAMS = pltpu.CompilerParams(vmem_limit_bytes=40 * 1024 * 1024)
HEAD_COLUMNS = PER_HEAD * WIDTH
HALF_COLUMNS = 2 * HEAD_COLUMNS
VMEM = pl.BlockSpec(memory_space=pltpu.VMEM)
HBM = pl.BlockSpec(memory_space=pltpu.HBM)


def pack(short, k, v, av_t):
    half = 2 * WIDTH

    def chosen(array, first):
        return jnp.where(first, array[:, :half], array[:, half:])

    def stacked(first):
        pieces = [chosen(k, first), chosen(v, first)]
        return [piece[:, h * WIDTH : (h + 1) * WIDTH] for piece in pieces for h in range(2)]

    sel = jnp.concatenate(stacked(short == 0) + [av_t], axis=0)
    oth = jnp.concatenate(stacked(short == 1), axis=0)
    return sel, oth


def attend_short(*operands):
    return pl.pallas_call(
        short_kernel,
        in_specs=[VMEM] * 6,
        out_specs=[VMEM] * 4,
        out_shape=[
            shape((ROWS, HALF_COLUMNS)),
            shape((HALF_ADAPTER_ROWS, WIDTH)),
            shape((UNIT, WIDTH)),
            shape((UNIT, WIDTH)),
        ],
        compiler_params=PARAMS,
        cost_estimate=pl.CostEstimate(flops=700_000_000, bytes_accessed=3_000_000, transcendentals=0),
        name="short",
    )(*operands)


def attend_long(*operands):
    return pl.pallas_call(
        long_kernel,
        in_specs=[VMEM] * 11,
        out_specs=[VMEM] * 6,
        out_shape=[
            shape((ROWS, HALF_COLUMNS)),
            shape((ADAPTER_ROWS, WIDTH)),
            shape((UNIT, WIDTH)),
            shape((2 * UNIT, WIDTH)),
            shape((UNIT, WIDTH)),
            shape((UNIT, WIDTH)),
        ],
        compiler_params=PARAMS,
        cost_estimate=pl.CostEstimate(flops=1_400_000_000, bytes_accessed=4_000_000, transcendentals=0),
        name="long",
    )(*operands)


def gradients_out(*operands):
    out = shape((ROWS, KEY_VALUE_HEADS * WIDTH))
    return pl.pallas_call(
        gradients_kernel,
        in_specs=[VMEM] * 7,
        out_specs=[HBM, VMEM, VMEM],
        out_shape=[shape((ROWS, 2 * HALF_COLUMNS)), out, out],
        scratch_shapes=[pltpu.SemaphoreType.DMA((2,))],
        compiler_params=PARAMS,
        cost_estimate=pl.CostEstimate(flops=SUM_FLOPS, bytes_accessed=2_000_000, transcendentals=0),
        name="gradients_out",
    )(*operands)


def adapter_out(total):
    return pl.pallas_call(
        adapter_kernel,
        in_specs=[VMEM],
        out_specs=[VMEM, VMEM],
        out_shape=[
            shape((RANK, QUERY_HEAD_COUNT * WIDTH), f32),
            shape((RANK, KEY_VALUE_HEADS * WIDTH), f32),
        ],
        compiler_params=PARAMS,
        name="adapter_out",
    )(total)


def copies_to_all(block, axes):
    size = lax.axis_size(axes)
    return lax.all_to_all(jnp.broadcast_to(block[None], (size,) + block.shape), axes, 0, 0)


def summed(pieces):
    return jnp.sum(pieces.astype(f32), axis=0).astype(bf16)


def sum_over_all(part):
    size = lax.axis_size(NEAR)
    mine = summed(lax.all_to_all(part.reshape(size, part.shape[0] // size, WIDTH), NEAR, 0, 0))
    mine = summed(copies_to_all(mine, FAR))
    return copies_to_all(mine, NEAR).reshape(part.shape)


def body(queries, keys, values, output_gradient, adapter_query_down, adapter_value_down):
    q, grad, aq_t = queries[0], output_gradient[0], adapter_query_down[0].T
    sel, oth = pack(group_place()[0], keys[0], values[0], adapter_value_down[0].T)
    one = passed_along(sel, 1)
    other = passed_along(oth, 1, range(0, CTX_SIZE, 2))
    two = passed_along(one, 1)
    three = passed_along(one, 2, range(1, CTX_SIZE, 2))
    dq_short, ads, own_short, backs = attend_short(aq_t, sel, one, other, q, grad)
    dq_long, part, own_long, r1, r2, r3 = attend_long(
        aq_t, sel, oth, one, other, two, three, ads, backs, q, grad
    )
    r1 = passed_along(r1, -1)
    r2 = passed_along(r2, -2)
    r3 = passed_along(r3, -3, range(1, CTX_SIZE, 2))
    dq, dk, dv = gradients_out(dq_short, dq_long, own_short, own_long, r1, r2, r3)
    total = sum_over_all(part)
    adapter_q, adapter_v = adapter_out(total)
    return dq[None], dk[None], dv[None], adapter_q, adapter_v


def solution(mesh):
    split = Mesh(mesh.devices.reshape(SIZES), AXES)
    tokens = P(DP, CTX, None)
    return jax.shard_map(
        body,
        mesh=split,
        in_specs=(tokens,) * 6,
        out_specs=(tokens, tokens, tokens, P(), P()),
        check_vma=False,
    )
```

```python
import jax
import jax.numpy as jnp
from jax import lax
from jax.experimental import pallas as pl
from jax.experimental.pallas import tpu as pltpu
from jax.sharding import Mesh, PartitionSpec as P

QUERY_HEAD_COUNT = 32
KEY_VALUE_HEADS = 4
WIDTH = 128
ROWS = 128
RANK = 16
GROUP_DEVS = 4
ADAPTER_SCALE = 2.0
SOFTMAX_SCALE = WIDTH ** (-0.5)
LOG2E = 1.4426950408889634
PER_HEAD = QUERY_HEAD_COUNT // KEY_VALUE_HEADS
HALF_HEADS = QUERY_HEAD_COUNT // 2
UNIT = 4 * ROWS
SEL_ROWS = UNIT + RANK
ADAPTER_ROWS = 768
HALF_ADAPTER_ROWS = (HALF_HEADS + 2) * RANK

AXES = ("x", "zl", "yh", "yl", "zh", "core")
SIZES = (4, 2, 4, 2, 4, 2)
CTX = ("x", "zl", "yh", "yl")
DP = ("zh", "core")
NEAR = ("x", "zl", "yl", "core")
FAR = ("yh", "zh")
CTX_SIZE = 64

NT = (((1,), (1,)), ((), ()))
NN = (((1,), (0,)), ((), ()))
bf16 = jnp.bfloat16
f32 = jnp.float32


def dot(a, b, dims):
    return lax.dot_general(a, b, dims, preferred_element_type=f32)


def group_place():
    position = lax.axis_index(CTX) % GROUP_DEVS
    return position // 2, position % 2


def head_columns(head):
    return pl.ds(pl.multiple_of(head * WIDTH, WIDTH), WIDTH)


def attend_head(q_wide, g_wide, keys, values, av_t, aq_t):
    count = len(keys)
    key_all = jnp.concatenate(keys, axis=0) if count > 1 else keys[0]
    value_all = jnp.concatenate(values, axis=0) if count > 1 else values[0]
    rows = PER_HEAD * ROWS
    allowed = lax.broadcasted_iota(jnp.int32, (ROWS, rows), 0) <= (
        lax.broadcasted_iota(jnp.int32, (ROWS, rows), 1) % ROWS
    )
    heads = [slice(h * WIDTH, (h + 1) * WIDTH) for h in range(PER_HEAD)]
    q = jnp.concatenate([q_wide[:, h] for h in heads], axis=0)
    grad = jnp.concatenate([g_wide[:, h] for h in heads], axis=0)
    scores = dot(key_all, q, NT)
    score_grad = dot(value_all, grad, NT)
    diagonal = jnp.where(allowed, scores[:ROWS], -1e30)
    scores = jnp.concatenate([diagonal, scores[ROWS:]], axis=0) if count > 1 else diagonal
    top = jnp.max(scores, axis=0, keepdims=True)
    raised = jnp.exp2((scores - top) * (SOFTMAX_SCALE * LOG2E))
    probs = raised * (1.0 / jnp.sum(raised, axis=0, keepdims=True))
    delta = jnp.sum(probs * score_grad, axis=0, keepdims=True)
    logit_grad = (probs * (score_grad - delta)).astype(bf16)
    dq_t = (dot(key_all.T, logit_grad, NN) * SOFTMAX_SCALE).astype(bf16)
    dq = jnp.concatenate([dq_t[:, h].T for h in heads], axis=1)
    dv = dot(probs.astype(bf16), grad, NN).astype(bf16)
    dk = (dot(logit_grad, q, NN) * SOFTMAX_SCALE).astype(bf16)
    av_all = jnp.concatenate(av_t, axis=1) if count > 1 else av_t[0]
    return dq, dk, dv, dot(aq_t, dq, NN).astype(bf16), dot(av_all, dv, NN).astype(bf16)


def attend_half(half, q_ref, g_ref, dq_ref, variants, aq_t, put_adapter, put_value):
    def columns(g):
        return pl.ds(pl.multiple_of(half * HALF_COLUMNS + g * HEAD_COLUMNS, WIDTH), HEAD_COLUMNS)

    def go(blocks, av_refs, outs):
        for g in range(2):
            keys = [ref[g * ROWS : (g + 1) * ROWS, :] for ref in blocks]
            values = [ref[(2 + g) * ROWS : (3 + g) * ROWS, :] for ref in blocks]
            av_t = [ref[UNIT:SEL_ROWS, :] for ref in av_refs]
            dq, dk, dv, ad_q, ad_v = attend_head(
                q_ref[:, columns(g)], g_ref[:, columns(g)], keys, values, av_t, aq_t
            )
            dq_ref[:, g * HEAD_COLUMNS : (g + 1) * HEAD_COLUMNS] = dq
            for h in range(PER_HEAD):
                put_adapter(g * PER_HEAD + h, ad_q[:, h * WIDTH : (h + 1) * WIDTH])
            put_value(g, ad_v)
            for n, (ref, base) in enumerate(outs):
                rows = slice(n * ROWS, (n + 1) * ROWS)
                ref[base + g * ROWS : base + (g + 1) * ROWS, :] = dk[rows]
                ref[base + (2 + g) * ROWS : base + (3 + g) * ROWS, :] = dv[rows]

    for condition, *rest in variants:
        pl.when(condition)(lambda rest=rest: go(*rest))


def short_kernel(aq_ref, sel_ref, one_ref, _, q_ref, g_ref, dq_ref, ad_ref, own_ref, back_ref):
    short, odd = group_place()

    def put_adapter(h, value):
        ad_ref[h * RANK : (h + 1) * RANK, :] = value

    def put_value(g, value):
        ad_ref[(HALF_HEADS + g) * RANK : (HALF_HEADS + g + 1) * RANK, :] = value

    variants = [
        (odd == 0, [sel_ref], [sel_ref], [(own_ref, 0)]),
        (odd == 1, [sel_ref, one_ref], [sel_ref, one_ref], [(own_ref, 0), (back_ref, 0)]),
    ]
    attend_half(short, q_ref, g_ref, dq_ref, variants, aq_ref[...], put_adapter, put_value)


def long_kernel(
    aq_ref, sel_ref, oth_ref, one_ref, other_ref, two_ref, three_ref, ads_ref, backs_ref, q_ref, g_ref,
    dq_ref, ad_ref, own_ref, r1_ref, r2_ref, r3_ref,
):
    short, odd = group_place()
    long = 1 - short
    n = HALF_HEADS * RANK

    def put_adapter(h, value):
        ad_ref[pl.ds(pl.multiple_of(long * n + h * RANK, RANK), RANK), :] = value

    def put_value(g, value):
        ad_ref[pl.ds(pl.multiple_of(2 * n + (long * 2 + g) * RANK, RANK), RANK), :] = value

    variants = [
        (
            odd == 0,
            [oth_ref, one_ref, two_ref],
            [sel_ref, one_ref, two_ref],
            [(own_ref, 0), (r1_ref, 0), (r2_ref, 0)],
        ),
        (
            odd == 1,
            [oth_ref, other_ref, two_ref, three_ref],
            [sel_ref, one_ref, two_ref, three_ref],
            [(own_ref, 0), (r1_ref, UNIT), (r2_ref, 0), (r3_ref, 0)],
        ),
    ]
    attend_half(long, q_ref, g_ref, dq_ref, variants, aq_ref[...], put_adapter, put_value)
    ad_ref[2 * n + 4 * RANK :, :] = jnp.zeros((ADAPTER_ROWS - 2 * n - 4 * RANK, WIDTH), bf16)
    ad_ref[pl.ds(pl.multiple_of(short * n, RANK), n), :] = ads_ref[:n, :]
    ad_ref[pl.ds(pl.multiple_of(2 * n + short * 2 * RANK, RANK), 2 * RANK), :] = ads_ref[n:, :]

    @pl.when(odd == 0)
    def _():
        r1_ref[UNIT:, :] = jnp.zeros((UNIT, WIDTH), bf16)

    @pl.when(odd == 1)
    def _():
        r1_ref[:UNIT, :] = backs_ref[...]


def gradients_kernel(
    dq_short_ref, dq_long_ref, short_ref, long_ref, r1_ref, r2_ref, r3_ref, dq_hbm, dk_ref, dv_ref, sems
):
    short, odd = group_place()
    even = odd == 0

    def half_out(ref, half, sem):
        columns = pl.ds(pl.multiple_of(half * HALF_COLUMNS, WIDTH), HALF_COLUMNS)
        return pltpu.make_async_copy(ref, dq_hbm.at[:, columns], sem)

    copies = [half_out(dq_short_ref, short, sems.at[0]), half_out(dq_long_ref, 1 - short, sems.at[1])]
    for copy in copies:
        copy.start()
    for part, ref in ((0, dk_ref), (1, dv_ref)):
        for h in range(2):
            base = (part * 2 + h) * ROWS
            rows = slice(base, base + ROWS)
            total = short_ref[rows, :].astype(f32) + r1_ref[rows, :].astype(f32)
            total = total + r2_ref[rows, :].astype(f32)
            total = total + jnp.where(even, r3_ref[rows, :].astype(f32), 0.0)
            ref[:, head_columns(short * 2 + h)] = total.astype(bf16)
            other = r1_ref[UNIT + base : UNIT + base + ROWS, :].astype(f32)
            total = long_ref[rows, :].astype(f32) + jnp.where(even, other, 0.0)
            ref[:, head_columns((1 - short) * 2 + h)] = total.astype(bf16)
    for copy in copies:
        copy.wait()


def adapter_kernel(sum_ref, aq_ref, av_ref):
    for h in range(QUERY_HEAD_COUNT):
        aq_ref[:, h * WIDTH : (h + 1) * WIDTH] = (
            sum_ref[h * RANK : (h + 1) * RANK, :].astype(f32) * ADAPTER_SCALE
        )
    for h in range(KEY_VALUE_HEADS):
        base = (QUERY_HEAD_COUNT + h) * RANK
        av_ref[:, h * WIDTH : (h + 1) * WIDTH] = sum_ref[base : base + RANK, :].astype(f32) * ADAPTER_SCALE


def shape(dims, kind=bf16):
    return jax.ShapeDtypeStruct(dims, kind)


def passed_along(block, distance, senders=range(CTX_SIZE)):
    return lax.ppermute(block, CTX, [(i, (i + distance) % CTX_SIZE) for i in senders])


SUM_FLOPS = 20_000_000_000
PARAMS = pltpu.CompilerParams(vmem_limit_bytes=40 * 1024 * 1024)
HEAD_COLUMNS = PER_HEAD * WIDTH
HALF_COLUMNS = 2 * HEAD_COLUMNS
VMEM = pl.BlockSpec(memory_space=pltpu.VMEM)
HBM = pl.BlockSpec(memory_space=pltpu.HBM)


def pack(short, k, v, av_t):
    half = 2 * WIDTH

    def chosen(array, first):
        return jnp.where(first, array[:, :half], array[:, half:])

    def stacked(first):
        pieces = [chosen(k, first), chosen(v, first)]
        return [piece[:, h * WIDTH : (h + 1) * WIDTH] for piece in pieces for h in range(2)]

    sel = jnp.concatenate(stacked(short == 0) + [av_t], axis=0)
    oth = jnp.concatenate(stacked(short == 1), axis=0)
    return sel, oth


def attend_short(*operands):
    return pl.pallas_call(
        short_kernel,
        in_specs=[VMEM] * 6,
        out_specs=[VMEM] * 4,
        out_shape=[
            shape((ROWS, HALF_COLUMNS)),
            shape((HALF_ADAPTER_ROWS, WIDTH)),
            shape((UNIT, WIDTH)),
            shape((UNIT, WIDTH)),
        ],
        compiler_params=PARAMS,
        cost_estimate=pl.CostEstimate(flops=700_000_000, bytes_accessed=3_000_000, transcendentals=0),
        name="short",
    )(*operands)


def attend_long(*operands):
    return pl.pallas_call(
        long_kernel,
        in_specs=[VMEM] * 11,
        out_specs=[VMEM] * 6,
        out_shape=[
            shape((ROWS, HALF_COLUMNS)),
            shape((ADAPTER_ROWS, WIDTH)),
            shape((UNIT, WIDTH)),
            shape((2 * UNIT, WIDTH)),
            shape((UNIT, WIDTH)),
            shape((UNIT, WIDTH)),
        ],
        compiler_params=PARAMS,
        cost_estimate=pl.CostEstimate(flops=1_400_000_000, bytes_accessed=4_000_000, transcendentals=0),
        name="long",
    )(*operands)


def gradients_out(*operands):
    out = shape((ROWS, KEY_VALUE_HEADS * WIDTH))
    return pl.pallas_call(
        gradients_kernel,
        in_specs=[VMEM] * 7,
        out_specs=[HBM, VMEM, VMEM],
        out_shape=[shape((ROWS, 2 * HALF_COLUMNS)), out, out],
        scratch_shapes=[pltpu.SemaphoreType.DMA((2,))],
        compiler_params=PARAMS,
        cost_estimate=pl.CostEstimate(flops=SUM_FLOPS, bytes_accessed=2_000_000, transcendentals=0),
        name="gradients_out",
    )(*operands)


def adapter_out(total):
    return pl.pallas_call(
        adapter_kernel,
        in_specs=[VMEM],
        out_specs=[VMEM, VMEM],
        out_shape=[
            shape((RANK, QUERY_HEAD_COUNT * WIDTH), f32),
            shape((RANK, KEY_VALUE_HEADS * WIDTH), f32),
        ],
        compiler_params=PARAMS,
        name="adapter_out",
    )(total)


def copies_to_all(block, axes):
    size = lax.axis_size(axes)
    return lax.all_to_all(jnp.broadcast_to(block[None], (size,) + block.shape), axes, 0, 0)


def summed(pieces):
    return jnp.sum(pieces.astype(f32), axis=0).astype(bf16)


def sum_over_all(part, beside):
    size = lax.axis_size(NEAR)
    mine = summed(lax.all_to_all(part.reshape(size, part.shape[0] // size, WIDTH), NEAR, 0, 0))
    mine = summed(copies_to_all(mine, FAR))
    mine, beside = lax.optimization_barrier((mine, beside))
    return copies_to_all(mine, NEAR).reshape(part.shape), beside


def body(queries, keys, values, output_gradient, adapter_query_down, adapter_value_down):
    q, grad, aq_t = queries[0], output_gradient[0], adapter_query_down[0].T
    sel, oth = pack(group_place()[0], keys[0], values[0], adapter_value_down[0].T)
    one = passed_along(sel, 1)
    other = passed_along(oth, 1, range(0, CTX_SIZE, 2))
    three = passed_along(one, 2, range(1, CTX_SIZE, 2))
    two = passed_along(one, 1)
    dq_short, ads, own_short, backs = attend_short(aq_t, sel, one, other, q, grad)
    dq_long, part, own_long, r1, r2, r3 = attend_long(
        aq_t, sel, oth, one, other, two, three, ads, backs, q, grad
    )
    r1 = passed_along(r1, -1)
    r2 = passed_along(r2, -2)
    r3 = passed_along(r3, -3, range(1, CTX_SIZE, 2))
    dq, dk, dv = gradients_out(dq_short, dq_long, own_short, own_long, r1, r2, r3)
    total, (dk, dv) = sum_over_all(part, (dk, dv))
    adapter_q, adapter_v = adapter_out(total)
    return dq[None], dk[None], dv[None], adapter_q, adapter_v


def solution(mesh):
    split = Mesh(mesh.devices.reshape(SIZES), AXES)
    tokens = P(DP, CTX, None)
    return jax.shard_map(
        body,
        mesh=split,
        in_specs=(tokens,) * 6,
        out_specs=(tokens, tokens, tokens, P(), P()),
        check_vma=False,
    )
```

```python
import jax
import jax.numpy as jnp
from jax import lax
from jax.experimental import pallas as pl
from jax.experimental.pallas import tpu as pltpu
from jax.sharding import Mesh, PartitionSpec as P

QUERY_HEAD_COUNT = 32
KEY_VALUE_HEADS = 4
WIDTH = 128
ROWS = 128
RANK = 16
GROUP_DEVS = 4
ADAPTER_SCALE = 2.0
SOFTMAX_SCALE = WIDTH ** (-0.5)
LOG2E = 1.4426950408889634
STRIP = ROWS
PER_HEAD = QUERY_HEAD_COUNT // KEY_VALUE_HEADS
HALF_HEADS = QUERY_HEAD_COUNT // 2
UNIT = 4 * ROWS
ADAPTER_ROWS = 768
HALF_ADAPTER_ROWS = (HALF_HEADS + 2) * RANK

AXES = ("x", "zl", "yh", "yl", "zh", "core")
SIZES = (4, 2, 4, 2, 4, 2)
CTX = ("x", "zl", "yh", "yl")
DP = ("zh", "core")
NEAR = ("x", "zl", "yl", "core")
FAR = ("yh", "zh")
CTX_SIZE = 64

NT = (((1,), (1,)), ((), ()))
NN = (((1,), (0,)), ((), ()))
bf16 = jnp.bfloat16
f32 = jnp.float32


def dot(a, b, dims):
    return lax.dot_general(a, b, dims, preferred_element_type=f32)


def group_place():
    position = lax.axis_index(CTX) % GROUP_DEVS
    return position // 2, position % 2


def head_columns(head):
    return pl.ds(pl.multiple_of(head * WIDTH, WIDTH), WIDTH)


def stacked(wide):
    return jnp.concatenate([wide[:, h * WIDTH : (h + 1) * WIDTH] for h in range(PER_HEAD)], axis=0)


def joined(blocks, axis):
    return jnp.concatenate(blocks, axis=axis) if len(blocks) > 1 else blocks[0]


def logits(scores, score_grad):
    columns = scores.shape[1]
    allowed = lax.broadcasted_iota(jnp.int32, (ROWS, columns), 0) <= (
        lax.broadcasted_iota(jnp.int32, (ROWS, columns), 1) % ROWS
    )
    diagonal = jnp.where(allowed, scores[:ROWS], -1e30)
    scores = joined([diagonal, scores[ROWS:]], 0) if scores.shape[0] > ROWS else diagonal
    top = jnp.max(scores, axis=0, keepdims=True)
    raised = jnp.exp2((scores - top) * (SOFTMAX_SCALE * LOG2E))
    probs = raised * (1.0 / jnp.sum(raised, axis=0, keepdims=True))
    delta = jnp.sum(probs * score_grad, axis=0, keepdims=True)
    return probs.astype(bf16), (probs * (score_grad - delta)).astype(bf16)


def attend(heads, aq_t):
    ready = []
    for q_wide, g_wide, keys, values, av_t in heads:
        q, grad, key_all = stacked(q_wide), stacked(g_wide), joined(keys, 0)
        ready.append((q, grad, key_all, dot(key_all, q, NT), dot(joined(values, 0), grad, NT), joined(av_t, 1)))
    out = []
    for q, grad, key_all, scores, score_grad, av_all in ready:
        strips = [
            logits(scores[:, c : c + STRIP], score_grad[:, c : c + STRIP])
            for c in range(0, PER_HEAD * ROWS, STRIP)
        ]
        weights, logit_grad = joined([w for w, _ in strips], 1), joined([l for _, l in strips], 1)
        dq_t = (dot(key_all.T, logit_grad, NN) * SOFTMAX_SCALE).astype(bf16)
        dq = jnp.concatenate([dq_t[:, h * ROWS : (h + 1) * ROWS].T for h in range(PER_HEAD)], axis=1)
        dv = dot(weights, grad, NN).astype(bf16)
        dk = (dot(logit_grad, q, NN) * SOFTMAX_SCALE).astype(bf16)
        out.append((dq, dk, dv, dot(aq_t, dq, NN).astype(bf16), dot(av_all, dv, NN).astype(bf16)))
    return out


def attend_half(half, q_ref, g_ref, dq_ref, variants, aq_t, put_adapter, put_value):
    def columns(g):
        return pl.ds(pl.multiple_of(half * HALF_COLUMNS + g * HEAD_COLUMNS, WIDTH), HEAD_COLUMNS)

    def go(blocks, av_refs, outs):
        heads = []
        for g in range(2):
            keys = [ref[g * ROWS : (g + 1) * ROWS, :] for ref in blocks]
            values = [ref[(2 + g) * ROWS : (3 + g) * ROWS, :] for ref in blocks]
            av_t = [ref[first : first + RANK, :] for ref, first in av_refs]
            heads.append((q_ref[:, columns(g)], g_ref[:, columns(g)], keys, values, av_t))
        for g, (dq, dk, dv, ad_q, ad_v) in enumerate(attend(heads, aq_t)):
            dq_ref[:, g * HEAD_COLUMNS : (g + 1) * HEAD_COLUMNS] = dq
            for h in range(PER_HEAD):
                put_adapter(g * PER_HEAD + h, ad_q[:, h * WIDTH : (h + 1) * WIDTH])
            put_value(g, ad_v)
            for n, (ref, base) in enumerate(outs):
                rows = slice(n * ROWS, (n + 1) * ROWS)
                ref[base + g * ROWS : base + (g + 1) * ROWS, :] = dk[rows]
                ref[base + (2 + g) * ROWS : base + (3 + g) * ROWS, :] = dv[rows]

    for condition, *rest in variants:
        pl.when(condition)(lambda rest=rest: go(*rest))


def short_kernel(aq_ref, av_ref, av1_ref, sel_ref, one_ref, _, q_ref, g_ref, dq_ref, ad_ref, own_ref, back_ref):
    short, odd = group_place()

    def put_adapter(h, value):
        ad_ref[h * RANK : (h + 1) * RANK, :] = value

    def put_value(g, value):
        ad_ref[(HALF_HEADS + g) * RANK : (HALF_HEADS + g + 1) * RANK, :] = value

    variants = [
        (odd == 0, [sel_ref], [(av_ref, 0)], [(own_ref, 0)]),
        (odd == 1, [sel_ref, one_ref], [(av_ref, 0), (av1_ref, 0)], [(own_ref, 0), (back_ref, 0)]),
    ]
    attend_half(short, q_ref, g_ref, dq_ref, variants, aq_ref[...], put_adapter, put_value)


def long_kernel(
    aq_ref, av_ref, av1_ref, far_ref, oth_ref, one_ref, other_ref, three_ref, two_ref, ads_ref, backs_ref, q_ref, g_ref,
    dq_ref, ad_ref, own_ref, r1_ref, r2_ref, r3_ref,
):
    short, odd = group_place()
    long = 1 - short
    n = HALF_HEADS * RANK

    def put_adapter(h, value):
        ad_ref[pl.ds(pl.multiple_of(long * n + h * RANK, RANK), RANK), :] = value

    def put_value(g, value):
        ad_ref[pl.ds(pl.multiple_of(2 * n + (long * 2 + g) * RANK, RANK), RANK), :] = value

    variants = [
        (
            odd == 0,
            [oth_ref, one_ref, two_ref],
            [(av_ref, 0), (av1_ref, 0), (far_ref, 0)],
            [(own_ref, 0), (r1_ref, 0), (r2_ref, 0)],
        ),
        (
            odd == 1,
            [oth_ref, other_ref, two_ref, three_ref],
            [(av_ref, 0), (av1_ref, 0), (far_ref, 0), (far_ref, RANK)],
            [(own_ref, 0), (r1_ref, UNIT), (r2_ref, 0), (r3_ref, 0)],
        ),
    ]
    attend_half(long, q_ref, g_ref, dq_ref, variants, aq_ref[...], put_adapter, put_value)
    ad_ref[2 * n + 4 * RANK :, :] = jnp.zeros((ADAPTER_ROWS - 2 * n - 4 * RANK, WIDTH), bf16)
    ad_ref[pl.ds(pl.multiple_of(short * n, RANK), n), :] = ads_ref[:n, :]
    ad_ref[pl.ds(pl.multiple_of(2 * n + short * 2 * RANK, RANK), 2 * RANK), :] = ads_ref[n:, :]

    @pl.when(odd == 0)
    def _():
        r1_ref[UNIT:, :] = jnp.zeros((UNIT, WIDTH), bf16)

    @pl.when(odd == 1)
    def _():
        r1_ref[:UNIT, :] = backs_ref[...]


def gradients_kernel(
    dq_short_ref, dq_long_ref, short_ref, long_ref, r1_ref, r2_ref, r3_ref, dq_hbm, dk_ref, dv_ref, sems
):
    short, odd = group_place()
    even = odd == 0

    def half_out(ref, half, sem):
        columns = pl.ds(pl.multiple_of(half * HALF_COLUMNS, WIDTH), HALF_COLUMNS)
        return pltpu.make_async_copy(ref, dq_hbm.at[:, columns], sem)

    copies = [half_out(dq_short_ref, short, sems.at[0]), half_out(dq_long_ref, 1 - short, sems.at[1])]
    for copy in copies:
        copy.start()
    for part, ref in ((0, dk_ref), (1, dv_ref)):
        for h in range(2):
            base = (part * 2 + h) * ROWS
            rows = slice(base, base + ROWS)
            total = short_ref[rows, :].astype(f32) + r1_ref[rows, :].astype(f32)
            total = total + r2_ref[rows, :].astype(f32)
            total = total + jnp.where(even, r3_ref[rows, :].astype(f32), 0.0)
            ref[:, head_columns(short * 2 + h)] = total.astype(bf16)
            other = r1_ref[UNIT + base : UNIT + base + ROWS, :].astype(f32)
            total = long_ref[rows, :].astype(f32) + jnp.where(even, other, 0.0)
            ref[:, head_columns((1 - short) * 2 + h)] = total.astype(bf16)
    for copy in copies:
        copy.wait()


def adapter_kernel(sum_ref, aq_ref, av_ref):
    for h in range(QUERY_HEAD_COUNT):
        aq_ref[:, h * WIDTH : (h + 1) * WIDTH] = (
            sum_ref[h * RANK : (h + 1) * RANK, :].astype(f32) * ADAPTER_SCALE
        )
    for h in range(KEY_VALUE_HEADS):
        base = (QUERY_HEAD_COUNT + h) * RANK
        av_ref[:, h * WIDTH : (h + 1) * WIDTH] = sum_ref[base : base + RANK, :].astype(f32) * ADAPTER_SCALE


def shape(dims, kind=bf16):
    return jax.ShapeDtypeStruct(dims, kind)


def passed_along(block, distance, senders=range(CTX_SIZE)):
    return lax.ppermute(block, CTX, [(i, (i + distance) % CTX_SIZE) for i in senders])


SUM_FLOPS = 20_000_000_000
PARAMS = pltpu.CompilerParams(vmem_limit_bytes=40 * 1024 * 1024)
HEAD_COLUMNS = PER_HEAD * WIDTH
HALF_COLUMNS = 2 * HEAD_COLUMNS
VMEM = pl.BlockSpec(memory_space=pltpu.VMEM)
HBM = pl.BlockSpec(memory_space=pltpu.HBM)


def pack(short, k, v):
    half = 2 * WIDTH

    def chosen(array, first):
        return jnp.where(first, array[:, :half], array[:, half:])

    def stacked_rows(first):
        pieces = [chosen(k, first), chosen(v, first)]
        return jnp.concatenate([p[:, h * WIDTH : (h + 1) * WIDTH] for p in pieces for h in range(2)], axis=0)

    return stacked_rows(short == 0), stacked_rows(short == 1)


def attend_short(*operands):
    return pl.pallas_call(
        short_kernel,
        in_specs=[VMEM] * 8,
        out_specs=[VMEM] * 4,
        out_shape=[
            shape((ROWS, HALF_COLUMNS)),
            shape((HALF_ADAPTER_ROWS, WIDTH)),
            shape((UNIT, WIDTH)),
            shape((UNIT, WIDTH)),
        ],
        compiler_params=PARAMS,
        cost_estimate=pl.CostEstimate(flops=700_000_000, bytes_accessed=3_000_000, transcendentals=0),
        name="short",
    )(*operands)


def attend_long(*operands):
    return pl.pallas_call(
        long_kernel,
        in_specs=[VMEM] * 13,
        out_specs=[VMEM] * 6,
        out_shape=[
            shape((ROWS, HALF_COLUMNS)),
            shape((ADAPTER_ROWS, WIDTH)),
            shape((UNIT, WIDTH)),
            shape((2 * UNIT, WIDTH)),
            shape((UNIT, WIDTH)),
            shape((UNIT, WIDTH)),
        ],
        compiler_params=PARAMS,
        cost_estimate=pl.CostEstimate(flops=1_400_000_000, bytes_accessed=4_000_000, transcendentals=0),
        name="long",
    )(*operands)


def gradients_out(*operands):
    out = shape((ROWS, KEY_VALUE_HEADS * WIDTH))
    return pl.pallas_call(
        gradients_kernel,
        in_specs=[VMEM] * 7,
        out_specs=[HBM, VMEM, VMEM],
        out_shape=[shape((ROWS, 2 * HALF_COLUMNS)), out, out],
        scratch_shapes=[pltpu.SemaphoreType.DMA((2,))],
        compiler_params=PARAMS,
        cost_estimate=pl.CostEstimate(flops=SUM_FLOPS, bytes_accessed=2_000_000, transcendentals=0),
        name="gradients_out",
    )(*operands)


def adapter_out(total):
    return pl.pallas_call(
        adapter_kernel,
        in_specs=[VMEM],
        out_specs=[VMEM, VMEM],
        out_shape=[
            shape((RANK, QUERY_HEAD_COUNT * WIDTH), f32),
            shape((RANK, KEY_VALUE_HEADS * WIDTH), f32),
        ],
        compiler_params=PARAMS,
        name="adapter_out",
    )(total)


def copies_to_all(block, axes):
    size = lax.axis_size(axes)
    return lax.all_to_all(jnp.broadcast_to(block[None], (size,) + block.shape), axes, 0, 0)


def summed(pieces):
    return jnp.sum(pieces.astype(f32), axis=0).astype(bf16)


def sum_over_all(part):
    size = lax.axis_size(NEAR)
    mine = summed(lax.all_to_all(part.reshape(size, part.shape[0] // size, WIDTH), NEAR, 0, 0))
    mine = summed(copies_to_all(mine, FAR))
    return copies_to_all(mine, NEAR).reshape(part.shape)


def body(queries, keys, values, output_gradient, adapter_query_down, adapter_value_down):
    q, grad, aq_t = queries[0], output_gradient[0], adapter_query_down[0].T
    av_t = adapter_value_down[0].T
    sel, oth = pack(group_place()[0], keys[0], values[0])
    one = passed_along(sel, 1)
    other = passed_along(oth, 1, range(0, CTX_SIZE, 2))
    av1 = passed_along(av_t, 1)
    near_av = jnp.concatenate([av_t, av1], axis=0)
    two = passed_along(one, 1)
    three = passed_along(one, 2, range(1, CTX_SIZE, 2))
    far = passed_along(near_av, 2)
    dq_short, ads, own_short, backs = attend_short(aq_t, av_t, av1, sel, one, other, q, grad)
    dq_long, part, own_long, r1, r2, r3 = attend_long(
        aq_t, av_t, av1, far, oth, one, other, three, two, ads, backs, q, grad
    )
    r1 = passed_along(r1, -1)
    r2 = passed_along(r2, -2)
    r3 = passed_along(r3, -3, range(1, CTX_SIZE, 2))
    dq, dk, dv = gradients_out(dq_short, dq_long, own_short, own_long, r1, r2, r3)
    total = sum_over_all(part)
    adapter_q, adapter_v = adapter_out(total)
    return dq[None], dk[None], dv[None], adapter_q, adapter_v


def solution(mesh):
    split = Mesh(mesh.devices.reshape(SIZES), AXES)
    tokens = P(DP, CTX, None)
    return jax.shard_map(
        body,
        mesh=split,
        in_specs=(tokens,) * 6,
        out_specs=(tokens, tokens, tokens, P(), P()),
        check_vma=False,
    )
```

```python
import jax
import jax.numpy as jnp
from jax import lax
from jax.experimental import pallas as pl
from jax.experimental.pallas import tpu as pltpu
from jax.sharding import Mesh, PartitionSpec as P

QUERY_HEAD_COUNT = 32
KEY_VALUE_HEADS = 4
WIDTH = 128
ROWS = 128
RANK = 16
GROUP_DEVS = 4
ADAPTER_SCALE = 2.0
SOFTMAX_SCALE = WIDTH ** (-0.5)
LOG2E = 1.4426950408889634
STRIP = ROWS
PER_HEAD = QUERY_HEAD_COUNT // KEY_VALUE_HEADS
HALF_HEADS = QUERY_HEAD_COUNT // 2
UNIT = 4 * ROWS
SEL_ROWS = UNIT + RANK
ADAPTER_ROWS = 768
HALF_ADAPTER_ROWS = (HALF_HEADS + 2) * RANK

AXES = ("x", "zl", "yh", "yl", "zh", "core")
SIZES = (4, 2, 4, 2, 4, 2)
CTX = ("x", "zl", "yh", "yl")
DP = ("zh", "core")
NEAR = ("x", "zl", "yl", "core")
FAR = ("yh", "zh")
CTX_SIZE = 64

NT = (((1,), (1,)), ((), ()))
NN = (((1,), (0,)), ((), ()))
bf16 = jnp.bfloat16
f32 = jnp.float32


def dot(a, b, dims):
    return lax.dot_general(a, b, dims, preferred_element_type=f32)


def group_place():
    position = lax.axis_index(CTX) % GROUP_DEVS
    return position // 2, position % 2


def head_columns(head):
    return pl.ds(pl.multiple_of(head * WIDTH, WIDTH), WIDTH)


def stacked(wide):
    return jnp.concatenate([wide[:, h * WIDTH : (h + 1) * WIDTH] for h in range(PER_HEAD)], axis=0)


def joined(blocks, axis):
    return jnp.concatenate(blocks, axis=axis) if len(blocks) > 1 else blocks[0]


def logits(scores, score_grad):
    columns = scores.shape[1]
    allowed = lax.broadcasted_iota(jnp.int32, (ROWS, columns), 0) <= (
        lax.broadcasted_iota(jnp.int32, (ROWS, columns), 1) % ROWS
    )
    diagonal = jnp.where(allowed, scores[:ROWS], -1e30)
    scores = joined([diagonal, scores[ROWS:]], 0) if scores.shape[0] > ROWS else diagonal
    top = jnp.max(scores, axis=0, keepdims=True)
    raised = jnp.exp2((scores - top) * (SOFTMAX_SCALE * LOG2E))
    probs = raised * (1.0 / jnp.sum(raised, axis=0, keepdims=True))
    delta = jnp.sum(probs * score_grad, axis=0, keepdims=True)
    return probs.astype(bf16), (probs * (score_grad - delta)).astype(bf16)


def attend(heads, aq_t):
    ready = []
    for q_wide, g_wide, keys, values, av_t in heads:
        q, grad, key_all = stacked(q_wide), stacked(g_wide), joined(keys, 0)
        ready.append((q, grad, key_all, dot(key_all, q, NT), dot(joined(values, 0), grad, NT), joined(av_t, 1)))
    out = []
    for q, grad, key_all, scores, score_grad, av_all in ready:
        strips = [
            logits(scores[:, c : c + STRIP], score_grad[:, c : c + STRIP])
            for c in range(0, PER_HEAD * ROWS, STRIP)
        ]
        weights, logit_grad = joined([w for w, _ in strips], 1), joined([l for _, l in strips], 1)
        dq_t = (dot(key_all.T, logit_grad, NN) * SOFTMAX_SCALE).astype(bf16)
        dq = jnp.concatenate([dq_t[:, h * ROWS : (h + 1) * ROWS].T for h in range(PER_HEAD)], axis=1)
        dv = dot(weights, grad, NN).astype(bf16)
        dk = (dot(logit_grad, q, NN) * SOFTMAX_SCALE).astype(bf16)
        out.append((dq, dk, dv, dot(aq_t, dq, NN).astype(bf16), dot(av_all, dv, NN).astype(bf16)))
    return out


def attend_half(half, q_ref, g_ref, dq_ref, variants, aq_t, put_adapter, put_value):
    def columns(g):
        return pl.ds(pl.multiple_of(half * HALF_COLUMNS + g * HEAD_COLUMNS, WIDTH), HEAD_COLUMNS)

    def go(blocks, av_refs, outs):
        heads = []
        for g in range(2):
            keys = [ref[g * ROWS : (g + 1) * ROWS, :] for ref in blocks]
            values = [ref[(2 + g) * ROWS : (3 + g) * ROWS, :] for ref in blocks]
            av_t = [ref[UNIT:SEL_ROWS, :] for ref in av_refs]
            heads.append((q_ref[:, columns(g)], g_ref[:, columns(g)], keys, values, av_t))
        for g, (dq, dk, dv, ad_q, ad_v) in enumerate(attend(heads, aq_t)):
            dq_ref[:, g * HEAD_COLUMNS : (g + 1) * HEAD_COLUMNS] = dq
            for h in range(PER_HEAD):
                put_adapter(g * PER_HEAD + h, ad_q[:, h * WIDTH : (h + 1) * WIDTH])
            put_value(g, ad_v)
            for n, (ref, base) in enumerate(outs):
                rows = slice(n * ROWS, (n + 1) * ROWS)
                ref[base + g * ROWS : base + (g + 1) * ROWS, :] = dk[rows]
                ref[base + (2 + g) * ROWS : base + (3 + g) * ROWS, :] = dv[rows]

    for condition, *rest in variants:
        pl.when(condition)(lambda rest=rest: go(*rest))


def short_kernel(aq_ref, sel_ref, one_ref, _, q_ref, g_ref, dq_ref, ad_ref, own_ref, back_ref):
    short, odd = group_place()

    def put_adapter(h, value):
        ad_ref[h * RANK : (h + 1) * RANK, :] = value

    def put_value(g, value):
        ad_ref[(HALF_HEADS + g) * RANK : (HALF_HEADS + g + 1) * RANK, :] = value

    variants = [
        (odd == 0, [sel_ref], [sel_ref], [(own_ref, 0)]),
        (odd == 1, [sel_ref, one_ref], [sel_ref, one_ref], [(own_ref, 0), (back_ref, 0)]),
    ]
    attend_half(short, q_ref, g_ref, dq_ref, variants, aq_ref[...], put_adapter, put_value)


def long_kernel(
    aq_ref, sel_ref, oth_ref, one_ref, other_ref, three_ref, two_ref, ads_ref, backs_ref, q_ref, g_ref,
    dq_ref, ad_ref, own_ref, r1_ref, r2_ref, r3_ref,
):
    short, odd = group_place()
    long = 1 - short
    n = HALF_HEADS * RANK

    def put_adapter(h, value):
        ad_ref[pl.ds(pl.multiple_of(long * n + h * RANK, RANK), RANK), :] = value

    def put_value(g, value):
        ad_ref[pl.ds(pl.multiple_of(2 * n + (long * 2 + g) * RANK, RANK), RANK), :] = value

    variants = [
        (
            odd == 0,
            [oth_ref, one_ref, two_ref],
            [sel_ref, one_ref, two_ref],
            [(own_ref, 0), (r1_ref, 0), (r2_ref, 0)],
        ),
        (
            odd == 1,
            [oth_ref, other_ref, two_ref, three_ref],
            [sel_ref, one_ref, two_ref, three_ref],
            [(own_ref, 0), (r1_ref, UNIT), (r2_ref, 0), (r3_ref, 0)],
        ),
    ]
    attend_half(long, q_ref, g_ref, dq_ref, variants, aq_ref[...], put_adapter, put_value)
    ad_ref[2 * n + 4 * RANK :, :] = jnp.zeros((ADAPTER_ROWS - 2 * n - 4 * RANK, WIDTH), bf16)
    ad_ref[pl.ds(pl.multiple_of(short * n, RANK), n), :] = ads_ref[:n, :]
    ad_ref[pl.ds(pl.multiple_of(2 * n + short * 2 * RANK, RANK), 2 * RANK), :] = ads_ref[n:, :]

    @pl.when(odd == 0)
    def _():
        r1_ref[UNIT:, :] = jnp.zeros((UNIT, WIDTH), bf16)

    @pl.when(odd == 1)
    def _():
        r1_ref[:UNIT, :] = backs_ref[...]


def gradients_kernel(
    dq_short_ref, dq_long_ref, short_ref, long_ref, r1_ref, r2_ref, r3_ref, dq_hbm, dk_ref, dv_ref, sems
):
    short, odd = group_place()
    even = odd == 0

    def half_out(ref, half, sem):
        columns = pl.ds(pl.multiple_of(half * HALF_COLUMNS, WIDTH), HALF_COLUMNS)
        return pltpu.make_async_copy(ref, dq_hbm.at[:, columns], sem)

    copies = [half_out(dq_short_ref, short, sems.at[0]), half_out(dq_long_ref, 1 - short, sems.at[1])]
    for copy in copies:
        copy.start()
    for part, ref in ((0, dk_ref), (1, dv_ref)):
        for h in range(2):
            base = (part * 2 + h) * ROWS
            rows = slice(base, base + ROWS)
            total = short_ref[rows, :].astype(f32) + r1_ref[rows, :].astype(f32)
            total = total + r2_ref[rows, :].astype(f32)
            total = total + jnp.where(even, r3_ref[rows, :].astype(f32), 0.0)
            ref[:, head_columns(short * 2 + h)] = total.astype(bf16)
            other = r1_ref[UNIT + base : UNIT + base + ROWS, :].astype(f32)
            total = long_ref[rows, :].astype(f32) + jnp.where(even, other, 0.0)
            ref[:, head_columns((1 - short) * 2 + h)] = total.astype(bf16)
    for copy in copies:
        copy.wait()


def adapter_kernel(sum_ref, aq_ref, av_ref):
    for h in range(QUERY_HEAD_COUNT):
        aq_ref[:, h * WIDTH : (h + 1) * WIDTH] = (
            sum_ref[h * RANK : (h + 1) * RANK, :].astype(f32) * ADAPTER_SCALE
        )
    for h in range(KEY_VALUE_HEADS):
        base = (QUERY_HEAD_COUNT + h) * RANK
        av_ref[:, h * WIDTH : (h + 1) * WIDTH] = sum_ref[base : base + RANK, :].astype(f32) * ADAPTER_SCALE


def shape(dims, kind=bf16):
    return jax.ShapeDtypeStruct(dims, kind)


def passed_along(block, distance, senders=range(CTX_SIZE)):
    return lax.ppermute(block, CTX, [(i, (i + distance) % CTX_SIZE) for i in senders])


SUM_FLOPS = 20_000_000_000
PARAMS = pltpu.CompilerParams(vmem_limit_bytes=40 * 1024 * 1024)
HEAD_COLUMNS = PER_HEAD * WIDTH
HALF_COLUMNS = 2 * HEAD_COLUMNS
VMEM = pl.BlockSpec(memory_space=pltpu.VMEM)
HBM = pl.BlockSpec(memory_space=pltpu.HBM)


def pack(short, k, v, av_t):
    half = 2 * WIDTH

    def chosen(array, first):
        return jnp.where(first, array[:, :half], array[:, half:])

    def stacked(first):
        pieces = [chosen(k, first), chosen(v, first)]
        return [piece[:, h * WIDTH : (h + 1) * WIDTH] for piece in pieces for h in range(2)]

    sel = jnp.concatenate(stacked(short == 0) + [av_t], axis=0)
    oth = jnp.concatenate(stacked(short == 1), axis=0)
    return sel, oth


def attend_short(*operands):
    return pl.pallas_call(
        short_kernel,
        in_specs=[VMEM] * 6,
        out_specs=[VMEM] * 4,
        out_shape=[
            shape((ROWS, HALF_COLUMNS)),
            shape((HALF_ADAPTER_ROWS, WIDTH)),
            shape((UNIT, WIDTH)),
            shape((UNIT, WIDTH)),
        ],
        compiler_params=PARAMS,
        cost_estimate=pl.CostEstimate(flops=700_000_000, bytes_accessed=3_000_000, transcendentals=0),
        name="short",
    )(*operands)


def attend_long(*operands):
    return pl.pallas_call(
        long_kernel,
        in_specs=[VMEM] * 11,
        out_specs=[VMEM] * 6,
        out_shape=[
            shape((ROWS, HALF_COLUMNS)),
            shape((ADAPTER_ROWS, WIDTH)),
            shape((UNIT, WIDTH)),
            shape((2 * UNIT, WIDTH)),
            shape((UNIT, WIDTH)),
            shape((UNIT, WIDTH)),
        ],
        compiler_params=PARAMS,
        cost_estimate=pl.CostEstimate(flops=1_400_000_000, bytes_accessed=4_000_000, transcendentals=0),
        name="long",
    )(*operands)


def gradients_out(*operands):
    out = shape((ROWS, KEY_VALUE_HEADS * WIDTH))
    return pl.pallas_call(
        gradients_kernel,
        in_specs=[VMEM] * 7,
        out_specs=[HBM, VMEM, VMEM],
        out_shape=[shape((ROWS, 2 * HALF_COLUMNS)), out, out],
        scratch_shapes=[pltpu.SemaphoreType.DMA((2,))],
        compiler_params=PARAMS,
        cost_estimate=pl.CostEstimate(flops=SUM_FLOPS, bytes_accessed=2_000_000, transcendentals=0),
        name="gradients_out",
    )(*operands)


def adapter_out(total):
    return pl.pallas_call(
        adapter_kernel,
        in_specs=[VMEM],
        out_specs=[VMEM, VMEM],
        out_shape=[
            shape((RANK, QUERY_HEAD_COUNT * WIDTH), f32),
            shape((RANK, KEY_VALUE_HEADS * WIDTH), f32),
        ],
        compiler_params=PARAMS,
        name="adapter_out",
    )(total)


def copies_to_all(block, axes):
    size = lax.axis_size(axes)
    return lax.all_to_all(jnp.broadcast_to(block[None], (size,) + block.shape), axes, 0, 0)


def summed(pieces):
    return jnp.sum(pieces.astype(f32), axis=0).astype(bf16)


def sum_over_all(part):
    size = lax.axis_size(NEAR)
    mine = summed(lax.all_to_all(part.reshape(size, part.shape[0] // size, WIDTH), NEAR, 0, 0))
    mine = summed(copies_to_all(mine, FAR))
    return copies_to_all(mine, NEAR).reshape(part.shape)


def body(queries, keys, values, output_gradient, adapter_query_down, adapter_value_down):
    q, grad, aq_t = queries[0], output_gradient[0], adapter_query_down[0].T
    sel, oth = pack(group_place()[0], keys[0], values[0], adapter_value_down[0].T)
    one = passed_along(sel, 1)
    other = passed_along(oth, 1, range(0, CTX_SIZE, 2))
    three = passed_along(one, 2, range(1, CTX_SIZE, 2))
    two = passed_along(one, 1)
    dq_short, ads, own_short, backs = attend_short(aq_t, sel, one, other, q, grad)
    dq_long, part, own_long, r1, r2, r3 = attend_long(
        aq_t, sel, oth, one, other, three, two, ads, backs, q, grad
    )
    r1 = passed_along(r1, -1)
    r2 = passed_along(r2, -2)
    r3 = passed_along(r3, -3, range(1, CTX_SIZE, 2))
    dq, dk, dv = gradients_out(dq_short, dq_long, own_short, own_long, r1, r2, r3)
    total = sum_over_all(part)
    adapter_q, adapter_v = adapter_out(total)
    return dq[None], dk[None], dv[None], adapter_q, adapter_v


def solution(mesh):
    split = Mesh(mesh.devices.reshape(SIZES), AXES)
    tokens = P(DP, CTX, None)
    return jax.shard_map(
        body,
        mesh=split,
        in_specs=(tokens,) * 6,
        out_specs=(tokens, tokens, tokens, P(), P()),
        check_vma=False,
    )
```

```python
import jax
import jax.numpy as jnp
from jax import lax
from jax.experimental import pallas as pl
from jax.experimental.pallas import tpu as pltpu
from jax.sharding import Mesh, PartitionSpec as P

QUERY_HEAD_COUNT = 32
KEY_VALUE_HEADS = 4
WIDTH = 128
ROWS = 128
RANK = 16
GROUP_DEVS = 4
ADAPTER_SCALE = 2.0
SOFTMAX_SCALE = WIDTH ** (-0.5)
LOG2E = 1.4426950408889634
STRIP = ROWS
PER_HEAD = QUERY_HEAD_COUNT // KEY_VALUE_HEADS
HALF_HEADS = QUERY_HEAD_COUNT // 2
UNIT = 4 * ROWS
SEL_ROWS = UNIT + RANK
ADAPTER_ROWS = 768
HALF_ADAPTER_ROWS = (HALF_HEADS + 2) * RANK

AXES = ("x", "zl", "yh", "yl", "zh", "core")
SIZES = (4, 2, 4, 2, 4, 2)
CTX = ("x", "zl", "yh", "yl")
DP = ("zh", "core")
NEAR = ("x", "zl", "yl", "core")
FAR = ("yh", "zh")
CTX_SIZE = 64

NT = (((1,), (1,)), ((), ()))
NN = (((1,), (0,)), ((), ()))
bf16 = jnp.bfloat16
f32 = jnp.float32


def dot(a, b, dims):
    return lax.dot_general(a, b, dims, preferred_element_type=f32)


def group_place():
    position = lax.axis_index(CTX) % GROUP_DEVS
    return position // 2, position % 2


def head_columns(head):
    return pl.ds(pl.multiple_of(head * WIDTH, WIDTH), WIDTH)


def stacked(wide):
    return jnp.concatenate([wide[:, h * WIDTH : (h + 1) * WIDTH] for h in range(PER_HEAD)], axis=0)


def joined(blocks, axis):
    return jnp.concatenate(blocks, axis=axis) if len(blocks) > 1 else blocks[0]


def logits(scores, score_grad):
    columns = scores.shape[1]
    allowed = lax.broadcasted_iota(jnp.int32, (ROWS, columns), 0) <= (
        lax.broadcasted_iota(jnp.int32, (ROWS, columns), 1) % ROWS
    )
    diagonal = jnp.where(allowed, scores[:ROWS], -1e30)
    scores = joined([diagonal, scores[ROWS:]], 0) if scores.shape[0] > ROWS else diagonal
    top = jnp.max(scores, axis=0, keepdims=True)
    raised = jnp.exp2((scores - top) * (SOFTMAX_SCALE * LOG2E))
    probs = raised * (1.0 / jnp.sum(raised, axis=0, keepdims=True))
    delta = jnp.sum(probs * score_grad, axis=0, keepdims=True)
    return probs.astype(bf16), (probs * (score_grad - delta)).astype(bf16)


def attend(heads, aq_t):
    ready = []
    for q_wide, g_wide, keys, values, av_t in heads:
        q, grad, key_all = stacked(q_wide), stacked(g_wide), joined(keys, 0)
        ready.append((q, grad, key_all, dot(key_all, q, NT), dot(joined(values, 0), grad, NT), joined(av_t, 1)))
    out = []
    for q, grad, key_all, scores, score_grad, av_all in ready:
        strips = [
            logits(scores[:, c : c + STRIP], score_grad[:, c : c + STRIP])
            for c in range(0, PER_HEAD * ROWS, STRIP)
        ]
        weights, logit_grad = joined([w for w, _ in strips], 1), joined([l for _, l in strips], 1)
        dq_t = (dot(key_all.T, logit_grad, NN) * SOFTMAX_SCALE).astype(bf16)
        dq = jnp.concatenate([dq_t[:, h * ROWS : (h + 1) * ROWS].T for h in range(PER_HEAD)], axis=1)
        dv = dot(weights, grad, NN).astype(bf16)
        dk = (dot(logit_grad, q, NN) * SOFTMAX_SCALE).astype(bf16)
        out.append((dq, dk, dv, dot(aq_t, dq, NN).astype(bf16), dot(av_all, dv, NN).astype(bf16)))
    return out


def attend_half(half, q_ref, g_ref, dq_ref, variants, aq_t, put_adapter, put_value):
    def columns(g):
        return pl.ds(pl.multiple_of(half * HALF_COLUMNS + g * HEAD_COLUMNS, WIDTH), HEAD_COLUMNS)

    def go(blocks, av_refs, outs):
        heads = []
        for g in range(2):
            keys = [ref[g * ROWS : (g + 1) * ROWS, :] for ref in blocks]
            values = [ref[(2 + g) * ROWS : (3 + g) * ROWS, :] for ref in blocks]
            av_t = [ref[UNIT:SEL_ROWS, :] for ref in av_refs]
            heads.append((q_ref[:, columns(g)], g_ref[:, columns(g)], keys, values, av_t))
        for g, (dq, dk, dv, ad_q, ad_v) in enumerate(attend(heads, aq_t)):
            dq_ref[:, g * HEAD_COLUMNS : (g + 1) * HEAD_COLUMNS] = dq
            for h in range(PER_HEAD):
                put_adapter(g * PER_HEAD + h, ad_q[:, h * WIDTH : (h + 1) * WIDTH])
            put_value(g, ad_v)
            for n, (ref, base) in enumerate(outs):
                rows = slice(n * ROWS, (n + 1) * ROWS)
                ref[base + g * ROWS : base + (g + 1) * ROWS, :] = dk[rows]
                ref[base + (2 + g) * ROWS : base + (3 + g) * ROWS, :] = dv[rows]

    for condition, *rest in variants:
        pl.when(condition)(lambda rest=rest: go(*rest))


def short_kernel(aq_ref, sel_ref, one_ref, _, q_ref, g_ref, dq_ref, ad_ref, own_ref, back_ref):
    short, odd = group_place()

    def put_adapter(h, value):
        ad_ref[h * RANK : (h + 1) * RANK, :] = value

    def put_value(g, value):
        ad_ref[(HALF_HEADS + g) * RANK : (HALF_HEADS + g + 1) * RANK, :] = value

    variants = [
        (odd == 0, [sel_ref], [sel_ref], [(own_ref, 0)]),
        (odd == 1, [sel_ref, one_ref], [sel_ref, one_ref], [(own_ref, 0), (back_ref, 0)]),
    ]
    attend_half(short, q_ref, g_ref, dq_ref, variants, aq_ref[...], put_adapter, put_value)


def long_kernel(
    aq_ref, sel_ref, oth_ref, one_ref, other_ref, three_ref, two_ref, ads_ref, backs_ref, q_ref, g_ref,
    dq_ref, ad_ref, own_ref, r1_ref, r2_ref,
):
    short, odd = group_place()
    long = 1 - short
    n = HALF_HEADS * RANK

    def put_adapter(h, value):
        ad_ref[pl.ds(pl.multiple_of(long * n + h * RANK, RANK), RANK), :] = value

    def put_value(g, value):
        ad_ref[pl.ds(pl.multiple_of(2 * n + (long * 2 + g) * RANK, RANK), RANK), :] = value

    variants = [
        (
            odd == 0,
            [oth_ref, one_ref, two_ref],
            [sel_ref, one_ref, two_ref],
            [(own_ref, 0), (r1_ref, 0), (r2_ref, 0)],
        ),
        (
            odd == 1,
            [oth_ref, other_ref, two_ref, three_ref],
            [sel_ref, one_ref, two_ref, three_ref],
            [(own_ref, 0), (r1_ref, UNIT), (r2_ref, 0), (r2_ref, UNIT)],
        ),
    ]
    attend_half(long, q_ref, g_ref, dq_ref, variants, aq_ref[...], put_adapter, put_value)
    ad_ref[2 * n + 4 * RANK :, :] = jnp.zeros((ADAPTER_ROWS - 2 * n - 4 * RANK, WIDTH), bf16)
    ad_ref[pl.ds(pl.multiple_of(short * n, RANK), n), :] = ads_ref[:n, :]
    ad_ref[pl.ds(pl.multiple_of(2 * n + short * 2 * RANK, RANK), 2 * RANK), :] = ads_ref[n:, :]

    @pl.when(odd == 0)
    def _():
        r1_ref[UNIT:, :] = jnp.zeros((UNIT, WIDTH), bf16)

    @pl.when(odd == 1)
    def _():
        r1_ref[:UNIT, :] = backs_ref[...]


def gradients_kernel(
    dq_short_ref, dq_long_ref, short_ref, long_ref, r1_ref, r2_ref, r3_ref, dq_hbm, dk_ref, dv_ref, sems
):
    short, odd = group_place()
    even = odd == 0

    def half_out(ref, half, sem):
        columns = pl.ds(pl.multiple_of(half * HALF_COLUMNS, WIDTH), HALF_COLUMNS)
        return pltpu.make_async_copy(ref, dq_hbm.at[:, columns], sem)

    copies = [half_out(dq_short_ref, short, sems.at[0]), half_out(dq_long_ref, 1 - short, sems.at[1])]
    for copy in copies:
        copy.start()
    for part, ref in ((0, dk_ref), (1, dv_ref)):
        for h in range(2):
            base = (part * 2 + h) * ROWS
            rows = slice(base, base + ROWS)
            total = short_ref[rows, :].astype(f32) + r1_ref[rows, :].astype(f32)
            total = total + r2_ref[rows, :].astype(f32)
            total = total + jnp.where(even, r3_ref[rows, :].astype(f32), 0.0)
            ref[:, head_columns(short * 2 + h)] = total.astype(bf16)
            other = r1_ref[UNIT + base : UNIT + base + ROWS, :].astype(f32)
            total = long_ref[rows, :].astype(f32) + jnp.where(even, other, 0.0)
            ref[:, head_columns((1 - short) * 2 + h)] = total.astype(bf16)
    for copy in copies:
        copy.wait()


def adapter_kernel(sum_ref, aq_ref, av_ref):
    for h in range(QUERY_HEAD_COUNT):
        aq_ref[:, h * WIDTH : (h + 1) * WIDTH] = (
            sum_ref[h * RANK : (h + 1) * RANK, :].astype(f32) * ADAPTER_SCALE
        )
    for h in range(KEY_VALUE_HEADS):
        base = (QUERY_HEAD_COUNT + h) * RANK
        av_ref[:, h * WIDTH : (h + 1) * WIDTH] = sum_ref[base : base + RANK, :].astype(f32) * ADAPTER_SCALE


def shape(dims, kind=bf16):
    return jax.ShapeDtypeStruct(dims, kind)


def passed_along(block, distance, senders=range(CTX_SIZE)):
    return lax.ppermute(block, CTX, [(i, (i + distance) % CTX_SIZE) for i in senders])


SUM_FLOPS = 20_000_000_000
PARAMS = pltpu.CompilerParams(vmem_limit_bytes=40 * 1024 * 1024)
HEAD_COLUMNS = PER_HEAD * WIDTH
HALF_COLUMNS = 2 * HEAD_COLUMNS
VMEM = pl.BlockSpec(memory_space=pltpu.VMEM)
HBM = pl.BlockSpec(memory_space=pltpu.HBM)


def pack(short, k, v, av_t):
    half = 2 * WIDTH

    def chosen(array, first):
        return jnp.where(first, array[:, :half], array[:, half:])

    def stacked(first):
        pieces = [chosen(k, first), chosen(v, first)]
        return [piece[:, h * WIDTH : (h + 1) * WIDTH] for piece in pieces for h in range(2)]

    sel = jnp.concatenate(stacked(short == 0) + [av_t], axis=0)
    oth = jnp.concatenate(stacked(short == 1), axis=0)
    return sel, oth


def attend_short(*operands):
    return pl.pallas_call(
        short_kernel,
        in_specs=[VMEM] * 6,
        out_specs=[VMEM] * 4,
        out_shape=[
            shape((ROWS, HALF_COLUMNS)),
            shape((HALF_ADAPTER_ROWS, WIDTH)),
            shape((UNIT, WIDTH)),
            shape((UNIT, WIDTH)),
        ],
        compiler_params=PARAMS,
        cost_estimate=pl.CostEstimate(flops=700_000_000, bytes_accessed=3_000_000, transcendentals=0),
        name="short",
    )(*operands)


def attend_long(*operands):
    return pl.pallas_call(
        long_kernel,
        in_specs=[VMEM] * 11,
        out_specs=[VMEM] * 5,
        out_shape=[
            shape((ROWS, HALF_COLUMNS)),
            shape((ADAPTER_ROWS, WIDTH)),
            shape((UNIT, WIDTH)),
            shape((2 * UNIT, WIDTH)),
            shape((2 * UNIT, WIDTH)),
        ],
        compiler_params=PARAMS,
        cost_estimate=pl.CostEstimate(flops=1_400_000_000, bytes_accessed=4_000_000, transcendentals=0),
        name="long",
    )(*operands)


def gradients_out(*operands):
    out = shape((ROWS, KEY_VALUE_HEADS * WIDTH))
    return pl.pallas_call(
        gradients_kernel,
        in_specs=[VMEM] * 7,
        out_specs=[HBM, VMEM, VMEM],
        out_shape=[shape((ROWS, 2 * HALF_COLUMNS)), out, out],
        scratch_shapes=[pltpu.SemaphoreType.DMA((2,))],
        compiler_params=PARAMS,
        cost_estimate=pl.CostEstimate(flops=SUM_FLOPS, bytes_accessed=2_000_000, transcendentals=0),
        name="gradients_out",
    )(*operands)


def adapter_out(total):
    return pl.pallas_call(
        adapter_kernel,
        in_specs=[VMEM],
        out_specs=[VMEM, VMEM],
        out_shape=[
            shape((RANK, QUERY_HEAD_COUNT * WIDTH), f32),
            shape((RANK, KEY_VALUE_HEADS * WIDTH), f32),
        ],
        compiler_params=PARAMS,
        name="adapter_out",
    )(total)


def copies_to_all(block, axes):
    size = lax.axis_size(axes)
    return lax.all_to_all(jnp.broadcast_to(block[None], (size,) + block.shape), axes, 0, 0)


def summed(pieces):
    return jnp.sum(pieces.astype(f32), axis=0).astype(bf16)


def sum_over_all(part):
    size = lax.axis_size(NEAR)
    mine = summed(lax.all_to_all(part.reshape(size, part.shape[0] // size, WIDTH), NEAR, 0, 0))
    mine = summed(copies_to_all(mine, FAR))
    return copies_to_all(mine, NEAR).reshape(part.shape)


def body(queries, keys, values, output_gradient, adapter_query_down, adapter_value_down):
    q, grad, aq_t = queries[0], output_gradient[0], adapter_query_down[0].T
    sel, oth = pack(group_place()[0], keys[0], values[0], adapter_value_down[0].T)
    one = passed_along(sel, 1)
    other = passed_along(oth, 1, range(0, CTX_SIZE, 2))
    three = passed_along(one, 2, range(1, CTX_SIZE, 2))
    two = passed_along(one, 1)
    dq_short, ads, own_short, backs = attend_short(aq_t, sel, one, other, q, grad)
    dq_long, part, own_long, r1, r2 = attend_long(
        aq_t, sel, oth, one, other, three, two, ads, backs, q, grad
    )
    r1 = passed_along(r1, -1)
    r2 = passed_along(r2, -2)
    r3 = passed_along(r2[UNIT:], -1, range(1, CTX_SIZE, 2))
    dq, dk, dv = gradients_out(dq_short, dq_long, own_short, own_long, r1, r2, r3)
    total = sum_over_all(part)
    adapter_q, adapter_v = adapter_out(total)
    return dq[None], dk[None], dv[None], adapter_q, adapter_v


def solution(mesh):
    split = Mesh(mesh.devices.reshape(SIZES), AXES)
    tokens = P(DP, CTX, None)
    return jax.shard_map(
        body,
        mesh=split,
        in_specs=(tokens,) * 6,
        out_specs=(tokens, tokens, tokens, P(), P()),
        check_vma=False,
    )
```

```python
import jax
import jax.numpy as jnp
from jax import lax
from jax.experimental import pallas as pl
from jax.experimental.pallas import tpu as pltpu
from jax.sharding import Mesh, PartitionSpec as P

QUERY_HEAD_COUNT = 32
KEY_VALUE_HEADS = 4
WIDTH = 128
ROWS = 128
RANK = 16
GROUP_DEVS = 4
ADAPTER_SCALE = 2.0
SOFTMAX_SCALE = WIDTH ** (-0.5)
LOG2E = 1.4426950408889634
STRIP = ROWS
PER_HEAD = QUERY_HEAD_COUNT // KEY_VALUE_HEADS
HALF_HEADS = QUERY_HEAD_COUNT // 2
UNIT = 4 * ROWS
SEL_ROWS = UNIT + RANK
ADAPTER_ROWS = 768
HALF_ADAPTER_ROWS = (HALF_HEADS + 2) * RANK

AXES = ("x", "zl", "yh", "yl", "zh", "core")
SIZES = (4, 2, 4, 2, 4, 2)
CTX = ("x", "zl", "yh", "yl")
DP = ("zh", "core")
NEAR = ("x", "zl", "yl", "core")
FAR = ("yh", "zh")
CTX_SIZE = 64

NT = (((1,), (1,)), ((), ()))
NN = (((1,), (0,)), ((), ()))
bf16 = jnp.bfloat16
f32 = jnp.float32


def dot(a, b, dims):
    return lax.dot_general(a, b, dims, preferred_element_type=f32)


def group_place():
    position = lax.axis_index(CTX) % GROUP_DEVS
    return position // 2, position % 2


def head_columns(head):
    return pl.ds(pl.multiple_of(head * WIDTH, WIDTH), WIDTH)


def stacked(wide):
    return jnp.concatenate([wide[:, h * WIDTH : (h + 1) * WIDTH] for h in range(PER_HEAD)], axis=0)


def joined(blocks, axis):
    return jnp.concatenate(blocks, axis=axis) if len(blocks) > 1 else blocks[0]


def logits(scores, score_grad):
    columns = scores.shape[1]
    allowed = lax.broadcasted_iota(jnp.int32, (ROWS, columns), 0) <= (
        lax.broadcasted_iota(jnp.int32, (ROWS, columns), 1) % ROWS
    )
    diagonal = jnp.where(allowed, scores[:ROWS], -1e30)
    scores = joined([diagonal, scores[ROWS:]], 0) if scores.shape[0] > ROWS else diagonal
    top = jnp.max(scores, axis=0, keepdims=True)
    raised = jnp.exp2((scores - top) * (SOFTMAX_SCALE * LOG2E))
    probs = raised * (1.0 / jnp.sum(raised, axis=0, keepdims=True))
    delta = jnp.sum(probs * score_grad, axis=0, keepdims=True)
    return probs.astype(bf16), (probs * (score_grad - delta)).astype(bf16)


def attend(heads, aq_t):
    ready = []
    for q_wide, g_wide, keys, values, av_t in heads:
        q, grad, key_all = stacked(q_wide), stacked(g_wide), joined(keys, 0)
        ready.append((q, grad, key_all, dot(key_all, q, NT), dot(joined(values, 0), grad, NT), joined(av_t, 1)))
    out = []
    for q, grad, key_all, scores, score_grad, av_all in ready:
        strips = [
            logits(scores[:, c : c + STRIP], score_grad[:, c : c + STRIP])
            for c in range(0, PER_HEAD * ROWS, STRIP)
        ]
        weights, logit_grad = joined([w for w, _ in strips], 1), joined([l for _, l in strips], 1)
        dq_t = (dot(key_all.T, logit_grad, NN) * SOFTMAX_SCALE).astype(bf16)
        dq = jnp.concatenate([dq_t[:, h * ROWS : (h + 1) * ROWS].T for h in range(PER_HEAD)], axis=1)
        dv = dot(weights, grad, NN).astype(bf16)
        dk = (dot(logit_grad, q, NN) * SOFTMAX_SCALE).astype(bf16)
        out.append((dq, dk, dv, dot(aq_t, dq, NN).astype(bf16), dot(av_all, dv, NN).astype(bf16)))
    return out


def attend_half(half, q_ref, g_ref, dq_ref, variants, aq_t, put_adapter, put_value):
    def columns(g):
        return pl.ds(pl.multiple_of(half * HALF_COLUMNS + g * HEAD_COLUMNS, WIDTH), HEAD_COLUMNS)

    def go(blocks, av_refs, outs):
        heads = []
        for g in range(2):
            keys = [ref[g * ROWS : (g + 1) * ROWS, :] for ref in blocks]
            values = [ref[(2 + g) * ROWS : (3 + g) * ROWS, :] for ref in blocks]
            av_t = [ref[UNIT:SEL_ROWS, :] for ref in av_refs]
            heads.append((q_ref[:, columns(g)], g_ref[:, columns(g)], keys, values, av_t))
        for g, (dq, dk, dv, ad_q, ad_v) in enumerate(attend(heads, aq_t)):
            dq_ref[:, g * HEAD_COLUMNS : (g + 1) * HEAD_COLUMNS] = dq
            for h in range(PER_HEAD):
                put_adapter(g * PER_HEAD + h, ad_q[:, h * WIDTH : (h + 1) * WIDTH])
            put_value(g, ad_v)
            for n, (ref, base) in enumerate(outs):
                rows = slice(n * ROWS, (n + 1) * ROWS)
                ref[base + g * ROWS : base + (g + 1) * ROWS, :] = dk[rows]
                ref[base + (2 + g) * ROWS : base + (3 + g) * ROWS, :] = dv[rows]

    for condition, *rest in variants:
        pl.when(condition)(lambda rest=rest: go(*rest))


def short_kernel(aq_ref, sel_ref, one_ref, _, q_ref, g_ref, dq_ref, ad_ref, own_ref, back_ref):
    short, odd = group_place()

    def put_adapter(h, value):
        ad_ref[h * RANK : (h + 1) * RANK, :] = value

    def put_value(g, value):
        ad_ref[(HALF_HEADS + g) * RANK : (HALF_HEADS + g + 1) * RANK, :] = value

    variants = [
        (odd == 0, [sel_ref], [sel_ref], [(own_ref, 0)]),
        (odd == 1, [sel_ref, one_ref], [sel_ref, one_ref], [(own_ref, 0), (back_ref, 0)]),
    ]
    attend_half(short, q_ref, g_ref, dq_ref, variants, aq_ref[...], put_adapter, put_value)


def long_kernel(
    aq_ref, sel_ref, oth_ref, one_ref, other_ref, three_ref, two_ref, ads_ref, backs_ref, q_ref, g_ref,
    dq_ref, ad_ref, own_ref, r1_ref, r2_ref, r3_ref,
):
    short, odd = group_place()
    long = 1 - short
    n = HALF_HEADS * RANK

    def put_adapter(h, value):
        ad_ref[pl.ds(pl.multiple_of(long * n + h * RANK, RANK), RANK), :] = value

    def put_value(g, value):
        ad_ref[pl.ds(pl.multiple_of(2 * n + (long * 2 + g) * RANK, RANK), RANK), :] = value

    variants = [
        (
            odd == 0,
            [oth_ref, one_ref, two_ref],
            [sel_ref, one_ref, two_ref],
            [(own_ref, 0), (r1_ref, 0), (r2_ref, 0)],
        ),
        (
            odd == 1,
            [oth_ref, other_ref, two_ref, three_ref],
            [sel_ref, one_ref, two_ref, three_ref],
            [(own_ref, 0), (r1_ref, UNIT), (r2_ref, 0), (r3_ref, 0)],
        ),
    ]
    attend_half(long, q_ref, g_ref, dq_ref, variants, aq_ref[...], put_adapter, put_value)
    ad_ref[2 * n + 4 * RANK :, :] = jnp.zeros((ADAPTER_ROWS - 2 * n - 4 * RANK, WIDTH), bf16)
    ad_ref[pl.ds(pl.multiple_of(short * n, RANK), n), :] = ads_ref[:n, :]
    ad_ref[pl.ds(pl.multiple_of(2 * n + short * 2 * RANK, RANK), 2 * RANK), :] = ads_ref[n:, :]

    @pl.when(odd == 0)
    def _():
        r1_ref[UNIT:, :] = jnp.zeros((UNIT, WIDTH), bf16)

    @pl.when(odd == 1)
    def _():
        r1_ref[:UNIT, :] = backs_ref[...]


def add_kernel(own_ref, r2_ref, out_ref):
    out_ref[...] = own_ref[...].astype(f32) + r2_ref[...].astype(f32)


def gradients_kernel(
    dq_short_ref, dq_long_ref, short_ref, long_ref, r1_ref, r3_ref, dq_hbm, dk_ref, dv_ref, sems
):
    short, odd = group_place()
    even = odd == 0

    def half_out(ref, half, sem):
        columns = pl.ds(pl.multiple_of(half * HALF_COLUMNS, WIDTH), HALF_COLUMNS)
        return pltpu.make_async_copy(ref, dq_hbm.at[:, columns], sem)

    copies = [half_out(dq_short_ref, short, sems.at[0]), half_out(dq_long_ref, 1 - short, sems.at[1])]
    for copy in copies:
        copy.start()
    for part, ref in ((0, dk_ref), (1, dv_ref)):
        for h in range(2):
            base = (part * 2 + h) * ROWS
            rows = slice(base, base + ROWS)
            total = short_ref[rows, :] + r1_ref[rows, :].astype(f32)
            total = total + jnp.where(even, r3_ref[rows, :].astype(f32), 0.0)
            ref[:, head_columns(short * 2 + h)] = total.astype(bf16)
            other = r1_ref[UNIT + base : UNIT + base + ROWS, :].astype(f32)
            total = long_ref[rows, :].astype(f32) + jnp.where(even, other, 0.0)
            ref[:, head_columns((1 - short) * 2 + h)] = total.astype(bf16)
    for copy in copies:
        copy.wait()


def adapter_kernel(sum_ref, aq_ref, av_ref):
    for h in range(QUERY_HEAD_COUNT):
        aq_ref[:, h * WIDTH : (h + 1) * WIDTH] = (
            sum_ref[h * RANK : (h + 1) * RANK, :].astype(f32) * ADAPTER_SCALE
        )
    for h in range(KEY_VALUE_HEADS):
        base = (QUERY_HEAD_COUNT + h) * RANK
        av_ref[:, h * WIDTH : (h + 1) * WIDTH] = sum_ref[base : base + RANK, :].astype(f32) * ADAPTER_SCALE


def shape(dims, kind=bf16):
    return jax.ShapeDtypeStruct(dims, kind)


def passed_along(block, distance, senders=range(CTX_SIZE)):
    return lax.ppermute(block, CTX, [(i, (i + distance) % CTX_SIZE) for i in senders])


SUM_FLOPS = 20_000_000_000
PARAMS = pltpu.CompilerParams(vmem_limit_bytes=40 * 1024 * 1024)
HEAD_COLUMNS = PER_HEAD * WIDTH
HALF_COLUMNS = 2 * HEAD_COLUMNS
VMEM = pl.BlockSpec(memory_space=pltpu.VMEM)
HBM = pl.BlockSpec(memory_space=pltpu.HBM)


def pack(short, k, v, av_t):
    half = 2 * WIDTH

    def chosen(array, first):
        return jnp.where(first, array[:, :half], array[:, half:])

    def stacked(first):
        pieces = [chosen(k, first), chosen(v, first)]
        return [piece[:, h * WIDTH : (h + 1) * WIDTH] for piece in pieces for h in range(2)]

    sel = jnp.concatenate(stacked(short == 0) + [av_t], axis=0)
    oth = jnp.concatenate(stacked(short == 1), axis=0)
    return sel, oth


def attend_short(*operands):
    return pl.pallas_call(
        short_kernel,
        in_specs=[VMEM] * 6,
        out_specs=[VMEM] * 4,
        out_shape=[
            shape((ROWS, HALF_COLUMNS)),
            shape((HALF_ADAPTER_ROWS, WIDTH)),
            shape((UNIT, WIDTH)),
            shape((UNIT, WIDTH)),
        ],
        compiler_params=PARAMS,
        cost_estimate=pl.CostEstimate(flops=700_000_000, bytes_accessed=3_000_000, transcendentals=0),
        name="short",
    )(*operands)


def attend_long(*operands):
    return pl.pallas_call(
        long_kernel,
        in_specs=[VMEM] * 11,
        out_specs=[VMEM] * 6,
        out_shape=[
            shape((ROWS, HALF_COLUMNS)),
            shape((ADAPTER_ROWS, WIDTH)),
            shape((UNIT, WIDTH)),
            shape((2 * UNIT, WIDTH)),
            shape((UNIT, WIDTH)),
            shape((UNIT, WIDTH)),
        ],
        compiler_params=PARAMS,
        cost_estimate=pl.CostEstimate(flops=1_400_000_000, bytes_accessed=4_000_000, transcendentals=0),
        name="long",
    )(*operands)


def add_second(*operands):
    return pl.pallas_call(
        add_kernel,
        in_specs=[VMEM] * 2,
        out_specs=VMEM,
        out_shape=shape((UNIT, WIDTH), f32),
        compiler_params=PARAMS,
        cost_estimate=pl.CostEstimate(flops=SUM_FLOPS, bytes_accessed=500_000, transcendentals=0),
        name="add_second",
    )(*operands)


def gradients_out(*operands):
    out = shape((ROWS, KEY_VALUE_HEADS * WIDTH))
    return pl.pallas_call(
        gradients_kernel,
        in_specs=[VMEM] * 6,
        out_specs=[HBM, VMEM, VMEM],
        out_shape=[shape((ROWS, 2 * HALF_COLUMNS)), out, out],
        scratch_shapes=[pltpu.SemaphoreType.DMA((2,))],
        compiler_params=PARAMS,
        cost_estimate=pl.CostEstimate(flops=SUM_FLOPS, bytes_accessed=2_000_000, transcendentals=0),
        name="gradients_out",
    )(*operands)


def adapter_out(total):
    return pl.pallas_call(
        adapter_kernel,
        in_specs=[VMEM],
        out_specs=[VMEM, VMEM],
        out_shape=[
            shape((RANK, QUERY_HEAD_COUNT * WIDTH), f32),
            shape((RANK, KEY_VALUE_HEADS * WIDTH), f32),
        ],
        compiler_params=PARAMS,
        name="adapter_out",
    )(total)


def copies_to_all(block, axes):
    size = lax.axis_size(axes)
    return lax.all_to_all(jnp.broadcast_to(block[None], (size,) + block.shape), axes, 0, 0)


def summed(pieces):
    return jnp.sum(pieces.astype(f32), axis=0).astype(bf16)


def sum_near(part):
    size = lax.axis_size(NEAR)
    return summed(lax.all_to_all(part.reshape(size, part.shape[0] // size, WIDTH), NEAR, 0, 0))


def sum_far(mine):
    return summed(copies_to_all(mine, FAR))


def body(queries, keys, values, output_gradient, adapter_query_down, adapter_value_down):
    q, grad, aq_t = queries[0], output_gradient[0], adapter_query_down[0].T
    sel, oth = pack(group_place()[0], keys[0], values[0], adapter_value_down[0].T)
    one = passed_along(sel, 1)
    other = passed_along(oth, 1, range(0, CTX_SIZE, 2))
    three = passed_along(one, 2, range(1, CTX_SIZE, 2))
    two = passed_along(one, 1)
    dq_short, ads, own_short, backs = attend_short(aq_t, sel, one, other, q, grad)
    dq_long, part, own_long, r1, r2, r3 = attend_long(
        aq_t, sel, oth, one, other, three, two, ads, backs, q, grad
    )
    r1 = passed_along(r1, -1)
    r2 = passed_along(r2, -2)
    mine, r3 = lax.optimization_barrier((sum_near(part), r3))
    r3 = passed_along(r3, -3, range(1, CTX_SIZE, 2))
    mine, sums_short = lax.optimization_barrier((sum_far(mine), add_second(own_short, r2)))
    total = copies_to_all(mine, NEAR).reshape(part.shape)
    dq, dk, dv = gradients_out(dq_short, dq_long, sums_short, own_long, r1, r3)
    adapter_q, adapter_v = adapter_out(total)
    return dq[None], dk[None], dv[None], adapter_q, adapter_v


def solution(mesh):
    split = Mesh(mesh.devices.reshape(SIZES), AXES)
    tokens = P(DP, CTX, None)
    return jax.shard_map(
        body,
        mesh=split,
        in_specs=(tokens,) * 6,
        out_specs=(tokens, tokens, tokens, P(), P()),
        check_vma=False,
    )
```

```python
import jax
import jax.numpy as jnp
from jax import lax
from jax.experimental import pallas as pl
from jax.experimental.pallas import tpu as pltpu
from jax.sharding import Mesh, PartitionSpec as P

QUERY_HEAD_COUNT = 32
KEY_VALUE_HEADS = 4
WIDTH = 128
ROWS = 128
RANK = 16
GROUP_DEVS = 4
ADAPTER_SCALE = 2.0
SOFTMAX_SCALE = WIDTH ** (-0.5)
LOG2E = 1.4426950408889634
STRIP = ROWS
PER_HEAD = QUERY_HEAD_COUNT // KEY_VALUE_HEADS
HALF_HEADS = QUERY_HEAD_COUNT // 2
UNIT = 4 * ROWS
SEL_ROWS = UNIT + RANK
ADAPTER_ROWS = 768
HALF_ADAPTER_ROWS = (HALF_HEADS + 2) * RANK

AXES = ("x", "zl", "yh", "yl", "zh", "core")
SIZES = (4, 2, 4, 2, 4, 2)
CTX = ("x", "zl", "yh", "yl")
DP = ("zh", "core")
NEAR = ("x", "zl", "yl", "core")
FAR = ("yh", "zh")
CTX_SIZE = 64

NT = (((1,), (1,)), ((), ()))
NN = (((1,), (0,)), ((), ()))
bf16 = jnp.bfloat16
f32 = jnp.float32


def dot(a, b, dims):
    return lax.dot_general(a, b, dims, preferred_element_type=f32)


def group_place():
    position = lax.axis_index(CTX) % GROUP_DEVS
    return position // 2, position % 2


def head_columns(head):
    return pl.ds(pl.multiple_of(head * WIDTH, WIDTH), WIDTH)


def stacked(wide):
    return jnp.concatenate([wide[:, h * WIDTH : (h + 1) * WIDTH] for h in range(PER_HEAD)], axis=0)


def joined(blocks, axis):
    return jnp.concatenate(blocks, axis=axis) if len(blocks) > 1 else blocks[0]


def logits(scores, score_grad):
    columns = scores.shape[1]
    allowed = lax.broadcasted_iota(jnp.int32, (ROWS, columns), 0) <= (
        lax.broadcasted_iota(jnp.int32, (ROWS, columns), 1) % ROWS
    )
    diagonal = jnp.where(allowed, scores[:ROWS], -1e30)
    scores = joined([diagonal, scores[ROWS:]], 0) if scores.shape[0] > ROWS else diagonal
    top = jnp.max(scores, axis=0, keepdims=True)
    raised = jnp.exp2((scores - top) * (SOFTMAX_SCALE * LOG2E))
    probs = raised * (1.0 / jnp.sum(raised, axis=0, keepdims=True))
    delta = jnp.sum(probs * score_grad, axis=0, keepdims=True)
    return probs.astype(bf16), (probs * (score_grad - delta)).astype(bf16)


def attend(heads, aq_t):
    ready = []
    for q_wide, g_wide, keys, values, av_t in heads:
        q, grad, key_all = stacked(q_wide), stacked(g_wide), joined(keys, 0)
        ready.append((q, grad, key_all, dot(key_all, q, NT), dot(joined(values, 0), grad, NT), joined(av_t, 1)))
    out = []
    for q, grad, key_all, scores, score_grad, av_all in ready:
        strips = [
            logits(scores[:, c : c + STRIP], score_grad[:, c : c + STRIP])
            for c in range(0, PER_HEAD * ROWS, STRIP)
        ]
        weights, logit_grad = joined([w for w, _ in strips], 1), joined([l for _, l in strips], 1)
        dq_t = (dot(key_all.T, logit_grad, NN) * SOFTMAX_SCALE).astype(bf16)
        dq = jnp.concatenate([dq_t[:, h * ROWS : (h + 1) * ROWS].T for h in range(PER_HEAD)], axis=1)
        dv = dot(weights, grad, NN).astype(bf16)
        dk = (dot(logit_grad, q, NN) * SOFTMAX_SCALE).astype(bf16)
        out.append((dq, dk, dv, dot(aq_t, dq, NN).astype(bf16), dot(av_all, dv, NN).astype(bf16)))
    return out


def attend_half(half, q_ref, g_ref, dq_ref, variants, aq_t, put_adapter, put_value):
    def columns(g):
        return pl.ds(pl.multiple_of(half * HALF_COLUMNS + g * HEAD_COLUMNS, WIDTH), HEAD_COLUMNS)

    def go(blocks, av_refs, outs):
        heads = []
        for g in range(2):
            keys = [ref[g * ROWS : (g + 1) * ROWS, :] for ref in blocks]
            values = [ref[(2 + g) * ROWS : (3 + g) * ROWS, :] for ref in blocks]
            av_t = [ref[UNIT:SEL_ROWS, :] for ref in av_refs]
            heads.append((q_ref[:, columns(g)], g_ref[:, columns(g)], keys, values, av_t))
        for g, (dq, dk, dv, ad_q, ad_v) in enumerate(attend(heads, aq_t)):
            dq_ref[:, g * HEAD_COLUMNS : (g + 1) * HEAD_COLUMNS] = dq
            for h in range(PER_HEAD):
                put_adapter(g * PER_HEAD + h, ad_q[:, h * WIDTH : (h + 1) * WIDTH])
            put_value(g, ad_v)
            for n, (ref, base) in enumerate(outs):
                rows = slice(n * ROWS, (n + 1) * ROWS)
                ref[base + g * ROWS : base + (g + 1) * ROWS, :] = dk[rows]
                ref[base + (2 + g) * ROWS : base + (3 + g) * ROWS, :] = dv[rows]

    for condition, *rest in variants:
        pl.when(condition)(lambda rest=rest: go(*rest))


def short_kernel(aq_ref, sel_ref, one_ref, _, q_ref, g_ref, dq_ref, ad_ref, own_ref, back_ref):
    short, odd = group_place()

    def put_adapter(h, value):
        ad_ref[h * RANK : (h + 1) * RANK, :] = value

    def put_value(g, value):
        ad_ref[(HALF_HEADS + g) * RANK : (HALF_HEADS + g + 1) * RANK, :] = value

    variants = [
        (odd == 0, [sel_ref], [sel_ref], [(own_ref, 0)]),
        (odd == 1, [sel_ref, one_ref], [sel_ref, one_ref], [(own_ref, 0), (back_ref, 0)]),
    ]
    attend_half(short, q_ref, g_ref, dq_ref, variants, aq_ref[...], put_adapter, put_value)


def long_kernel(
    aq_ref, sel_ref, oth_ref, one_ref, other_ref, three_ref, two_ref, ads_ref, backs_ref, q_ref, g_ref,
    dq_ref, ad_ref, own_ref, r1_ref, r2_ref, r3_ref,
):
    short, odd = group_place()
    long = 1 - short
    n = HALF_HEADS * RANK

    def put_adapter(h, value):
        ad_ref[pl.ds(pl.multiple_of(long * n + h * RANK, RANK), RANK), :] = value

    def put_value(g, value):
        ad_ref[pl.ds(pl.multiple_of(2 * n + (long * 2 + g) * RANK, RANK), RANK), :] = value

    variants = [
        (
            odd == 0,
            [oth_ref, one_ref, two_ref],
            [sel_ref, one_ref, two_ref],
            [(own_ref, 0), (r1_ref, 0), (r2_ref, 0)],
        ),
        (
            odd == 1,
            [oth_ref, other_ref, two_ref, three_ref],
            [sel_ref, one_ref, two_ref, three_ref],
            [(own_ref, 0), (r1_ref, UNIT), (r2_ref, 0), (r3_ref, 0)],
        ),
    ]
    attend_half(long, q_ref, g_ref, dq_ref, variants, aq_ref[...], put_adapter, put_value)
    ad_ref[2 * n + 4 * RANK :, :] = jnp.zeros((ADAPTER_ROWS - 2 * n - 4 * RANK, WIDTH), bf16)
    ad_ref[pl.ds(pl.multiple_of(short * n, RANK), n), :] = ads_ref[:n, :]
    ad_ref[pl.ds(pl.multiple_of(2 * n + short * 2 * RANK, RANK), 2 * RANK), :] = ads_ref[n:, :]

    @pl.when(odd == 0)
    def _():
        r1_ref[UNIT:, :] = jnp.zeros((UNIT, WIDTH), bf16)

    @pl.when(odd == 1)
    def _():
        r1_ref[:UNIT, :] = backs_ref[...]


def gradients_kernel(
    dq_short_ref, dq_long_ref, short_ref, long_ref, r1_ref, r2_ref, r3_ref, dq_hbm, dk_ref, dv_ref, sems
):
    short, odd = group_place()
    even = odd == 0

    def half_out(ref, half, sem):
        columns = pl.ds(pl.multiple_of(half * HALF_COLUMNS, WIDTH), HALF_COLUMNS)
        return pltpu.make_async_copy(ref, dq_hbm.at[:, columns], sem)

    copies = [half_out(dq_short_ref, short, sems.at[0]), half_out(dq_long_ref, 1 - short, sems.at[1])]
    for copy in copies:
        copy.start()
    for part, ref in ((0, dk_ref), (1, dv_ref)):
        for h in range(2):
            base = (part * 2 + h) * ROWS
            rows = slice(base, base + ROWS)
            total = short_ref[rows, :].astype(f32) + r1_ref[rows, :].astype(f32)
            total = total + r2_ref[rows, :].astype(f32)
            total = total + jnp.where(even, r3_ref[rows, :].astype(f32), 0.0)
            ref[:, head_columns(short * 2 + h)] = total.astype(bf16)
            other = r1_ref[UNIT + base : UNIT + base + ROWS, :].astype(f32)
            total = long_ref[rows, :].astype(f32) + jnp.where(even, other, 0.0)
            ref[:, head_columns((1 - short) * 2 + h)] = total.astype(bf16)
    for copy in copies:
        copy.wait()


def adapter_kernel(sum_ref, aq_ref, av_ref):
    for h in range(QUERY_HEAD_COUNT):
        aq_ref[:, h * WIDTH : (h + 1) * WIDTH] = (
            sum_ref[h * RANK : (h + 1) * RANK, :].astype(f32) * ADAPTER_SCALE
        )
    for h in range(KEY_VALUE_HEADS):
        base = (QUERY_HEAD_COUNT + h) * RANK
        av_ref[:, h * WIDTH : (h + 1) * WIDTH] = sum_ref[base : base + RANK, :].astype(f32) * ADAPTER_SCALE


def shape(dims, kind=bf16):
    return jax.ShapeDtypeStruct(dims, kind)


def passed_along(block, distance, senders=range(CTX_SIZE)):
    return lax.ppermute(block, CTX, [(i, (i + distance) % CTX_SIZE) for i in senders])


SUM_FLOPS = 20_000_000_000
PARAMS = pltpu.CompilerParams(vmem_limit_bytes=40 * 1024 * 1024)
HEAD_COLUMNS = PER_HEAD * WIDTH
HALF_COLUMNS = 2 * HEAD_COLUMNS
VMEM = pl.BlockSpec(memory_space=pltpu.VMEM)
HBM = pl.BlockSpec(memory_space=pltpu.HBM)


def pack(short, k, v, av_t):
    half = 2 * WIDTH

    def chosen(array, first):
        return jnp.where(first, array[:, :half], array[:, half:])

    def stacked(first):
        pieces = [chosen(k, first), chosen(v, first)]
        return [piece[:, h * WIDTH : (h + 1) * WIDTH] for piece in pieces for h in range(2)]

    sel = jnp.concatenate(stacked(short == 0) + [av_t], axis=0)
    oth = jnp.concatenate(stacked(short == 1), axis=0)
    return sel, oth


def attend_short(*operands):
    return pl.pallas_call(
        short_kernel,
        in_specs=[VMEM] * 6,
        out_specs=[VMEM] * 4,
        out_shape=[
            shape((ROWS, HALF_COLUMNS)),
            shape((HALF_ADAPTER_ROWS, WIDTH)),
            shape((UNIT, WIDTH)),
            shape((UNIT, WIDTH)),
        ],
        compiler_params=PARAMS,
        cost_estimate=pl.CostEstimate(flops=700_000_000, bytes_accessed=3_000_000, transcendentals=0),
        name="short",
    )(*operands)


def attend_long(*operands):
    return pl.pallas_call(
        long_kernel,
        in_specs=[VMEM] * 11,
        out_specs=[VMEM] * 6,
        out_shape=[
            shape((ROWS, HALF_COLUMNS)),
            shape((ADAPTER_ROWS, WIDTH)),
            shape((UNIT, WIDTH)),
            shape((2 * UNIT, WIDTH)),
            shape((UNIT, WIDTH)),
            shape((UNIT, WIDTH)),
        ],
        compiler_params=PARAMS,
        cost_estimate=pl.CostEstimate(flops=1_400_000_000, bytes_accessed=4_000_000, transcendentals=0),
        name="long",
    )(*operands)


def gradients_out(*operands):
    out = shape((ROWS, KEY_VALUE_HEADS * WIDTH))
    return pl.pallas_call(
        gradients_kernel,
        in_specs=[VMEM] * 7,
        out_specs=[HBM, VMEM, VMEM],
        out_shape=[shape((ROWS, 2 * HALF_COLUMNS)), out, out],
        scratch_shapes=[pltpu.SemaphoreType.DMA((2,))],
        compiler_params=PARAMS,
        cost_estimate=pl.CostEstimate(flops=SUM_FLOPS, bytes_accessed=2_000_000, transcendentals=0),
        name="gradients_out",
    )(*operands)


def adapter_out(total):
    return pl.pallas_call(
        adapter_kernel,
        in_specs=[VMEM],
        out_specs=[VMEM, VMEM],
        out_shape=[
            shape((RANK, QUERY_HEAD_COUNT * WIDTH), f32),
            shape((RANK, KEY_VALUE_HEADS * WIDTH), f32),
        ],
        compiler_params=PARAMS,
        name="adapter_out",
    )(total)


def copies_to_all(block, axes):
    size = lax.axis_size(axes)
    return lax.all_to_all(jnp.broadcast_to(block[None], (size,) + block.shape), axes, 0, 0)


def summed(pieces):
    return jnp.sum(pieces.astype(f32), axis=0).astype(bf16)


def sum_over_all(part):
    size = lax.axis_size(NEAR)
    mine = summed(lax.all_to_all(part.reshape(size, part.shape[0] // size, WIDTH), NEAR, 0, 0))
    mine = summed(copies_to_all(mine, FAR))
    return copies_to_all(mine, NEAR).reshape(part.shape)


def body(queries, keys, values, output_gradient, adapter_query_down, adapter_value_down):
    q, grad, aq_t = queries[0], output_gradient[0], adapter_query_down[0].T
    sel, oth = pack(group_place()[0], keys[0], values[0], adapter_value_down[0].T)
    one = passed_along(sel, 1)
    other = passed_along(oth, 1, range(0, CTX_SIZE, 2))
    later, _ = lax.optimization_barrier((sel, oth))
    two = passed_along(later, 2)
    three = passed_along(one, 2, range(1, CTX_SIZE, 2))
    dq_short, ads, own_short, backs = attend_short(aq_t, sel, one, other, q, grad)
    dq_long, part, own_long, r1, r2, r3 = attend_long(
        aq_t, sel, oth, one, other, three, two, ads, backs, q, grad
    )
    r1 = passed_along(r1, -1)
    r2 = passed_along(r2, -2)
    r3 = passed_along(r3, -3, range(1, CTX_SIZE, 2))
    dq, dk, dv = gradients_out(dq_short, dq_long, own_short, own_long, r1, r2, r3)
    total = sum_over_all(part)
    adapter_q, adapter_v = adapter_out(total)
    return dq[None], dk[None], dv[None], adapter_q, adapter_v


def solution(mesh):
    split = Mesh(mesh.devices.reshape(SIZES), AXES)
    tokens = P(DP, CTX, None)
    return jax.shard_map(
        body,
        mesh=split,
        in_specs=(tokens,) * 6,
        out_specs=(tokens, tokens, tokens, P(), P()),
        check_vma=False,
    )
```

```python
import jax
import jax.numpy as jnp
from jax import lax
from jax.experimental import pallas as pl
from jax.experimental.pallas import tpu as pltpu
from jax.sharding import Mesh, PartitionSpec as P

QUERY_HEAD_COUNT = 32
KEY_VALUE_HEADS = 4
WIDTH = 128
ROWS = 128
RANK = 16
GROUP_DEVS = 4
ADAPTER_SCALE = 2.0
SOFTMAX_SCALE = WIDTH ** (-0.5)
LOG2E = 1.4426950408889634
STRIP = ROWS
PER_HEAD = QUERY_HEAD_COUNT // KEY_VALUE_HEADS
HALF_HEADS = QUERY_HEAD_COUNT // 2
UNIT = 4 * ROWS
SEL_ROWS = UNIT + RANK
ADAPTER_ROWS = 768
HALF_ADAPTER_ROWS = (HALF_HEADS + 2) * RANK

AXES = ("x", "zl", "yh", "yl", "zh", "core")
SIZES = (4, 2, 4, 2, 4, 2)
CTX = ("x", "zl", "yh", "yl")
DP = ("zh", "core")
NEAR = ("x", "zl", "yl", "core")
FAR = ("yh", "zh")
CTX_SIZE = 64

NT = (((1,), (1,)), ((), ()))
NN = (((1,), (0,)), ((), ()))
bf16 = jnp.bfloat16
f32 = jnp.float32


def dot(a, b, dims):
    return lax.dot_general(a, b, dims, preferred_element_type=f32)


def group_place():
    position = lax.axis_index(CTX) % GROUP_DEVS
    return position // 2, position % 2


def head_columns(head):
    return pl.ds(pl.multiple_of(head * WIDTH, WIDTH), WIDTH)


def stacked(wide):
    return jnp.concatenate([wide[:, h * WIDTH : (h + 1) * WIDTH] for h in range(PER_HEAD)], axis=0)


def joined(blocks, axis):
    return jnp.concatenate(blocks, axis=axis) if len(blocks) > 1 else blocks[0]


def logits(scores, score_grad):
    columns = scores.shape[1]
    allowed = lax.broadcasted_iota(jnp.int32, (ROWS, columns), 0) <= (
        lax.broadcasted_iota(jnp.int32, (ROWS, columns), 1) % ROWS
    )
    diagonal = jnp.where(allowed, scores[:ROWS], -1e30)
    scores = joined([diagonal, scores[ROWS:]], 0) if scores.shape[0] > ROWS else diagonal
    top = jnp.max(scores, axis=0, keepdims=True)
    raised = jnp.exp2((scores - top) * (SOFTMAX_SCALE * LOG2E))
    probs = raised * (1.0 / jnp.sum(raised, axis=0, keepdims=True))
    delta = jnp.sum(probs * score_grad, axis=0, keepdims=True)
    return probs.astype(bf16), (probs * (score_grad - delta)).astype(bf16)


def attend(heads, aq_t):
    ready = []
    for q_wide, g_wide, keys, values, av_t in heads:
        q, grad, key_all = stacked(q_wide), stacked(g_wide), joined(keys, 0)
        ready.append((q, grad, key_all, dot(key_all, q, NT), dot(joined(values, 0), grad, NT), joined(av_t, 1)))
    out = []
    for q, grad, key_all, scores, score_grad, av_all in ready:
        strips = [
            logits(scores[:, c : c + STRIP], score_grad[:, c : c + STRIP])
            for c in range(0, PER_HEAD * ROWS, STRIP)
        ]
        weights, logit_grad = joined([w for w, _ in strips], 1), joined([l for _, l in strips], 1)
        dq_t = (dot(key_all.T, logit_grad, NN) * SOFTMAX_SCALE).astype(bf16)
        dq = jnp.concatenate([dq_t[:, h * ROWS : (h + 1) * ROWS].T for h in range(PER_HEAD)], axis=1)
        dv = dot(weights, grad, NN).astype(bf16)
        dk = (dot(logit_grad, q, NN) * SOFTMAX_SCALE).astype(bf16)
        out.append((dq, dk, dv, dot(aq_t, dq, NN).astype(bf16), dot(av_all, dv, NN).astype(bf16)))
    return out


def attend_half(half, q_ref, g_ref, dq_ref, variants, aq_t, put_adapter, put_value):
    def columns(g):
        return pl.ds(pl.multiple_of(half * HALF_COLUMNS + g * HEAD_COLUMNS, WIDTH), HEAD_COLUMNS)

    def go(blocks, av_refs, outs):
        heads = []
        for g in range(2):
            keys = [ref[g * ROWS : (g + 1) * ROWS, :] for ref in blocks]
            values = [ref[(2 + g) * ROWS : (3 + g) * ROWS, :] for ref in blocks]
            av_t = [ref[UNIT:SEL_ROWS, :] for ref in av_refs]
            heads.append((q_ref[:, columns(g)], g_ref[:, columns(g)], keys, values, av_t))
        for g, (dq, dk, dv, ad_q, ad_v) in enumerate(attend(heads, aq_t)):
            dq_ref[:, g * HEAD_COLUMNS : (g + 1) * HEAD_COLUMNS] = dq
            for h in range(PER_HEAD):
                put_adapter(g * PER_HEAD + h, ad_q[:, h * WIDTH : (h + 1) * WIDTH])
            put_value(g, ad_v)
            for n, (ref, base) in enumerate(outs):
                rows = slice(n * ROWS, (n + 1) * ROWS)
                ref[base + g * ROWS : base + (g + 1) * ROWS, :] = dk[rows]
                ref[base + (2 + g) * ROWS : base + (3 + g) * ROWS, :] = dv[rows]

    for condition, *rest in variants:
        pl.when(condition)(lambda rest=rest: go(*rest))


def short_kernel(aq_ref, sel_ref, one_ref, q_ref, g_ref, dq_ref, ad_ref, own_ref, back_ref):
    short, odd = group_place()

    def put_adapter(h, value):
        ad_ref[h * RANK : (h + 1) * RANK, :] = value

    def put_value(g, value):
        ad_ref[(HALF_HEADS + g) * RANK : (HALF_HEADS + g + 1) * RANK, :] = value

    variants = [
        (odd == 0, [sel_ref], [sel_ref], [(own_ref, 0)]),
        (odd == 1, [sel_ref, one_ref], [sel_ref, one_ref], [(own_ref, 0), (back_ref, 0)]),
    ]
    attend_half(short, q_ref, g_ref, dq_ref, variants, aq_ref[...], put_adapter, put_value)


def long_kernel(
    aq_ref, sel_ref, oth_ref, one_ref, other_ref, three_ref, two_ref, ads_ref, backs_ref, q_ref, g_ref,
    dq_ref, ad_ref, own_ref, r1_ref, r2_ref, r3_ref,
):
    short, odd = group_place()
    long = 1 - short
    n = HALF_HEADS * RANK

    def put_adapter(h, value):
        ad_ref[pl.ds(pl.multiple_of(long * n + h * RANK, RANK), RANK), :] = value

    def put_value(g, value):
        ad_ref[pl.ds(pl.multiple_of(2 * n + (long * 2 + g) * RANK, RANK), RANK), :] = value

    variants = [
        (
            odd == 0,
            [oth_ref, one_ref, two_ref],
            [sel_ref, one_ref, two_ref],
            [(own_ref, 0), (r1_ref, 0), (r2_ref, 0)],
        ),
        (
            odd == 1,
            [oth_ref, other_ref, two_ref, three_ref],
            [sel_ref, one_ref, two_ref, three_ref],
            [(own_ref, 0), (r1_ref, UNIT), (r2_ref, 0), (r3_ref, 0)],
        ),
    ]
    attend_half(long, q_ref, g_ref, dq_ref, variants, aq_ref[...], put_adapter, put_value)
    ad_ref[2 * n + 4 * RANK :, :] = jnp.zeros((ADAPTER_ROWS - 2 * n - 4 * RANK, WIDTH), bf16)
    ad_ref[pl.ds(pl.multiple_of(short * n, RANK), n), :] = ads_ref[:n, :]
    ad_ref[pl.ds(pl.multiple_of(2 * n + short * 2 * RANK, RANK), 2 * RANK), :] = ads_ref[n:, :]

    @pl.when(odd == 0)
    def _():
        r1_ref[UNIT:, :] = jnp.zeros((UNIT, WIDTH), bf16)

    @pl.when(odd == 1)
    def _():
        r1_ref[:UNIT, :] = backs_ref[...]


def gradients_kernel(
    dq_short_ref, dq_long_ref, short_ref, long_ref, r1_ref, r2_ref, r3_ref, dq_hbm, dk_ref, dv_ref, sems
):
    short, odd = group_place()
    even = odd == 0

    def half_out(ref, half, sem):
        columns = pl.ds(pl.multiple_of(half * HALF_COLUMNS, WIDTH), HALF_COLUMNS)
        return pltpu.make_async_copy(ref, dq_hbm.at[:, columns], sem)

    copies = [half_out(dq_short_ref, short, sems.at[0]), half_out(dq_long_ref, 1 - short, sems.at[1])]
    for copy in copies:
        copy.start()
    for part, ref in ((0, dk_ref), (1, dv_ref)):
        for h in range(2):
            base = (part * 2 + h) * ROWS
            rows = slice(base, base + ROWS)
            total = short_ref[rows, :].astype(f32) + r1_ref[rows, :].astype(f32)
            total = total + r2_ref[rows, :].astype(f32)
            total = total + jnp.where(even, r3_ref[rows, :].astype(f32), 0.0)
            ref[:, head_columns(short * 2 + h)] = total.astype(bf16)
            other = r1_ref[UNIT + base : UNIT + base + ROWS, :].astype(f32)
            total = long_ref[rows, :].astype(f32) + jnp.where(even, other, 0.0)
            ref[:, head_columns((1 - short) * 2 + h)] = total.astype(bf16)
    for copy in copies:
        copy.wait()


def adapter_kernel(sum_ref, aq_ref, av_ref):
    for h in range(QUERY_HEAD_COUNT):
        aq_ref[:, h * WIDTH : (h + 1) * WIDTH] = (
            sum_ref[h * RANK : (h + 1) * RANK, :].astype(f32) * ADAPTER_SCALE
        )
    for h in range(KEY_VALUE_HEADS):
        base = (QUERY_HEAD_COUNT + h) * RANK
        av_ref[:, h * WIDTH : (h + 1) * WIDTH] = sum_ref[base : base + RANK, :].astype(f32) * ADAPTER_SCALE


def shape(dims, kind=bf16):
    return jax.ShapeDtypeStruct(dims, kind)


def passed_along(block, distance, senders=range(CTX_SIZE)):
    return lax.ppermute(block, CTX, [(i, (i + distance) % CTX_SIZE) for i in senders])


SUM_FLOPS = 20_000_000_000
PARAMS = pltpu.CompilerParams(vmem_limit_bytes=40 * 1024 * 1024)
HEAD_COLUMNS = PER_HEAD * WIDTH
HALF_COLUMNS = 2 * HEAD_COLUMNS
VMEM = pl.BlockSpec(memory_space=pltpu.VMEM)
HBM = pl.BlockSpec(memory_space=pltpu.HBM)


def pack(short, k, v, av_t):
    half = 2 * WIDTH

    def chosen(array, first):
        return jnp.where(first, array[:, :half], array[:, half:])

    def stacked(first):
        pieces = [chosen(k, first), chosen(v, first)]
        return [piece[:, h * WIDTH : (h + 1) * WIDTH] for piece in pieces for h in range(2)]

    sel = jnp.concatenate(stacked(short == 0) + [av_t], axis=0)
    oth = jnp.concatenate(stacked(short == 1) + [av_t, av_t], axis=0)
    return sel, oth


def attend_short(*operands):
    return pl.pallas_call(
        short_kernel,
        in_specs=[VMEM] * 5,
        out_specs=[VMEM] * 4,
        out_shape=[
            shape((ROWS, HALF_COLUMNS)),
            shape((HALF_ADAPTER_ROWS, WIDTH)),
            shape((UNIT, WIDTH)),
            shape((UNIT, WIDTH)),
        ],
        compiler_params=PARAMS,
        cost_estimate=pl.CostEstimate(flops=700_000_000, bytes_accessed=3_000_000, transcendentals=0),
        name="short",
    )(*operands)


def attend_long(*operands):
    return pl.pallas_call(
        long_kernel,
        in_specs=[VMEM] * 11,
        out_specs=[VMEM] * 6,
        out_shape=[
            shape((ROWS, HALF_COLUMNS)),
            shape((ADAPTER_ROWS, WIDTH)),
            shape((UNIT, WIDTH)),
            shape((2 * UNIT, WIDTH)),
            shape((UNIT, WIDTH)),
            shape((UNIT, WIDTH)),
        ],
        compiler_params=PARAMS,
        cost_estimate=pl.CostEstimate(flops=1_400_000_000, bytes_accessed=4_000_000, transcendentals=0),
        name="long",
    )(*operands)


def gradients_out(*operands):
    out = shape((ROWS, KEY_VALUE_HEADS * WIDTH))
    return pl.pallas_call(
        gradients_kernel,
        in_specs=[VMEM] * 7,
        out_specs=[HBM, VMEM, VMEM],
        out_shape=[shape((ROWS, 2 * HALF_COLUMNS)), out, out],
        scratch_shapes=[pltpu.SemaphoreType.DMA((2,))],
        compiler_params=PARAMS,
        cost_estimate=pl.CostEstimate(flops=SUM_FLOPS, bytes_accessed=2_000_000, transcendentals=0),
        name="gradients_out",
    )(*operands)


def adapter_out(total):
    return pl.pallas_call(
        adapter_kernel,
        in_specs=[VMEM],
        out_specs=[VMEM, VMEM],
        out_shape=[
            shape((RANK, QUERY_HEAD_COUNT * WIDTH), f32),
            shape((RANK, KEY_VALUE_HEADS * WIDTH), f32),
        ],
        compiler_params=PARAMS,
        name="adapter_out",
    )(total)


def copies_to_all(block, axes):
    size = lax.axis_size(axes)
    return lax.all_to_all(jnp.broadcast_to(block[None], (size,) + block.shape), axes, 0, 0)


def summed(pieces):
    return jnp.sum(pieces.astype(f32), axis=0).astype(bf16)


def sum_over_all(part):
    size = lax.axis_size(NEAR)
    mine = summed(lax.all_to_all(part.reshape(size, part.shape[0] // size, WIDTH), NEAR, 0, 0))
    mine = summed(copies_to_all(mine, FAR))
    return copies_to_all(mine, NEAR).reshape(part.shape)


def body(queries, keys, values, output_gradient, adapter_query_down, adapter_value_down):
    q, grad, aq_t = queries[0], output_gradient[0], adapter_query_down[0].T
    sel, oth = pack(group_place()[0], keys[0], values[0], adapter_value_down[0].T)
    one = passed_along(sel, 1)
    other = passed_along(oth, 1, range(0, CTX_SIZE, 2))
    later, _ = lax.optimization_barrier((sel, oth))
    two = passed_along(later, 2)
    three = passed_along(one, 2, range(1, CTX_SIZE, 2))
    dq_short, ads, own_short, backs = attend_short(aq_t, sel, one, q, grad)
    dq_long, part, own_long, r1, r2, r3 = attend_long(
        aq_t, sel, oth, one, other, three, two, ads, backs, q, grad
    )
    r1 = passed_along(r1, -1)
    r2 = passed_along(r2, -2)
    r3 = passed_along(r3, -3, range(1, CTX_SIZE, 2))
    dq, dk, dv = gradients_out(dq_short, dq_long, own_short, own_long, r1, r2, r3)
    total = sum_over_all(part)
    adapter_q, adapter_v = adapter_out(total)
    return dq[None], dk[None], dv[None], adapter_q, adapter_v


def solution(mesh):
    split = Mesh(mesh.devices.reshape(SIZES), AXES)
    tokens = P(DP, CTX, None)
    return jax.shard_map(
        body,
        mesh=split,
        in_specs=(tokens,) * 6,
        out_specs=(tokens, tokens, tokens, P(), P()),
        check_vma=False,
    )
```
